128 devices in a mesh: tm: 8 (over z, core), height: 16 (over x, y).
Axes of the slice: x: 4, y: 4, z: 4, core: 2. Of those that a mesh axis runs over, the one named last changes fastest.
Arguments:
- tokens: bfloat16 [16, 32, 64, 1536], P('tm', 'height'), may hold values from -6 to 6
- norm_gain: float32 [1536], replicated, may hold values from 0.5 to 1.5
- in_weight: bfloat16 [1536, 3072], replicated, may hold values from -0.15625 to 0.15625
- bc_weight: bfloat16 [1536, 512], replicated, may hold values from -0.15625 to 0.15625
- dt_weight: bfloat16 [1536, 48], replicated, may hold values from -0.15625 to 0.15625
- dt_bias: float32 [48], replicated, may hold values from -1 to 1
- decay_rate: float32 [2, 24], replicated, may hold values from 0.00032552084 to 0.05
- out_gain: float32 [1536], replicated, may hold values from 0.5 to 1.5
- out_weight: bfloat16 [1536, 1536], replicated, may hold values from -0.15625 to 0.15625
Outputs:
- mixed: bfloat16 [16, 32, 64, 1536], P('tm', 'height')
The draws below stay inside these ranges and needn't reach their ends.
All inputs are finite; a program needn't handle non-finite values.
Results may differ from the reference program's by a relative error of at most 0.02.
Values may be sent and summed in bfloat16 or wider, within the bound.
A program may use at most 192 MiB of HBM per device.

```python
import math
import jax
import jax.numpy as jnp
from jax import lax

D = 1536
HEADS = 24
HEAD_DIM = 64
STATE = 128
W = 64
INNER = 1536
FRAMES = 16
ROWS = 32


def steps_of(own_key, extent, split, low, top_value):
    loudness = 1.0
    for dim, parts in split:
        draws = jax.random.uniform(jax.random.fold_in(jax.random.fold_in(own_key, 6), dim), (parts,), jnp.float32, low / len(split), top_value / len(split))
        loudness = loudness * jnp.repeat(jnp.exp(draws), extent[dim] // parts).reshape((-1,) + (1,) * (len(extent) - 1 - dim))
    return loudness


def scatter_about(stream_key, shape, scale, bound, split=(), held_as=jnp.bfloat16):
    values = jax.random.normal(stream_key, shape, jnp.float32) * scale
    if len(split) > 0:
        values = steps_of(stream_key, shape, split, -0.22, 0.18) * values
    return jnp.clip(values, min=-bound, max=bound).astype(held_as)


def setup_inputs(seed: int = 0) -> dict:
    key_list = jax.random.split(jax.random.key(seed), 10)
    tokens = scatter_about(key_list[0], (FRAMES, ROWS, W, D), 1.0, 6.0, ((0, 8), (1, 16)))
    norm_gain = jnp.clip(1.0 + 0.1 * jax.random.normal(key_list[1], (D,), jnp.float32), 0.5, 1.5)
    in_weight = scatter_about(key_list[2], (D, 2 * INNER), D ** -0.5, 0.15625)
    bc_weight = scatter_about(key_list[3], (D, 4 * STATE), D ** -0.5, 0.15625)
    dt_weight = scatter_about(key_list[4], (D, 2 * HEADS), D ** -0.5, 0.15625)
    dt_bias = jnp.clip(jax.random.uniform(key_list[5], (2 * HEADS,), jnp.float32, -1.0, 1.0), -1.0, 1.0)
    decay_rate = jnp.clip(jnp.exp(jax.random.uniform(key_list[6], (2, HEADS), jnp.float32, math.log(0.00032552084), math.log(0.05))), 0.00032552084, 0.05)
    out_gain = jnp.clip(1.0 + 0.1 * jax.random.normal(key_list[7], (INNER,), jnp.float32), 0.5, 1.5)
    out_weight = scatter_about(key_list[8], (INNER, D), INNER ** -0.5, 0.15625)
    return dict(tokens=tokens, norm_gain=norm_gain, in_weight=in_weight, bc_weight=bc_weight, dt_weight=dt_weight, dt_bias=dt_bias, decay_rate=decay_rate, out_gain=out_gain, out_weight=out_weight)


PRECISE = lax.Precision.HIGH
EPSILON = 1e-05

def stored(values):
    return lax.optimization_barrier(values.astype(jnp.bfloat16))

def rms_scale(values, scaling):
    mean_square = lax.optimization_barrier(jnp.mean(values * values, axis=-1, keepdims=True))
    return values * lax.rsqrt(mean_square + EPSILON) * scaling

def block_step(carried, pieces):
    inputs, b_proj, c_proj, dt_values, log_decay = pieces
    running = jnp.cumsum(log_decay, axis=0)
    length = inputs.shape[0]
    causal = jnp.arange(length)[:, None] >= jnp.arange(length)[None, :]
    spread = running[:, None, :] - running[None, :, :]
    decays = jnp.exp(jnp.where(causal[:, :, None], spread, -jnp.inf))
    scores = jnp.dot(c_proj.astype(jnp.bfloat16), b_proj.astype(jnp.bfloat16).T, preferred_element_type=jnp.float32)
    weights = scores[:, :, None] * decays * dt_values[None, :, :]
    within = jnp.einsum('ijh,jhp->ihp', weights, inputs, precision=PRECISE)
    earlier = jnp.einsum('in,hpn->ihp', c_proj, carried, precision=PRECISE)
    outputs = within + jnp.exp(running)[:, :, None] * earlier
    to_end = jnp.exp(running[-1][None, :] - running) * dt_values
    fresh_state = jnp.einsum('jh,jhp,jn->hpn', to_end, inputs, b_proj, precision=PRECISE)
    carried = jnp.exp(running[-1])[:, None, None] * carried + fresh_state
    return (carried, outputs)

def run_blocks(inputs, b_proj, c_proj, dt_values, log_decay, initial, block_len):
    blocks = inputs.shape[0] // block_len

    def split_blocks(operand):
        return operand.reshape((blocks, block_len) + operand.shape[1:])
    final_state, outputs = lax.scan(block_step, initial, (split_blocks(inputs), split_blocks(b_proj), split_blocks(c_proj), split_blocks(dt_values), split_blocks(log_decay)))
    return (outputs.reshape(inputs.shape), final_state)

def direction(inputs, b_proj, c_proj, dt_values, log_decay, block_len):
    initial = jnp.zeros((HEADS, HEAD_DIM, STATE), jnp.float32)
    outputs, _ = run_blocks(inputs, b_proj, c_proj, dt_values, log_decay, initial, block_len)
    return outputs

def reference(tokens, norm_gain, in_weight, bc_weight, dt_weight, dt_bias, decay_rate, out_gain, out_weight):
    flat_tokens = tokens.reshape(-1, D).astype(jnp.float32)
    normed = stored(rms_scale(flat_tokens, norm_gain))
    projected = stored(jnp.dot(normed, in_weight, preferred_element_type=jnp.float32))
    bc_values = stored(jnp.dot(normed, bc_weight, preferred_element_type=jnp.float32)).astype(jnp.float32)
    dt_logits = stored(jnp.dot(normed, dt_weight, preferred_element_type=jnp.float32))
    dt_values = jax.nn.softplus(dt_logits.astype(jnp.float32) + dt_bias)
    log_decay = -dt_values * decay_rate.reshape(-1)
    grid = (FRAMES, ROWS, W)
    inputs = projected[:, :INNER].astype(jnp.float32).reshape(grid + (HEADS, HEAD_DIM))
    gate_values = projected[:, INNER:].astype(jnp.float32).reshape(grid + (INNER,))
    bc_values = bc_values.reshape(grid + (4 * STATE,))
    dt_values = dt_values.reshape(grid + (2 * HEADS,))
    log_decay = log_decay.reshape(grid + (2 * HEADS,))
    spatial_len = ROWS * W
    spatial_block = math.gcd(256, spatial_len)

    def spatial(pieces):
        inputs_f, bc_f, dt_f, decay_f = pieces
        outputs = direction(inputs_f.reshape(spatial_len, HEADS, HEAD_DIM), bc_f[..., :STATE].reshape(spatial_len, STATE), bc_f[..., STATE:2 * STATE].reshape(spatial_len, STATE), dt_f[..., :HEADS].reshape(spatial_len, HEADS), decay_f[..., :HEADS].reshape(spatial_len, HEADS), spatial_block)
        return outputs.reshape(ROWS, W, INNER)
    spatial_out = lax.map(spatial, (inputs, bc_values, dt_values, log_decay))
    temporal_len = W * FRAMES
    temporal_block = math.gcd(256, temporal_len)

    def temporal(pieces):
        inputs_r, bc_r, dt_r, decay_r = pieces
        outputs = direction(inputs_r.reshape(temporal_len, HEADS, HEAD_DIM), bc_r[..., 2 * STATE:3 * STATE].reshape(temporal_len, STATE), bc_r[..., 3 * STATE:].reshape(temporal_len, STATE), dt_r[..., HEADS:].reshape(temporal_len, HEADS), decay_r[..., HEADS:].reshape(temporal_len, HEADS), temporal_block)
        return outputs.reshape(W, FRAMES, INNER)

    def row_major(operand):
        return jnp.moveaxis(operand, 0, 2)
    temporal_out = lax.map(temporal, (row_major(inputs), row_major(bc_values), row_major(dt_values), row_major(log_decay)))
    temporal_out = stored(jnp.moveaxis(temporal_out, 2, 0))
    combined = spatial_out + temporal_out.astype(jnp.float32)
    gated = combined * jax.nn.silu(gate_values)
    normed_out = stored(rms_scale(gated, out_gain)).reshape(-1, INNER)
    mixed = jnp.dot(normed_out, out_weight, preferred_element_type=jnp.float32)
    return mixed.astype(jnp.bfloat16).reshape(FRAMES, ROWS, W, D)
```

```python
import functools

import jax
import jax.numpy as jnp
from jax import lax
from jax.experimental import pallas as pl
from jax.experimental.pallas import tpu as pltpu
from jax.sharding import PartitionSpec as P

EPSILON = 1e-05
LOG2E = 1.4426950408889634
BF16 = jnp.bfloat16
F32 = jnp.float32

D = 1536
INNER = 1536
HEADS = 24
STATE = 128
COLS = 64
TM = 8
HT = 16
GROUPS = 4
GHEADS = HEADS // GROUPS
GL = GHEADS * 64
TOK = 256
CHUNK_COLS = 16
CHUNKS = COLS // CHUNK_COLS


def mm(a, b):
    return jnp.dot(a, b, preferred_element_type=F32)


def mm_tokens(a, b):
    return lax.dot_general(a, b, (((0,), (0,)), ((), ())), preferred_element_type=F32)


def softplus(v):
    return jnp.maximum(v, 0.0) + jnp.log1p(jnp.exp(-jnp.abs(v)))


def parts(v, count):
    pieces, rest = [], v
    for _ in range(count):
        piece = rest.astype(BF16).astype(F32)
        pieces.append(piece)
        rest = rest - piece
    return jnp.concatenate(pieces, axis=1).astype(BF16)


def cumulative(order, v):
    width = v.shape[1]
    sums = mm(order, parts(v, 3))
    return sums[:, :width] + sums[:, width : 2 * width] + sums[:, 2 * width :]


def iota(shape, dim):
    return lax.broadcasted_iota(jnp.int32, shape, dim)


def kernel(
    tokens, gain, w_in, w_bc, w_dt, dt_bias, rate, out_gain, w_out, out,
    tok_v, w_in_v, w_bc_v, w_dt_v, w_out_v,
    normed, x_all, gate, bc_s, bct_send, l_send, d_send, s_send,
    xt, bct, ltr, d_recv, s_recv, inc_send, inc_recv, y_send, y_recv,
    xd_s, sp_out, e_run, run_s, runt_s, spread_s, spread_t, order_t, lcol, state, d_exp,
    load_sem, x_ssem, x_rsem, b_ssem, b_rsem, l_ssem, l_rsem, d_ssem, d_rsem,
    s_ssem, s_rsem, i_ssem, i_rsem, y_ssem, y_rsem,
):
    t = lax.axis_index("tm")
    h = lax.axis_index("height")
    z = t // 2
    core = t % 2

    def remote(src, dst, ssem, rsem, **where):
        return pltpu.make_async_remote_copy(
            src_ref=src, dst_ref=dst, send_sem=ssem, recv_sem=rsem,
            device_id=where, device_id_type=pl.DeviceIdType.MESH,
        )

    def group_at(step):
        return (z + 1 + step) % GROUPS

    def lanes_of(group):
        return pl.ds(pl.multiple_of(group * GL, 128), GL)

    loads = [
        pltpu.make_async_copy(tokens, tok_v, load_sem.at[0]),
        pltpu.make_async_copy(w_bc, w_bc_v, load_sem.at[1]),
        pltpu.make_async_copy(w_dt, w_dt_v, load_sem.at[2]),
    ]
    for step in range(GROUPS):
        where = lanes_of(group_at(step))
        loads.append(pltpu.make_async_copy(w_in.at[:, where], w_in_v.at[:, where], load_sem.at[3 + step]))
    for step in range(2):
        where = pl.ds(INNER + 768 * step, 768)
        loads.append(pltpu.make_async_copy(w_in.at[:, where], w_in_v.at[:, where], load_sem.at[7 + step]))
    loads.append(pltpu.make_async_copy(w_out, w_out_v, load_sem.at[9]))
    for load in loads:
        load.start()

    barrier = pltpu.get_barrier_semaphore()

    @pl.loop(1, TM)
    def _(k):
        pl.semaphore_signal(barrier, inc=1, device_id={"tm": (t + k) % TM}, device_id_type=pl.DeviceIdType.MESH)

    @pl.loop(1, HT)
    def _(k):
        pl.semaphore_signal(barrier, inc=1, device_id={"height": (h + k) % HT}, device_id_type=pl.DeviceIdType.MESH)

    spread_s[...] = ((iota((96, INNER), 0) & 31) == (iota((96, INNER), 1) >> 6)).astype(F32).astype(BF16)
    spread_t[...] = ((iota((16, GL), 0) & 7) == (iota((16, GL), 1) >> 6)).astype(F32).astype(BF16)

    def place(index):
        return (index & 15) * 16 + ((index >> 4) & 7) * 2 + (index >> 7)

    order_t[...] = (place(iota((TOK, TOK), 0)) >= place(iota((TOK, TOK), 1))).astype(F32).astype(BF16)

    loads[0].wait()

    @pl.loop(0, 8)
    def _(k):
        rows = pl.ds(pl.multiple_of(k * 32, 32), 32)
        v = tok_v[rows, :].astype(F32)
        mean_square = jnp.mean(v * v, axis=-1, keepdims=True)
        normed[rows, :] = (v * lax.rsqrt(mean_square + EPSILON) * gain[...]).astype(BF16)

    loads[1].wait()
    bc = mm(normed[...], w_bc_v[...]).astype(BF16)
    bc_s[...] = bc[:, : 2 * STATE]
    for f in range(2):
        for r in range(2):
            at = 128 * f + 64 * r
            bct_send[r, f] = bc[at : at + 64, 2 * STATE :]
    loads[2].wait()
    logits = mm(normed[...], w_dt_v[...]).astype(BF16).astype(F32)
    dt = softplus(logits + dt_bias[...])
    rates = jnp.concatenate([rate[0:1, :], rate[1:2, :]], axis=1)
    decay = -dt * rates * LOG2E
    both = jnp.concatenate([dt, decay, jnp.zeros((TOK, 32), F32)], axis=1)
    for r in range(2):
        turned = jnp.concatenate([both[64 * r : 64 * r + 64], both[128 + 64 * r : 192 + 64 * r]], axis=0).T
        for g in range(GROUPS):
            l_send[g, r, 0:8] = turned[24 + 6 * g : 32 + 6 * g]
            l_send[g, r, 8:16] = turned[72 + 6 * g : 80 + 6 * g]

    pad = jnp.zeros((TOK, 8), F32)
    dt_s = jnp.concatenate([dt[:, :HEADS], pad], axis=1)
    decay_s = jnp.concatenate([decay[:, :HEADS], pad], axis=1)
    row, col = iota((TOK, TOK), 0), iota((TOK, TOK), 1)
    order_s = ((row >= col) & ((row >> 7) == (col >> 7))).astype(F32).astype(BF16)
    run = cumulative(order_s, decay_s)
    run_s[...] = run
    for f in range(2):
        runt_s[f] = jnp.concatenate([run[128 * f : 128 * f + 128], jnp.zeros((128, 96), F32)], axis=1).T[:32]
    ends = [run[127:128], run[255:256]]
    for f in range(2):
        d_send[f] = jnp.broadcast_to(
            jnp.concatenate([jnp.exp2(ends[f]), jnp.zeros((1, 96), F32)], axis=1), (8, 128)
        )
    end = jnp.concatenate([jnp.broadcast_to(e, (128, 32)) for e in ends], axis=0)
    to_end = parts(jnp.exp2(end - run) * dt_s, 2)
    dt_parts = parts(dt_s, 2)
    from_start = parts(jnp.exp2(run), 2)

    pl.semaphore_wait(barrier, TM - 1 + HT - 1)

    def bc_copy(to):
        return remote(bct_send.at[to % 2], bct.at[t], b_ssem.at[to], b_rsem.at[t], tm=to)

    def l_copy(to):
        return remote(l_send.at[to // 2, to % 2], ltr.at[t], l_ssem.at[to], l_rsem.at[t], tm=to)

    @pl.loop(1, TM)
    def _(k):
        to = (t + k) % TM
        l_copy(to).start()
        bc_copy(to).start()

    bct[t] = bct_send[core]
    ltr[t] = l_send[z, core]

    def owned(p):
        return p // 8, pl.ds(pl.multiple_of((p % 8) * 16, 16), 16)

    def d_copy(to):
        return remote(d_send.at[to // 8], d_recv.at[h], d_ssem.at[to], d_rsem.at[h], height=to)

    @pl.loop(1, HT)
    def _(k):
        d_copy((h + k) % HT).start()

    d_recv[h] = d_send[h // 8]

    def x_source(to):
        rows = pl.ds(pl.multiple_of((to % 2) * COLS, COLS), COLS)
        return x_all.at[:, rows, lanes_of(to // 2)]

    def x_copy(to):
        return remote(x_source(to), xt.at[t], x_ssem.at[to], x_rsem.at[t], tm=to)

    for step in range(GROUPS):
        group = group_at(step)
        loads[3 + step].wait()
        xg = mm(normed[...], w_in_v[:, lanes_of(group)]).astype(BF16)
        x_all[0, :, lanes_of(group)] = xg[:128]
        x_all[1, :, lanes_of(group)] = xg[128:]
        for c in range(2):
            to = group * 2 + c
            if step < GROUPS - 1:
                x_copy(to).start()
            else:
                @pl.when(to != t)
                def _():
                    x_copy(to).start()

                @pl.when(to == t)
                def _():
                    for f in range(2):
                        xt[t, f] = xg[128 * f + COLS * c : 128 * f + COLS * c + COLS]

    for g in range(GROUPS):
        lanes = pl.ds(GL * g, GL)
        spread = spread_s[0:64, lanes]
        weight = mm(to_end, spread)
        steps = mm(dt_parts, spread)
        e_run[:, lanes] = mm(from_start, spread)
        for f in range(2):
            rows = slice(128 * f, 128 * f + 128)
            x = x_all[f, :, lanes].astype(F32)
            xd_s[f, :, lanes] = (x * steps[rows]).astype(BF16)
            s_send[f, :, lanes] = mm_tokens(
                bc_s[rows, :STATE], (x * weight[rows]).astype(BF16)
            ).astype(BF16)

    def s_copy(to):
        f, rows = owned(to)
        return remote(s_send.at[f, rows], s_recv.at[h], s_ssem.at[to], s_rsem.at[h], height=to)

    @pl.loop(1, HT)
    def _(k):
        s_copy((h + k) % HT).start()

    own_f, own_rows = owned(h)
    s_recv[h] = s_send[own_f, own_rows, :]

    for step in range(2):
        loads[7 + step].wait()

        @pl.loop(0, 2)
        def _(k):
            lanes = pl.ds(pl.multiple_of(768 * step + 384 * k, 128), 384)
            source = pl.ds(pl.multiple_of(INNER + 768 * step + 384 * k, 128), 384)
            v = mm(normed[...], w_in_v[:, source]).astype(BF16).astype(F32)
            gate[:, lanes] = v / (1.0 + jnp.exp(-v))

    half = iota((128, 128), 1) < 64
    causal = iota((128, 128), 0) >= iota((128, 128), 1)

    @pl.loop(0, 2)
    def _(f):
        rows = pl.ds(pl.multiple_of(f * 128, 128), 128)
        b, c = bc_s[rows, :STATE], bc_s[rows, STATE:]
        scores = lax.dot_general(c, b, (((1,), (1,)), ((), ())), preferred_element_type=F32)
        scores = jnp.where(causal, scores, 0.0)
        run_f, runt_f = run_s[rows, :], runt_s[f]
        for pair in range(HEADS // 2):
            weights = []
            for head in (2 * pair, 2 * pair + 1):
                spread = run_f[:, head : head + 1] - runt_f[head : head + 1, :]
                weights.append((scores * jnp.exp2(jnp.minimum(spread, 0.0))).astype(BF16))
            lanes = pl.ds(128 * pair, 128)
            x = xd_s[f, :, lanes]
            none = jnp.zeros_like(x)
            both_x = jnp.concatenate([jnp.where(half, x, none), jnp.where(half, none, x)], axis=0)
            sp_out[rows, lanes] = mm(jnp.concatenate(weights, axis=1), both_x)

    @pl.loop(1, HT)
    def _(k):
        source = (h + k) % HT
        remote(d_send.at[0], d_recv.at[source], d_ssem.at[source], d_rsem.at[source], height=source).wait_recv()

    totals = jnp.concatenate([d_recv[k, 0:1, :32] for k in range(HT)], axis=0)
    d_exp[...] = mm(parts(totals, 3), spread_s[...])

    @pl.loop(1, HT)
    def _(k):
        source = (h + k) % HT
        remote(s_send.at[0, pl.ds(0, 16)], s_recv.at[source], s_ssem.at[source], s_rsem.at[source], height=source).wait_recv()

    before = jnp.zeros((16, INNER), F32)
    for k in range(HT):
        inc_send[k] = before.astype(BF16)
        if k < HT - 1:
            before = before * d_exp[k : k + 1, :] + s_recv[k].astype(F32)

    def i_copy(to):
        f, rows = owned(h)
        return remote(inc_send.at[to], inc_recv.at[f, rows], i_ssem.at[to], i_rsem.at[h], height=to)

    @pl.loop(1, HT)
    def _(k):
        i_copy((h + k) % HT).start()

    inc_recv[own_f, own_rows, :] = inc_send[h]

    @pl.loop(1, TM)
    def _(k):
        source = (t + k) % TM
        remote(l_send.at[0, 0], ltr.at[source], l_ssem.at[source], l_rsem.at[source], tm=source).wait_recv()
        remote(bct_send.at[0], bct.at[source], b_ssem.at[source], b_rsem.at[source], tm=source).wait_recv()

    columns = ltr[...].reshape(TM * 16, 128).T
    for s in range(TM):
        lcol[s] = columns[:, 16 * s : 16 * s + 16]

    @pl.loop(1, TM)
    def _(k):
        source = (t + k) % TM
        remote(x_all.at[:, pl.ds(0, COLS), pl.ds(0, GL)], xt.at[source], x_ssem.at[source], x_rsem.at[source], tm=source).wait_recv()

    state[...] = jnp.zeros_like(state)

    def y_copy(to, cols):
        return remote(
            y_send.at[to, :, cols], y_recv.at[t, :, cols], y_ssem.at[to], y_rsem.at[t], tm=to
        )

    @pl.loop(0, CHUNKS)
    def _(chunk):
        cols = pl.ds(pl.multiple_of(chunk * CHUNK_COLS, CHUNK_COLS), CHUNK_COLS)

        def tokens_of(f):
            return pl.ds(pl.multiple_of(f * COLS + chunk * CHUNK_COLS, CHUNK_COLS), CHUNK_COLS)

        def gathered(get, width):
            return jnp.concatenate([get(f).reshape(128, width) for f in range(2)], axis=0)

        x = gathered(lambda f: xt[:, f, cols, :], GL)
        bcv = gathered(lambda f: bct[:, f, cols, :], 2 * STATE)
        dl = gathered(lambda f: lcol[:, tokens_of(f), :], 16)
        b, c = bcv[:, :STATE], bcv[:, STATE:]
        dtv, decays = dl[:, :8], dl[:, 8:]
        runs = cumulative(order_t[...], decays)
        runs_row = jnp.concatenate([runs, jnp.zeros((TOK, 120), F32)], axis=1).T[:8]
        last = runs[TOK - 1 : TOK]
        weight = mm(parts(jnp.exp2(last - runs) * dtv, 2), spread_t[...])
        steps = mm(parts(dtv, 2), spread_t[...])
        grown = mm(parts(jnp.exp2(runs), 2), spread_t[...])
        scores = lax.dot_general(c, b, (((1,), (1,)), ((), ())), preferred_element_type=F32)
        scores = scores * order_t[...].astype(F32)
        xf = x.astype(F32)
        xd = (xf * steps).astype(BF16)
        xw = (xf * weight).astype(BF16)
        earlier = mm(c, state[...].astype(BF16)) * grown
        state[...] = state[...] * grown[TOK - 1 : TOK] + mm_tokens(b, xw)
        half_x = iota((TOK, 128), 1) < 64
        for pair in range(GHEADS // 2):
            weights = []
            for head in (2 * pair, 2 * pair + 1):
                spread = runs[:, head : head + 1] - runs_row[head : head + 1, :]
                weights.append((scores * jnp.exp2(jnp.minimum(spread, 0.0))).astype(BF16))
            lanes = slice(128 * pair, 128 * pair + 128)
            xp = xd[:, lanes]
            none = jnp.zeros_like(xp)
            both_x = jnp.concatenate([jnp.where(half_x, xp, none), jnp.where(half_x, none, xp)], axis=0)
            y = mm(jnp.concatenate(weights, axis=1), both_x) + earlier[:, lanes]
            y = y.astype(BF16)
            for f in range(2):
                y_send[:, f, cols, lanes] = y[128 * f : 128 * f + 128].reshape(TM, CHUNK_COLS, 128)

        @pl.loop(1, TM)
        def _(k):
            y_copy((t + k) % TM, cols).start()

    y_recv[t] = y_send[t]

    @pl.loop(1, HT)
    def _(k):
        source = (h + k) % HT
        f, rows = owned(source)
        remote(inc_send.at[source], inc_recv.at[f, rows], i_ssem.at[source], i_rsem.at[source], height=source).wait_recv()

    for f in range(2):
        rows = slice(128 * f, 128 * f + 128)
        for g in range(GROUPS):
            lanes = slice(GL * g, GL * g + GL)
            sp_out[rows, lanes] += e_run[rows, lanes] * mm(bc_s[rows, STATE:], inc_recv[f, :, lanes])

    @pl.loop(1, TM)
    def _(k):
        source = (t + k) % TM
        remote(y_send.at[source], y_recv.at[source], y_ssem.at[source], y_rsem.at[source], tm=source).wait_recv()

    @pl.loop(0, 8)
    def _(k):
        f, r, part = k // 4, (k // 2) % 2, k % 2
        rows = pl.ds(pl.multiple_of(k * 32, 32), 32)
        cols = pl.ds(pl.multiple_of(part * 32, 32), 32)
        temporal = jnp.concatenate([y_recv[2 * g + r, f, cols, :] for g in range(GROUPS)], axis=1)
        gated = (sp_out[rows, :] + temporal.astype(F32)) * gate[rows, :]
        mean_square = jnp.mean(gated * gated, axis=-1, keepdims=True)
        normed[rows, :] = (gated * lax.rsqrt(mean_square + EPSILON) * out_gain[...]).astype(BF16)

    loads[9].wait()

    @pl.loop(0, 4)
    def _(k):
        lanes = pl.ds(pl.multiple_of(384 * k, 128), 384)
        out[:, lanes] = mm(normed[...], w_out_v[:, lanes]).astype(BF16)

    @pl.loop(1, TM)
    def _(k):
        to = (t + k) % TM
        l_copy(to).wait_send()
        bc_copy(to).wait_send()
        x_copy(to).wait_send()
        y_copy(to, pl.ds(0, COLS)).wait_send()

    @pl.loop(1, HT)
    def _(k):
        to = (h + k) % HT
        d_copy(to).wait_send()
        s_copy(to).wait_send()
        i_copy(to).wait_send()


def per_device(tokens, norm_gain, in_weight, bc_weight, dt_weight, dt_bias, decay_rate, out_gain, out_weight):
    vmem = pl.BlockSpec(memory_space=pltpu.VMEM)
    hbm = pl.BlockSpec(memory_space=pl.ANY)
    dma = pltpu.SemaphoreType.DMA
    out = pl.pallas_call(
        kernel,
        out_shape=jax.ShapeDtypeStruct((TOK, D), BF16),
        in_specs=[hbm, vmem, hbm, hbm, hbm, vmem, vmem, vmem, hbm],
        out_specs=vmem,
        scratch_shapes=[
            pltpu.VMEM((TOK, D), BF16),
            pltpu.VMEM((D, 2 * INNER), BF16),
            pltpu.VMEM((D, 4 * STATE), BF16),
            pltpu.VMEM((D, 2 * HEADS), BF16),
            pltpu.VMEM((INNER, D), BF16),
            pltpu.VMEM((TOK, D), BF16),
            pltpu.VMEM((2, 128, INNER), BF16),
            pltpu.VMEM((TOK, INNER), F32),
            pltpu.VMEM((TOK, 2 * STATE), BF16),
            pltpu.VMEM((2, 2, COLS, 2 * STATE), BF16),
            pltpu.VMEM((GROUPS, 2, 16, 128), F32),
            pltpu.VMEM((2, 8, 128), F32),
            pltpu.VMEM((2, STATE, INNER), BF16),
            pltpu.VMEM((TM, 2, COLS, GL), BF16),
            pltpu.VMEM((TM, 2, COLS, 2 * STATE), BF16),
            pltpu.VMEM((TM, 16, 128), F32),
            pltpu.VMEM((HT, 8, 128), F32),
            pltpu.VMEM((HT, 16, INNER), BF16),
            pltpu.VMEM((HT, 16, INNER), BF16),
            pltpu.VMEM((2, STATE, INNER), BF16),
            pltpu.VMEM((TM, 2, COLS, GL), BF16),
            pltpu.VMEM((TM, 2, COLS, GL), BF16),
            pltpu.VMEM((2, 128, INNER), BF16),
            pltpu.VMEM((TOK, INNER), F32),
            pltpu.VMEM((TOK, INNER), F32),
            pltpu.VMEM((TOK, 32), F32),
            pltpu.VMEM((2, 32, 128), F32),
            pltpu.VMEM((96, INNER), BF16),
            pltpu.VMEM((16, GL), BF16),
            pltpu.VMEM((TOK, TOK), BF16),
            pltpu.VMEM((TM, 128, 16), F32),
            pltpu.VMEM((STATE, GL), F32),
            pltpu.VMEM((HT, INNER), F32),
            dma((10,)),
            dma((TM,)), dma((TM,)), dma((TM,)), dma((TM,)), dma((TM,)), dma((TM,)),
            dma((HT,)), dma((HT,)), dma((HT,)), dma((HT,)), dma((HT,)), dma((HT,)),
            dma((TM,)), dma((TM,)),
        ],
        compiler_params=pltpu.CompilerParams(
            collective_id=0, has_side_effects=True, vmem_limit_bytes=56 * 1024 * 1024
        ),
        name="layer",
    )(
        tokens.reshape(TOK, D),
        norm_gain.reshape(1, D),
        in_weight,
        bc_weight,
        dt_weight,
        dt_bias.reshape(1, 2 * HEADS),
        decay_rate,
        out_gain.reshape(1, INNER),
        out_weight,
    )
    return out.reshape(tokens.shape)


def solution(mesh):
    in_specs = (P("tm", "height", None, None), P(), P(), P(), P(), P(), P(), P(), P())
    out_specs = P("tm", "height", None, None)
    return jax.shard_map(
        per_device, mesh=mesh, in_specs=in_specs, out_specs=out_specs, check_vma=False
    )
```

```python
import functools

import jax
import jax.numpy as jnp
from jax import lax
from jax.experimental import pallas as pl
from jax.experimental.pallas import tpu as pltpu
from jax.sharding import PartitionSpec as P

EPSILON = 1e-05
LOG2E = 1.4426950408889634
BF16 = jnp.bfloat16
F32 = jnp.float32

D = 1536
INNER = 1536
HEADS = 24
STATE = 128
COLS = 64
TM = 8
HT = 16
GROUPS = 4
GHEADS = HEADS // GROUPS
GL = GHEADS * 64
HALF = INNER // 2
TOK = 256
CHUNK_COLS = 16
CHUNKS = COLS // CHUNK_COLS


def mm(a, b):
    return jnp.dot(a, b, preferred_element_type=F32)


def mm_tokens(a, b):
    return lax.dot_general(a, b, (((0,), (0,)), ((), ())), preferred_element_type=F32)


def mm_rows(a, b):
    return lax.dot_general(a, b, (((1,), (1,)), ((), ())), preferred_element_type=F32)


def softplus(v):
    return jnp.maximum(v, 0.0) + jnp.log1p(jnp.exp(-jnp.abs(v)))


def parts(v, count):
    pieces, rest = [], v
    for _ in range(count):
        piece = rest.astype(BF16).astype(F32)
        pieces.append(piece)
        rest = rest - piece
    return jnp.concatenate(pieces, axis=1).astype(BF16)


def cumulative(order, v):
    width = v.shape[1]
    sums = mm(order, parts(v, 3))
    return sums[:, :width] + sums[:, width : 2 * width] + sums[:, 2 * width :]


def iota(shape, dim):
    return lax.broadcasted_iota(jnp.int32, shape, dim)


def kernel(
    tokens, gain, w_in, w_bc, w_dt, dt_bias, rate, out_gain, w_out, out,
    tok_v, w_in_v, w_bc_v, w_dt_v, w_out_v,
    normed, x_all, gate, bc_s, bct_send, l_send, d_send, s_send,
    xt, bct, ltr, d_recv, s_recv, inc_send, inc_recv, y_send, y_recv,
    xd_s, sp_out, e_run, run_s, runt_s, spread_s, spread_t, order_t, lcol, state, d_exp,
    load_sem, x_ssem, x_rsem, b_ssem, b_rsem, f_ssem, l_ssem, l_rsem, d_ssem, d_rsem,
    s_ssem, s_rsem, i_ssem, i_rsem, y_ssem, y_rsem,
):
    t = lax.axis_index("tm")
    h = lax.axis_index("height")

    def remote(src, dst, ssem, rsem, **where):
        return pltpu.make_async_remote_copy(
            src_ref=src, dst_ref=dst, send_sem=ssem, recv_sem=rsem,
            device_id=where, device_id_type=pl.DeviceIdType.MESH,
        )

    own_row, own_group = t // GROUPS, t % GROUPS

    def lanes_of(index):
        return pl.ds(pl.multiple_of(index * GL, 128), GL)

    def half_lanes(start, half):
        return pl.ds(pl.multiple_of(start + half * HALF, 128), HALF)

    loads = [
        pltpu.make_async_copy(tokens, tok_v, load_sem.at[0]),
        pltpu.make_async_copy(w_bc, w_bc_v, load_sem.at[1]),
        pltpu.make_async_copy(w_dt, w_dt_v, load_sem.at[2]),
    ]
    for step in range(4):
        where = pl.ds(HALF * step, HALF)
        loads.append(pltpu.make_async_copy(w_in.at[:, where], w_in_v.at[:, where], load_sem.at[3 + step]))
    loads.append(pltpu.make_async_copy(w_out, w_out_v, load_sem.at[7]))
    for load in loads[:5]:
        load.start()

    barrier = pltpu.get_barrier_semaphore()

    @pl.loop(1, TM)
    def _(k):
        pl.semaphore_signal(barrier, inc=1, device_id={"tm": (t + k) % TM}, device_id_type=pl.DeviceIdType.MESH)

    @pl.loop(1, HT)
    def _(k):
        pl.semaphore_signal(barrier, inc=1, device_id={"height": (h + k) % HT}, device_id_type=pl.DeviceIdType.MESH)

    spread_s[...] = ((iota((96, INNER), 0) & 31) == (iota((96, INNER), 1) >> 6)).astype(F32).astype(BF16)
    spread_t[...] = ((iota((16, GL), 0) & 7) == (iota((16, GL), 1) >> 6)).astype(F32).astype(BF16)

    def place(index):
        return (index & 15) * 16 + ((index >> 4) & 7) * 2 + (index >> 7)

    order_t[...] = (place(iota((TOK, TOK), 0)) >= place(iota((TOK, TOK), 1))).astype(F32).astype(BF16)

    loads[0].wait()

    @pl.loop(0, 8)
    def _(k):
        rows = pl.ds(pl.multiple_of(k * 32, 32), 32)
        v = tok_v[rows, :].astype(F32)
        mean_square = jnp.mean(v * v, axis=-1, keepdims=True)
        normed[rows, :] = (v * lax.rsqrt(mean_square + EPSILON) * gain[...].reshape(1, D)).astype(BF16)

    loads[1].wait()
    bc = mm(normed[...], w_bc_v[...]).astype(BF16)
    bc_s[...] = bc[:, : 2 * STATE]
    for f in range(2):
        for r in range(2):
            at = 128 * f + 64 * r
            bct_send[r, f] = bc[at : at + 64, 2 * STATE :]
    loads[2].wait()
    logits = mm_rows(normed[...], w_dt_v[...]).astype(BF16).astype(F32)
    dt = softplus(logits + dt_bias[...])
    rates = jnp.concatenate([rate[0:1, :], rate[1:2, :]], axis=1)
    decay = -dt * rates * LOG2E
    both = jnp.concatenate([dt, decay, jnp.zeros((TOK, 32), F32)], axis=1)
    for r in range(2):
        turned = jnp.concatenate([both[64 * r : 64 * r + 64], both[128 + 64 * r : 192 + 64 * r]], axis=0).T
        for g in range(GROUPS):
            l_send[g, r, 0:8] = turned[24 + 6 * g : 32 + 6 * g]
            l_send[g, r, 8:16] = turned[72 + 6 * g : 80 + 6 * g]

    pad = jnp.zeros((TOK, 8), F32)
    dt_s = jnp.concatenate([dt[:, :HEADS], pad], axis=1)
    decay_s = jnp.concatenate([decay[:, :HEADS], pad], axis=1)
    row, col = iota((TOK, TOK), 0), iota((TOK, TOK), 1)
    order_s = ((row >= col) & ((row >> 7) == (col >> 7))).astype(F32).astype(BF16)
    run = cumulative(order_s, decay_s)
    run_s[...] = run
    for f in range(2):
        runt_s[f] = jnp.concatenate([run[128 * f : 128 * f + 128], jnp.zeros((128, 96), F32)], axis=1).T[:32]
    ends = [run[127:128], run[255:256]]
    for f in range(2):
        d_send[f] = jnp.broadcast_to(
            jnp.concatenate([jnp.exp2(ends[f]), jnp.zeros((1, 96), F32)], axis=1), (8, 128)
        )
    end = jnp.concatenate([jnp.broadcast_to(e, (128, 32)) for e in ends], axis=0)
    to_end = parts(jnp.exp2(end - run) * dt_s, 2)
    dt_parts = parts(dt_s, 2)
    from_start = parts(jnp.exp2(run), 2)

    for half in range(2):
        loads[3 + half].wait()
        if half == 1:
            for load in loads[5:]:
                load.start()
        lanes = pl.ds(HALF * half, HALF)
        xh = mm(normed[...], w_in_v[:, lanes]).astype(BF16)
        x_all[0, :, lanes] = xh[:128]
        x_all[1, :, lanes] = xh[128:]

    pl.semaphore_wait(barrier, TM - 1 + HT - 1)

    def l_copy(to):
        return remote(l_send.at[to % GROUPS, to // GROUPS], ltr.at[t], l_ssem.at[to], l_rsem.at[t], tm=to)

    def bc_copy(to):
        return remote(bct_send.at[to // GROUPS], bct.at[t], b_ssem.at[to], b_rsem.at[t], tm=to)

    def bc_pass(source):
        return remote(bct.at[source], bct.at[source], f_ssem.at[source], b_rsem.at[source], tm=t ^ 1)

    def chunk_of(chunk):
        return pl.ds(pl.multiple_of(chunk * CHUNK_COLS, CHUNK_COLS), CHUNK_COLS)

    def x_copy(to, chunk):
        rows = pl.ds(pl.multiple_of((to // GROUPS) * COLS + chunk * CHUNK_COLS, CHUNK_COLS), CHUNK_COLS)
        return remote(
            x_all.at[:, rows, lanes_of(to % GROUPS)], xt.at[t, :, chunk_of(chunk)],
            x_ssem.at[to], x_rsem.at[chunk, t], tm=to,
        )

    def owned(p):
        return p // 8, pl.ds(pl.multiple_of((p % 8) * 16, 16), 16)

    def d_copy(to):
        return remote(d_send.at[to // 8], d_recv.at[h], d_ssem.at[to], d_rsem.at[h], height=to)

    bc_copy(t ^ 1).start()

    @pl.loop(1, 4)
    def _(k):
        bc_copy((t + 2 * k) % TM).start()

    @pl.loop(1, TM)
    def _(k):
        l_copy((t + k) % TM).start()

    @pl.loop(0, CHUNKS)
    def _(chunk):
        @pl.loop(1, TM)
        def _(k):
            x_copy((t + k) % TM, chunk).start()

    @pl.loop(1, HT)
    def _(k):
        d_copy((h + k) % HT).start()

    bct[t] = bct_send[own_row]
    ltr[t] = l_send[own_group, own_row]
    d_recv[h] = d_send[h // 8]
    own_rows = pl.ds(pl.multiple_of(own_row * COLS, COLS), COLS)
    for f in range(2):
        xt[t, f] = x_all[f, own_rows, lanes_of(own_group)]

    def s_copy(to, half):
        f, rows = owned(to)
        return remote(s_send.at[half, f, rows], s_recv.at[half, h], s_ssem.at[to], s_rsem.at[half, h], height=to)

    own_f, own_n = owned(h)
    for half in range(2):
        for part in range(2):
            lanes = pl.ds(HALF * half + GL * part, GL)
            spread = spread_s[0:64, lanes]
            weight = mm(to_end, spread)
            steps = mm(dt_parts, spread)
            e_run[:, lanes] = mm(from_start, spread)
            for f in range(2):
                rows = slice(128 * f, 128 * f + 128)
                x = x_all[f, :, lanes].astype(F32)
                xd_s[f, :, lanes] = (x * steps[rows]).astype(BF16)
                s_send[half, f, :, pl.ds(GL * part, GL)] = mm_tokens(
                    bc_s[rows, :STATE], (x * weight[rows]).astype(BF16)
                ).astype(BF16)

        @pl.loop(1, HT)
        def _(k):
            s_copy((h + k) % HT, half).start()

        s_recv[half, h] = s_send[half, own_f, own_n, :]

    @pl.loop(0, 4)
    def _(k):
        for step in range(2):
            @pl.when(k == 2 * step)
            def _():
                loads[5 + step].wait()
        v = mm(normed[...], w_in_v[:, pl.ds(pl.multiple_of(INNER + GL * k, 128), GL)]).astype(BF16).astype(F32)
        gate[:, lanes_of(k)] = v / (1.0 + jnp.exp(-v))

    @pl.loop(1, 4)
    def _(k):
        source = (t + 2 * k) % TM
        remote(bct_send.at[0], bct.at[source], b_ssem.at[source], b_rsem.at[source], tm=source).wait_recv()
        bc_pass(source).start()

    half = iota((128, 128), 1) < 64
    causal = iota((128, 128), 0) >= iota((128, 128), 1)

    @pl.loop(0, 2)
    def _(f):
        rows = pl.ds(pl.multiple_of(f * 128, 128), 128)
        b, c = bc_s[rows, :STATE], bc_s[rows, STATE:]
        scores = mm_rows(c, b)
        scores = jnp.where(causal, scores, 0.0)
        run_f, runt_f = run_s[rows, :], runt_s[f]
        for pair in range(HEADS // 2):
            weights = []
            for head in (2 * pair, 2 * pair + 1):
                spread = run_f[:, head : head + 1] - runt_f[head : head + 1, :]
                weights.append((scores * jnp.exp2(jnp.minimum(spread, 0.0))).astype(BF16))
            lanes = pl.ds(128 * pair, 128)
            x = xd_s[f, :, lanes]
            none = jnp.zeros_like(x)
            both_x = jnp.concatenate([jnp.where(half, x, none), jnp.where(half, none, x)], axis=0)
            sp_out[rows, lanes] = mm(jnp.concatenate(weights, axis=1), both_x)

    @pl.loop(1, HT)
    def _(k):
        source = (h + k) % HT
        remote(d_send.at[0], d_recv.at[source], d_ssem.at[source], d_rsem.at[source], height=source).wait_recv()

    totals = jnp.concatenate([d_recv[k, 0:1, :32] for k in range(HT)], axis=0)
    totals = parts(totals, 3)
    for half in range(2):
        d_exp[half] = mm(totals, spread_s[:, pl.ds(HALF * half, HALF)])

    def i_copy(to, half):
        f, rows = owned(h)
        return remote(
            inc_send.at[half, to], inc_recv.at[half, f, rows], i_ssem.at[to], i_rsem.at[half, h], height=to
        )

    def prefix(half):
        @pl.loop(1, HT)
        def _(k):
            source = (h + k) % HT
            remote(
                s_send.at[0, 0, pl.ds(0, 16)], s_recv.at[half, source],
                s_ssem.at[source], s_rsem.at[half, source], height=source,
            ).wait_recv()

        before = jnp.zeros((16, HALF), F32)
        for k in range(HT):
            inc_send[half, k] = before.astype(BF16)
            if k < HT - 1:
                before = before * d_exp[half, k : k + 1, :] + s_recv[half, k].astype(F32)

        @pl.loop(1, HT)
        def _(k):
            i_copy((h + k) % HT, half).start()

        inc_recv[half, own_f, own_n, :] = inc_send[half, h]

    @pl.loop(1, TM)
    def _(k):
        source = (t + k) % TM
        remote(l_send.at[0, 0], ltr.at[source], l_ssem.at[source], l_rsem.at[source], tm=source).wait_recv()

    @pl.loop(0, 4)
    def _(k):
        source = (t + 2 * k) % TM ^ 1
        remote(bct_send.at[0], bct.at[source], b_ssem.at[source], b_rsem.at[source], tm=source).wait_recv()

    columns = ltr[...].reshape(TM * 16, 128).T
    for s in range(TM):
        lcol[s] = columns[:, 16 * s : 16 * s + 16]

    state[...] = jnp.zeros_like(state)

    def y_copy(to, cols):
        return remote(
            y_send.at[to, :, cols], y_recv.at[t, :, cols], y_ssem.at[to], y_rsem.at[t], tm=to
        )

    @pl.loop(0, CHUNKS)
    def _(chunk):
        cols = chunk_of(chunk)

        @pl.loop(1, TM)
        def _(k):
            source = (t + k) % TM
            remote(
                x_all.at[:, pl.ds(0, CHUNK_COLS), pl.ds(0, GL)], xt.at[source, :, cols],
                x_ssem.at[source], x_rsem.at[chunk, source], tm=source,
            ).wait_recv()

        def tokens_of(f):
            return pl.ds(pl.multiple_of(f * COLS + chunk * CHUNK_COLS, CHUNK_COLS), CHUNK_COLS)

        def gathered(get, width):
            return jnp.concatenate([get(f).reshape(128, width) for f in range(2)], axis=0)

        x = gathered(lambda f: xt[:, f, cols, :], GL)
        bcv = gathered(lambda f: bct[:, f, cols, :], 2 * STATE)
        dl = gathered(lambda f: lcol[:, tokens_of(f), :], 16)
        b, c = bcv[:, :STATE], bcv[:, STATE:]
        dtv, decays = dl[:, :8], dl[:, 8:]
        runs = cumulative(order_t[...], decays)
        runs_row = jnp.concatenate([runs, jnp.zeros((TOK, 120), F32)], axis=1).T[:8]
        last = runs[TOK - 1 : TOK]
        weight = mm(parts(jnp.exp2(last - runs) * dtv, 2), spread_t[...])
        steps = mm(parts(dtv, 2), spread_t[...])
        grown = mm(parts(jnp.exp2(runs), 2), spread_t[...])
        scores = mm_rows(c, b)
        scores = scores * order_t[...].astype(F32)
        xf = x.astype(F32)
        xd = (xf * steps).astype(BF16)
        xw = (xf * weight).astype(BF16)
        earlier = mm(c, state[...].astype(BF16)) * grown
        state[...] = state[...] * grown[TOK - 1 : TOK] + mm_tokens(b, xw)
        half_x = iota((TOK, 128), 1) < 64
        for pair in range(GHEADS // 2):
            weights = []
            for head in (2 * pair, 2 * pair + 1):
                spread = runs[:, head : head + 1] - runs_row[head : head + 1, :]
                weights.append((scores * jnp.exp2(jnp.minimum(spread, 0.0))).astype(BF16))
            lanes = slice(128 * pair, 128 * pair + 128)
            xp = xd[:, lanes]
            none = jnp.zeros_like(xp)
            both_x = jnp.concatenate([jnp.where(half_x, xp, none), jnp.where(half_x, none, xp)], axis=0)
            y = mm(jnp.concatenate(weights, axis=1), both_x) + earlier[:, lanes]
            y = y.astype(BF16)
            for f in range(2):
                y_send[:, f, cols, lanes] = y[128 * f : 128 * f + 128].reshape(TM, CHUNK_COLS, 128)

        @pl.loop(1, TM)
        def _(k):
            y_copy((t + k) % TM, cols).start()

        @pl.when(chunk < 2)
        def _():
            prefix(chunk)

    y_recv[t] = y_send[t]

    for half in range(2):
        @pl.loop(1, HT)
        def _(k):
            source = (h + k) % HT
            f, rows = owned(source)
            remote(
                inc_send.at[half, source], inc_recv.at[half, f, rows],
                i_ssem.at[source], i_rsem.at[half, source], height=source,
            ).wait_recv()

        for f in range(2):
            rows = slice(128 * f, 128 * f + 128)
            for part in range(2):
                lanes = pl.ds(HALF * half + GL * part, GL)
                earlier = mm(bc_s[rows, STATE:], inc_recv[half, f, :, pl.ds(GL * part, GL)])
                sp_out[rows, lanes] += e_run[rows, lanes] * earlier

    @pl.loop(1, TM)
    def _(k):
        source = (t + k) % TM
        remote(y_send.at[source], y_recv.at[source], y_ssem.at[source], y_rsem.at[source], tm=source).wait_recv()

    @pl.loop(0, 8)
    def _(k):
        f, r, part = k // 4, (k // 2) % 2, k % 2
        rows = pl.ds(pl.multiple_of(k * 32, 32), 32)
        cols = pl.ds(pl.multiple_of(part * 32, 32), 32)
        temporal = jnp.concatenate([y_recv[GROUPS * r + g, f, cols, :] for g in range(GROUPS)], axis=1)
        gated = (sp_out[rows, :] + temporal.astype(F32)) * gate[rows, :]
        mean_square = jnp.mean(gated * gated, axis=-1, keepdims=True)
        normed[rows, :] = (gated * lax.rsqrt(mean_square + EPSILON) * out_gain[...].reshape(1, INNER)).astype(BF16)

    loads[7].wait()

    @pl.loop(0, 4)
    def _(k):
        lanes = pl.ds(pl.multiple_of(384 * k, 128), 384)
        out[:, lanes] = mm(normed[...], w_out_v[:, lanes]).astype(BF16)

    bc_copy(t ^ 1).wait_send()

    @pl.loop(1, 4)
    def _(k):
        bc_copy((t + 2 * k) % TM).wait_send()
        bc_pass((t + 2 * k) % TM).wait_send()

    @pl.loop(1, TM)
    def _(k):
        to = (t + k) % TM
        l_copy(to).wait_send()
        remote(xt.at[to], xt.at[to], x_ssem.at[to], x_rsem.at[0, to], tm=to).wait_send()
        y_copy(to, pl.ds(0, COLS)).wait_send()

    @pl.loop(1, HT)
    def _(k):
        to = (h + k) % HT
        d_copy(to).wait_send()
        for half in range(2):
            s_copy(to, half).wait_send()
            i_copy(to, half).wait_send()


def per_device(tokens, norm_gain, in_weight, bc_weight, dt_weight, dt_bias, decay_rate, out_gain, out_weight):
    vmem = pl.BlockSpec(memory_space=pltpu.VMEM)
    hbm = pl.BlockSpec(memory_space=pl.ANY)
    dma = pltpu.SemaphoreType.DMA
    out = pl.pallas_call(
        kernel,
        out_shape=jax.ShapeDtypeStruct((TOK, D), BF16),
        in_specs=[hbm, vmem, hbm, hbm, hbm, vmem, vmem, vmem, hbm],
        out_specs=vmem,
        scratch_shapes=[
            pltpu.VMEM((TOK, D), BF16),
            pltpu.VMEM((D, 2 * INNER), BF16),
            pltpu.VMEM((D, 4 * STATE), BF16),
            pltpu.VMEM((2 * HEADS, D), BF16),
            pltpu.VMEM((INNER, D), BF16),
            pltpu.VMEM((TOK, D), BF16),
            pltpu.VMEM((2, 128, INNER), BF16),
            pltpu.VMEM((TOK, INNER), F32),
            pltpu.VMEM((TOK, 2 * STATE), BF16),
            pltpu.VMEM((2, 2, COLS, 2 * STATE), BF16),
            pltpu.VMEM((GROUPS, 2, 16, 128), F32),
            pltpu.VMEM((2, 8, 128), F32),
            pltpu.VMEM((2, 2, STATE, HALF), BF16),
            pltpu.VMEM((TM, 2, COLS, GL), BF16),
            pltpu.VMEM((TM, 2, COLS, 2 * STATE), BF16),
            pltpu.VMEM((TM, 16, 128), F32),
            pltpu.VMEM((HT, 8, 128), F32),
            pltpu.VMEM((2, HT, 16, HALF), BF16),
            pltpu.VMEM((2, HT, 16, HALF), BF16),
            pltpu.VMEM((2, 2, STATE, HALF), BF16),
            pltpu.VMEM((TM, 2, COLS, GL), BF16),
            pltpu.VMEM((TM, 2, COLS, GL), BF16),
            pltpu.VMEM((2, 128, INNER), BF16),
            pltpu.VMEM((TOK, INNER), F32),
            pltpu.VMEM((TOK, INNER), F32),
            pltpu.VMEM((TOK, 32), F32),
            pltpu.VMEM((2, 32, 128), F32),
            pltpu.VMEM((96, INNER), BF16),
            pltpu.VMEM((16, GL), BF16),
            pltpu.VMEM((TOK, TOK), BF16),
            pltpu.VMEM((TM, 128, 16), F32),
            pltpu.VMEM((STATE, GL), F32),
            pltpu.VMEM((2, HT, HALF), F32),
            dma((8,)),
            dma((TM,)), dma((CHUNKS, TM)),
            dma((TM,)), dma((TM,)), dma((TM,)),
            dma((TM,)), dma((TM,)),
            dma((HT,)), dma((HT,)),
            dma((HT,)), dma((2, HT)),
            dma((HT,)), dma((2, HT)),
            dma((TM,)), dma((TM,)),
        ],
        compiler_params=pltpu.CompilerParams(
            collective_id=0, has_side_effects=True, vmem_limit_bytes=56 * 1024 * 1024
        ),
        name="layer",
    )(
        tokens.reshape(TOK, D),
        norm_gain,
        in_weight,
        bc_weight,
        dt_weight.T,
        dt_bias.reshape(1, 2 * HEADS),
        decay_rate,
        out_gain,
        out_weight,
    )
    return out.reshape(tokens.shape)


def solution(mesh):
    in_specs = (P("tm", "height", None, None), P(), P(), P(), P(), P(), P(), P(), P())
    out_specs = P("tm", "height", None, None)
    return jax.shard_map(
        per_device, mesh=mesh, in_specs=in_specs, out_specs=out_specs, check_vma=False
    )
```

```python
import functools

import jax
import jax.numpy as jnp
from jax import lax
from jax.experimental import pallas as pl
from jax.experimental.pallas import tpu as pltpu
from jax.sharding import PartitionSpec as P

EPSILON = 1e-05
LOG2E = 1.4426950408889634
BF16 = jnp.bfloat16
F32 = jnp.float32

D = 1536
INNER = 1536
HEADS = 24
STATE = 128
COLS = 64
TM = 8
HT = 16
GROUPS = 4
GHEADS = HEADS // GROUPS
GL = GHEADS * 64
HALF = INNER // 2
TOK = 256
CHUNK_COLS = 16
CHUNKS = COLS // CHUNK_COLS


def mm(a, b):
    return jnp.dot(a, b, preferred_element_type=F32)


def mm_tokens(a, b):
    return lax.dot_general(a, b, (((0,), (0,)), ((), ())), preferred_element_type=F32)


def mm_rows(a, b):
    return lax.dot_general(a, b, (((1,), (1,)), ((), ())), preferred_element_type=F32)


def softplus(v):
    return jnp.maximum(v, 0.0) + jnp.log1p(jnp.exp(-jnp.abs(v)))


def parts(v, count):
    pieces, rest = [], v
    for _ in range(count):
        piece = rest.astype(BF16).astype(F32)
        pieces.append(piece)
        rest = rest - piece
    return jnp.concatenate(pieces, axis=1).astype(BF16)


def cumulative(order, v):
    width = v.shape[1]
    sums = mm(order, parts(v, 3))
    return sums[:, :width] + sums[:, width : 2 * width] + sums[:, 2 * width :]


def iota(shape, dim):
    return lax.broadcasted_iota(jnp.int32, shape, dim)


def kernel(
    tokens, gain, w_in, w_bc, w_dt, dt_bias, rate, out_gain, out,
    tok_v, w_in_v, w_bc_v, w_dt_v,
    normed, x_all, gate, bc_s, bct_send, l_send, d_send, s_send,
    xt, bct, ltr, d_recv, s_recv, inc_send, inc_recv, y_send, y_recv,
    xd_s, sp_out, e_run, run_s, runt_s, spread_s, spread_t, order_t, lcol, state, d_exp,
    load_sem, x_ssem, x_rsem, b_ssem, b_rsem, f_ssem, l_ssem, l_rsem, d_ssem, d_rsem,
    s_ssem, s_rsem, i_ssem, i_rsem, y_ssem, y_rsem,
):
    t = lax.axis_index("tm")
    h = lax.axis_index("height")

    def remote(src, dst, ssem, rsem, **where):
        return pltpu.make_async_remote_copy(
            src_ref=src, dst_ref=dst, send_sem=ssem, recv_sem=rsem,
            device_id=where, device_id_type=pl.DeviceIdType.MESH,
        )

    own_row, own_group = t // GROUPS, t % GROUPS

    def lanes_of(index):
        return pl.ds(pl.multiple_of(index * GL, 128), GL)

    def half_lanes(start, half):
        return pl.ds(pl.multiple_of(start + half * HALF, 128), HALF)

    loads = [
        pltpu.make_async_copy(tokens, tok_v, load_sem.at[0]),
        pltpu.make_async_copy(w_bc, w_bc_v, load_sem.at[1]),
        pltpu.make_async_copy(w_dt, w_dt_v, load_sem.at[2]),
    ]
    for step in range(4):
        where = pl.ds(HALF * step, HALF)
        loads.append(pltpu.make_async_copy(w_in.at[:, where], w_in_v.at[:, where], load_sem.at[3 + step]))
    for load in loads[:5]:
        load.start()

    barrier = pltpu.get_barrier_semaphore()

    @pl.loop(1, TM)
    def _(k):
        pl.semaphore_signal(barrier, inc=1, device_id={"tm": (t + k) % TM}, device_id_type=pl.DeviceIdType.MESH)

    @pl.loop(1, HT)
    def _(k):
        pl.semaphore_signal(barrier, inc=1, device_id={"height": (h + k) % HT}, device_id_type=pl.DeviceIdType.MESH)

    spread_s[...] = ((iota((96, INNER), 0) & 31) == (iota((96, INNER), 1) >> 6)).astype(F32).astype(BF16)
    spread_t[...] = ((iota((16, GL), 0) & 7) == (iota((16, GL), 1) >> 6)).astype(F32).astype(BF16)

    def place(index):
        return (index & 15) * 16 + ((index >> 4) & 7) * 2 + (index >> 7)

    order_t[...] = (place(iota((TOK, TOK), 0)) >= place(iota((TOK, TOK), 1))).astype(F32).astype(BF16)

    loads[0].wait()

    @pl.loop(0, 8)
    def _(k):
        rows = pl.ds(pl.multiple_of(k * 32, 32), 32)
        v = tok_v[rows, :].astype(F32)
        mean_square = jnp.mean(v * v, axis=-1, keepdims=True)
        normed[rows, :] = (v * lax.rsqrt(mean_square + EPSILON) * gain[...].reshape(1, D)).astype(BF16)

    loads[1].wait()
    bc = mm(normed[...], w_bc_v[...]).astype(BF16)
    bc_s[...] = bc[:, : 2 * STATE]
    for f in range(2):
        for r in range(2):
            at = 128 * f + 64 * r
            bct_send[r, f] = bc[at : at + 64, 2 * STATE :]

    pl.semaphore_wait(barrier, TM - 1 + HT - 1)

    def bc_copy(to):
        return remote(bct_send.at[to // GROUPS], bct.at[t], b_ssem.at[to], b_rsem.at[t], tm=to)

    def bc_pass(source):
        return remote(bct.at[source], bct.at[source], f_ssem.at[source], b_rsem.at[source], tm=t ^ 1)

    @pl.loop(1, 4)
    def _(k):
        bc_copy((t + 2 * k) % TM).start()

    bc_copy(t ^ 1).start()
    bct[t] = bct_send[own_row]

    def l_copy(to):
        return remote(l_send.at[to % GROUPS, to // GROUPS], ltr.at[t], l_ssem.at[to], l_rsem.at[t], tm=to)

    def chunk_of(chunk):
        return pl.ds(pl.multiple_of(chunk * CHUNK_COLS, CHUNK_COLS), CHUNK_COLS)

    def x_copy(to, chunk):
        rows = pl.ds(pl.multiple_of((to // GROUPS) * COLS + chunk * CHUNK_COLS, CHUNK_COLS), CHUNK_COLS)
        return remote(
            x_all.at[:, rows, lanes_of(to % GROUPS)], xt.at[t, :, chunk_of(chunk)],
            x_ssem.at[to], x_rsem.at[chunk, t], tm=to,
        )

    def owned(p):
        return p // 8, pl.ds(pl.multiple_of((p % 8) * 16, 16), 16)

    own_f, own_n = owned(h)

    def d_copy(to):
        return remote(d_send.at[to // 8], d_recv.at[h], d_ssem.at[to], d_rsem.at[h], height=to)

    def s_copy(to, half):
        f, rows = owned(to)
        return remote(s_send.at[half, f, rows], s_recv.at[half, h], s_ssem.at[to], s_rsem.at[half, h], height=to)

    def x_half(half):
        lanes = pl.ds(HALF * half, HALF)
        xh = mm(normed[...], w_in_v[:, lanes]).astype(BF16)
        x_all[0, :, lanes] = xh[:128]
        x_all[1, :, lanes] = xh[128:]

    loads[2].wait()
    loads[3].wait()
    x_half(0)
    logits = mm_rows(normed[...], w_dt_v[...]).astype(BF16).astype(F32)
    dt = softplus(logits + dt_bias[...])
    rates = jnp.concatenate([rate[0:1, :], rate[1:2, :]], axis=1)
    decay = -dt * rates * LOG2E
    both = jnp.concatenate([dt, decay, jnp.zeros((TOK, 32), F32)], axis=1)
    for r in range(2):
        turned = jnp.concatenate([both[64 * r : 64 * r + 64], both[128 + 64 * r : 192 + 64 * r]], axis=0).T
        for g in range(GROUPS):
            l_send[g, r, 0:8] = turned[24 + 6 * g : 32 + 6 * g]
            l_send[g, r, 8:16] = turned[72 + 6 * g : 80 + 6 * g]

    pad = jnp.zeros((TOK, 8), F32)
    dt_s = jnp.concatenate([dt[:, :HEADS], pad], axis=1)
    decay_s = jnp.concatenate([decay[:, :HEADS], pad], axis=1)
    row, col = iota((TOK, TOK), 0), iota((TOK, TOK), 1)
    order_s = ((row >= col) & ((row >> 7) == (col >> 7))).astype(F32).astype(BF16)
    run = cumulative(order_s, decay_s)
    run_s[...] = run
    for f in range(2):
        runt_s[f] = jnp.concatenate([run[128 * f : 128 * f + 128], jnp.zeros((128, 96), F32)], axis=1).T[:32]
    ends = [run[127:128], run[255:256]]
    for f in range(2):
        d_send[f] = jnp.broadcast_to(
            jnp.concatenate([jnp.exp2(ends[f]), jnp.zeros((1, 96), F32)], axis=1), (8, 128)
        )
    end = jnp.concatenate([jnp.broadcast_to(e, (128, 32)) for e in ends], axis=0)
    to_end = parts(jnp.exp2(end - run) * dt_s, 2)
    dt_parts = parts(dt_s, 2)
    from_start = parts(jnp.exp2(run), 2)

    def state_half(half):
        for part in range(2):
            lanes = pl.ds(HALF * half + GL * part, GL)
            spread = spread_s[0:64, lanes]
            weight = mm(to_end, spread)
            for f in range(2):
                rows = slice(128 * f, 128 * f + 128)
                x = x_all[f, :, lanes].astype(F32)
                s_send[half, f, :, pl.ds(GL * part, GL)] = mm_tokens(
                    bc_s[rows, :STATE], (x * weight[rows]).astype(BF16)
                ).astype(BF16)

        @pl.loop(1, HT)
        def _(k):
            s_copy((h + k) % HT, half).start()

        s_recv[half, h] = s_send[half, own_f, own_n, :]

    @pl.loop(1, HT)
    def _(k):
        d_copy((h + k) % HT).start()

    state_half(0)
    loads[4].wait()
    for load in loads[5:]:
        load.start()
    x_half(1)

    @pl.loop(1, TM)
    def _(k):
        l_copy((t + k) % TM).start()

    @pl.loop(0, CHUNKS)
    def _(chunk):
        @pl.loop(1, TM)
        def _(k):
            x_copy((t + k) % TM, chunk).start()

    state_half(1)

    ltr[t] = l_send[own_group, own_row]
    d_recv[h] = d_send[h // 8]
    own_rows = pl.ds(pl.multiple_of(own_row * COLS, COLS), COLS)
    for f in range(2):
        xt[t, f] = x_all[f, own_rows, lanes_of(own_group)]

    for part in range(4):
        lanes = pl.ds(GL * part, GL)
        steps = mm(dt_parts, spread_s[0:64, lanes])
        e_run[:, lanes] = mm(from_start, spread_s[0:64, lanes])
        for f in range(2):
            xd_s[f, :, lanes] = (x_all[f, :, lanes].astype(F32) * steps[128 * f : 128 * f + 128]).astype(BF16)

    @pl.loop(0, 4)
    def _(k):
        for step in range(2):
            @pl.when(k == 2 * step)
            def _():
                loads[5 + step].wait()
        v = mm(normed[...], w_in_v[:, pl.ds(pl.multiple_of(INNER + GL * k, 128), GL)]).astype(BF16).astype(F32)
        gate[:, lanes_of(k)] = v / (1.0 + jnp.exp(-v))

    @pl.loop(1, 4)
    def _(k):
        source = (t + 2 * k) % TM
        remote(bct_send.at[0], bct.at[source], b_ssem.at[source], b_rsem.at[source], tm=source).wait_recv()
        bc_pass(source).start()

    half = iota((128, 128), 1) < 64
    causal = iota((128, 128), 0) >= iota((128, 128), 1)

    @pl.loop(0, 2)
    def _(f):
        rows = pl.ds(pl.multiple_of(f * 128, 128), 128)
        b, c = bc_s[rows, :STATE], bc_s[rows, STATE:]
        scores = mm_rows(c, b)
        scores = jnp.where(causal, scores, 0.0)
        run_f, runt_f = run_s[rows, :], runt_s[f]
        for pair in range(HEADS // 2):
            weights = []
            for head in (2 * pair, 2 * pair + 1):
                spread = run_f[:, head : head + 1] - runt_f[head : head + 1, :]
                weights.append((scores * jnp.exp2(jnp.minimum(spread, 0.0))).astype(BF16))
            lanes = pl.ds(128 * pair, 128)
            x = xd_s[f, :, lanes]
            none = jnp.zeros_like(x)
            both_x = jnp.concatenate([jnp.where(half, x, none), jnp.where(half, none, x)], axis=0)
            sp_out[rows, lanes] = mm(jnp.concatenate(weights, axis=1), both_x)

    def band_decays():
        @pl.loop(1, HT)
        def _(k):
            source = (h + k) % HT
            remote(d_send.at[0], d_recv.at[source], d_ssem.at[source], d_rsem.at[source], height=source).wait_recv()

        totals = jnp.concatenate([d_recv[k, 0:1, :32] for k in range(HT)], axis=0)
        totals = parts(totals, 3)
        for half in range(2):
            d_exp[half] = mm(totals, spread_s[:, pl.ds(HALF * half, HALF)])

    def i_copy(to, half):
        f, rows = owned(h)
        return remote(
            inc_send.at[half, to], inc_recv.at[half, f, rows], i_ssem.at[to], i_rsem.at[half, h], height=to
        )

    def prefix(half):
        @pl.loop(1, HT)
        def _(k):
            source = (h + k) % HT
            remote(
                s_send.at[0, 0, pl.ds(0, 16)], s_recv.at[half, source],
                s_ssem.at[source], s_rsem.at[half, source], height=source,
            ).wait_recv()

        before = jnp.zeros((16, HALF), F32)
        for k in range(HT):
            inc_send[half, k] = before.astype(BF16)
            if k < HT - 1:
                before = before * d_exp[half, k : k + 1, :] + s_recv[half, k].astype(F32)

        @pl.loop(1, HT)
        def _(k):
            i_copy((h + k) % HT, half).start()

        inc_recv[half, own_f, own_n, :] = inc_send[half, h]

    @pl.loop(1, TM)
    def _(k):
        source = (t + k) % TM
        remote(l_send.at[0, 0], ltr.at[source], l_ssem.at[source], l_rsem.at[source], tm=source).wait_recv()

    @pl.loop(0, 4)
    def _(k):
        source = (t + 2 * k) % TM ^ 1
        remote(bct_send.at[0], bct.at[source], b_ssem.at[source], b_rsem.at[source], tm=source).wait_recv()

    columns = ltr[...].reshape(TM * 16, 128).T
    for s in range(TM):
        lcol[s] = columns[:, 16 * s : 16 * s + 16]

    state[...] = jnp.zeros_like(state)

    def y_copy(to, cols, half):
        return remote(
            y_send.at[to, :, cols], y_recv.at[t, :, cols], y_ssem.at[to], y_rsem.at[half, t], tm=to
        )

    @pl.loop(0, CHUNKS)
    def _(chunk):
        cols = chunk_of(chunk)

        @pl.loop(1, TM)
        def _(k):
            source = (t + k) % TM
            remote(
                x_all.at[:, pl.ds(0, CHUNK_COLS), pl.ds(0, GL)], xt.at[source, :, cols],
                x_ssem.at[source], x_rsem.at[chunk, source], tm=source,
            ).wait_recv()

        def tokens_of(f):
            return pl.ds(pl.multiple_of(f * COLS + chunk * CHUNK_COLS, CHUNK_COLS), CHUNK_COLS)

        def gathered(get, width):
            return jnp.concatenate([get(f).reshape(128, width) for f in range(2)], axis=0)

        x = gathered(lambda f: xt[:, f, cols, :], GL)
        bcv = gathered(lambda f: bct[:, f, cols, :], 2 * STATE)
        dl = gathered(lambda f: lcol[:, tokens_of(f), :], 16)
        b, c = bcv[:, :STATE], bcv[:, STATE:]
        dtv, decays = dl[:, :8], dl[:, 8:]
        runs = cumulative(order_t[...], decays)
        runs_row = jnp.concatenate([runs, jnp.zeros((TOK, 120), F32)], axis=1).T[:8]
        last = runs[TOK - 1 : TOK]
        weight = mm(parts(jnp.exp2(last - runs) * dtv, 2), spread_t[...])
        steps = mm(parts(dtv, 2), spread_t[...])
        grown = mm(parts(jnp.exp2(runs), 2), spread_t[...])
        scores = mm_rows(c, b)
        scores = scores * order_t[...].astype(F32)
        xf = x.astype(F32)
        xd = (xf * steps).astype(BF16)
        xw = (xf * weight).astype(BF16)
        earlier = mm(c, state[...].astype(BF16)) * grown
        state[...] = state[...] * grown[TOK - 1 : TOK] + mm_tokens(b, xw)
        half_x = iota((TOK, 128), 1) < 64
        for pair in range(GHEADS // 2):
            weights = []
            for head in (2 * pair, 2 * pair + 1):
                spread = runs[:, head : head + 1] - runs_row[head : head + 1, :]
                weights.append((scores * jnp.exp2(jnp.minimum(spread, 0.0))).astype(BF16))
            lanes = slice(128 * pair, 128 * pair + 128)
            xp = xd[:, lanes]
            none = jnp.zeros_like(xp)
            both_x = jnp.concatenate([jnp.where(half_x, xp, none), jnp.where(half_x, none, xp)], axis=0)
            y = mm(jnp.concatenate(weights, axis=1), both_x) + earlier[:, lanes]
            y = y.astype(BF16)
            for f in range(2):
                y_send[:, f, cols, lanes] = y[128 * f : 128 * f + 128].reshape(TM, CHUNK_COLS, 128)

        @pl.loop(1, TM)
        def _(k):
            y_copy((t + k) % TM, cols, chunk // 2).start()

        @pl.when(chunk == 0)
        def _():
            band_decays()

        @pl.when(chunk < 2)
        def _():
            prefix(chunk)

    y_recv[t] = y_send[t]

    for half in range(2):
        @pl.loop(1, HT)
        def _(k):
            source = (h + k) % HT
            f, rows = owned(source)
            remote(
                inc_send.at[half, source], inc_recv.at[half, f, rows],
                i_ssem.at[source], i_rsem.at[half, source], height=source,
            ).wait_recv()

        for f in range(2):
            rows = slice(128 * f, 128 * f + 128)
            for part in range(2):
                lanes = pl.ds(HALF * half + GL * part, GL)
                earlier = mm(bc_s[rows, STATE:], inc_recv[half, f, :, pl.ds(GL * part, GL)])
                sp_out[rows, lanes] += e_run[rows, lanes] * earlier

    @pl.loop(0, 2)
    def _(part):
        cols = pl.ds(pl.multiple_of(part * 32, 32), 32)

        @pl.loop(1, TM)
        def _(k):
            source = (t + k) % TM
            remote(
                y_send.at[source, :, cols], y_recv.at[source, :, cols],
                y_ssem.at[source], y_rsem.at[part, source], tm=source,
            ).wait_recv()

        @pl.loop(0, 4)
        def _(k):
            f, r = k // 2, k % 2
            rows = pl.ds(pl.multiple_of(k * COLS + part * 32, 32), 32)
            temporal = jnp.concatenate([y_recv[GROUPS * r + g, f, cols, :] for g in range(GROUPS)], axis=1)
            gated = (sp_out[rows, :] + temporal.astype(F32)) * gate[rows, :]
            mean_square = jnp.mean(gated * gated, axis=-1, keepdims=True)
            out[rows, :] = (gated * lax.rsqrt(mean_square + EPSILON) * out_gain[...].reshape(1, INNER)).astype(BF16)

    bc_copy(t ^ 1).wait_send()

    @pl.loop(1, 4)
    def _(k):
        bc_copy((t + 2 * k) % TM).wait_send()
        bc_pass((t + 2 * k) % TM).wait_send()

    @pl.loop(1, TM)
    def _(k):
        to = (t + k) % TM
        l_copy(to).wait_send()
        remote(xt.at[to], xt.at[to], x_ssem.at[to], x_rsem.at[0, to], tm=to).wait_send()
        y_copy(to, pl.ds(0, COLS), 0).wait_send()

    @pl.loop(1, HT)
    def _(k):
        to = (h + k) % HT
        d_copy(to).wait_send()
        for half in range(2):
            s_copy(to, half).wait_send()
            i_copy(to, half).wait_send()


def per_device(tokens, norm_gain, in_weight, bc_weight, dt_weight, dt_bias, decay_rate, out_gain, out_weight):
    vmem = pl.BlockSpec(memory_space=pltpu.VMEM)
    hbm = pl.BlockSpec(memory_space=pl.ANY)
    dma = pltpu.SemaphoreType.DMA
    normed_out = pl.pallas_call(
        kernel,
        out_shape=jax.ShapeDtypeStruct((TOK, INNER), BF16),
        in_specs=[hbm, vmem, hbm, hbm, hbm, vmem, vmem, vmem],
        out_specs=vmem,
        scratch_shapes=[
            pltpu.VMEM((TOK, D), BF16),
            pltpu.VMEM((D, 2 * INNER), BF16),
            pltpu.VMEM((D, 4 * STATE), BF16),
            pltpu.VMEM((2 * HEADS, D), BF16),
            pltpu.VMEM((TOK, D), BF16),
            pltpu.VMEM((2, 128, INNER), BF16),
            pltpu.VMEM((TOK, INNER), F32),
            pltpu.VMEM((TOK, 2 * STATE), BF16),
            pltpu.VMEM((2, 2, COLS, 2 * STATE), BF16),
            pltpu.VMEM((GROUPS, 2, 16, 128), F32),
            pltpu.VMEM((2, 8, 128), F32),
            pltpu.VMEM((2, 2, STATE, HALF), BF16),
            pltpu.VMEM((TM, 2, COLS, GL), BF16),
            pltpu.VMEM((TM, 2, COLS, 2 * STATE), BF16),
            pltpu.VMEM((TM, 16, 128), F32),
            pltpu.VMEM((HT, 8, 128), F32),
            pltpu.VMEM((2, HT, 16, HALF), BF16),
            pltpu.VMEM((2, HT, 16, HALF), BF16),
            pltpu.VMEM((2, 2, STATE, HALF), BF16),
            pltpu.VMEM((TM, 2, COLS, GL), BF16),
            pltpu.VMEM((TM, 2, COLS, GL), BF16),
            pltpu.VMEM((2, 128, INNER), BF16),
            pltpu.VMEM((TOK, INNER), F32),
            pltpu.VMEM((TOK, INNER), F32),
            pltpu.VMEM((TOK, 32), F32),
            pltpu.VMEM((2, 32, 128), F32),
            pltpu.VMEM((96, INNER), BF16),
            pltpu.VMEM((16, GL), BF16),
            pltpu.VMEM((TOK, TOK), BF16),
            pltpu.VMEM((TM, 128, 16), F32),
            pltpu.VMEM((STATE, GL), F32),
            pltpu.VMEM((2, HT, HALF), F32),
            dma((8,)),
            dma((TM,)), dma((CHUNKS, TM)),
            dma((TM,)), dma((TM,)), dma((TM,)),
            dma((TM,)), dma((TM,)),
            dma((HT,)), dma((HT,)),
            dma((HT,)), dma((2, HT)),
            dma((HT,)), dma((2, HT)),
            dma((TM,)), dma((2, TM)),
        ],
        compiler_params=pltpu.CompilerParams(
            collective_id=0, has_side_effects=True, vmem_limit_bytes=56 * 1024 * 1024
        ),
        name="layer",
    )(
        tokens.reshape(TOK, D),
        norm_gain,
        in_weight,
        bc_weight,
        dt_weight.T,
        dt_bias.reshape(1, 2 * HEADS),
        decay_rate,
        out_gain,
    )
    return mm(normed_out, out_weight).astype(BF16).reshape(tokens.shape)


def solution(mesh):
    in_specs = (P("tm", "height", None, None), P(), P(), P(), P(), P(), P(), P(), P())
    out_specs = P("tm", "height", None, None)
    return jax.shard_map(
        per_device, mesh=mesh, in_specs=in_specs, out_specs=out_specs, check_vma=False
    )
```

```python
import functools

import jax
import jax.numpy as jnp
from jax import lax
from jax.experimental import pallas as pl
from jax.experimental.pallas import tpu as pltpu
from jax.sharding import PartitionSpec as P

EPSILON = 1e-05
LOG2E = 1.4426950408889634
BF16 = jnp.bfloat16
F32 = jnp.float32

D = 1536
INNER = 1536
HEADS = 24
STATE = 128
COLS = 64
TM = 8
HT = 16
GROUPS = 4
GHEADS = HEADS // GROUPS
GL = GHEADS * 64
HALF = INNER // 2
TOK = 256
CHUNK_COLS = 16
CHUNKS = COLS // CHUNK_COLS


def mm(a, b):
    return jnp.dot(a, b, preferred_element_type=F32)


def mm_tokens(a, b):
    return lax.dot_general(a, b, (((0,), (0,)), ((), ())), preferred_element_type=F32)


def mm_rows(a, b):
    return lax.dot_general(a, b, (((1,), (1,)), ((), ())), preferred_element_type=F32)


def softplus(v):
    return jnp.maximum(v, 0.0) + jnp.log1p(jnp.exp(-jnp.abs(v)))


def parts(v, count):
    pieces, rest = [], v
    for _ in range(count):
        piece = rest.astype(BF16).astype(F32)
        pieces.append(piece)
        rest = rest - piece
    return jnp.concatenate(pieces, axis=1).astype(BF16)


def cumulative(order, v):
    width = v.shape[1]
    sums = mm(order, parts(v, 3))
    return sums[:, :width] + sums[:, width : 2 * width] + sums[:, 2 * width :]


def iota(shape, dim):
    return lax.broadcasted_iota(jnp.int32, shape, dim)


def kernel(
    tokens, gain_in, w_in, w_bc, w_dt, dt_bias_in, rate_in, out_gain_in, w_out, out,
    gain, dt_bias, rate, out_gain,
    tok_v, w_in_v, w_bc_v, w_dt_v, w_out_v,
    normed, x_all, gate, bc_s, bct_send, l_send, s_send,
    xt, bct, ltr, s_recv, inc_send, inc_recv, y_send, y_recv,
    xd_s, sp_out, e_run, run_s, runt_s, spread_s, spread_t, order_t, lcol, state, d_exp,
    mixed_v, load_sem, small_sem, out_sem, x_ssem, x_rsem, b_ssem, b_rsem, f_ssem, l_ssem, l_rsem,
    s_ssem, s_rsem, i_ssem, i_rsem, y_ssem, y_rsem,
):
    t = lax.axis_index("tm")
    h = lax.axis_index("height")

    def remote(src, dst, ssem, rsem, **where):
        return pltpu.make_async_remote_copy(
            src_ref=src, dst_ref=dst, send_sem=ssem, recv_sem=rsem,
            device_id=where, device_id_type=pl.DeviceIdType.MESH,
        )

    own_row, own_group = t // GROUPS, t % GROUPS

    def lanes_of(index):
        return pl.ds(pl.multiple_of(index * GL, 128), GL)

    def half_lanes(start, half):
        return pl.ds(pl.multiple_of(start + half * HALF, 128), HALF)

    loads = [
        pltpu.make_async_copy(tokens, tok_v, load_sem.at[0]),
        pltpu.make_async_copy(w_bc, w_bc_v, load_sem.at[1]),
        pltpu.make_async_copy(w_dt, w_dt_v, load_sem.at[2]),
    ]
    for step in range(4):
        where = pl.ds(HALF * step, HALF)
        loads.append(pltpu.make_async_copy(w_in.at[:, where], w_in_v.at[:, where], load_sem.at[3 + step]))
    loads.append(pltpu.make_async_copy(w_out, w_out_v, load_sem.at[7]))
    small = [
        pltpu.make_async_copy(source, target, small_sem.at[k])
        for k, (source, target) in enumerate(
            ((gain_in, gain), (dt_bias_in, dt_bias), (rate_in, rate), (out_gain_in, out_gain))
        )
    ]
    small[0].start()
    for load in loads[:5]:
        load.start()
    for load in small[1:]:
        load.start()

    barrier = pltpu.get_barrier_semaphore()

    @pl.loop(1, TM)
    def _(k):
        pl.semaphore_signal(barrier, inc=1, device_id={"tm": (t + k) % TM}, device_id_type=pl.DeviceIdType.MESH)

    @pl.loop(1, HT)
    def _(k):
        pl.semaphore_signal(barrier, inc=1, device_id={"height": (h + k) % HT}, device_id_type=pl.DeviceIdType.MESH)

    spread_s[...] = ((iota((96, INNER), 0) & 31) == (iota((96, INNER), 1) >> 6)).astype(F32).astype(BF16)
    spread_t[...] = ((iota((16, GL), 0) & 7) == (iota((16, GL), 1) >> 6)).astype(F32).astype(BF16)

    def place(index):
        return (index & 15) * 16 + ((index >> 4) & 7) * 2 + (index >> 7)

    order_t[...] = (place(iota((TOK, TOK), 0)) >= place(iota((TOK, TOK), 1))).astype(F32).astype(BF16)

    small[0].wait()
    loads[0].wait()

    @pl.loop(0, 8)
    def _(k):
        rows = pl.ds(pl.multiple_of(k * 32, 32), 32)
        v = tok_v[rows, :].astype(F32)
        mean_square = jnp.mean(v * v, axis=-1, keepdims=True)
        normed[rows, :] = (v * lax.rsqrt(mean_square + EPSILON) * gain[...].reshape(1, D)).astype(BF16)

    loads[1].wait()
    bc = mm(normed[...], w_bc_v[...]).astype(BF16)
    bc_s[...] = bc[:, : 2 * STATE]
    for f in range(2):
        for r in range(2):
            at = 128 * f + 64 * r
            bct_send[r, f] = bc[at : at + 64, 2 * STATE :]

    pl.semaphore_wait(barrier, TM - 1 + HT - 1)

    def bc_copy(to):
        return remote(bct_send.at[to // GROUPS], bct.at[t], b_ssem.at[to], b_rsem.at[t], tm=to)

    def bc_pass(source):
        return remote(bct.at[source], bct.at[source], f_ssem.at[source], b_rsem.at[source], tm=t ^ 1)

    @pl.loop(1, 4)
    def _(k):
        bc_copy((t + 2 * k) % TM).start()

    bc_copy(t ^ 1).start()
    bct[t] = bct_send[own_row]

    def l_copy(to):
        return remote(l_send.at[to % GROUPS, to // GROUPS], ltr.at[t], l_ssem.at[to], l_rsem.at[t], tm=to)

    def chunk_of(chunk):
        return pl.ds(pl.multiple_of(chunk * CHUNK_COLS, CHUNK_COLS), CHUNK_COLS)

    def x_copy(to, chunk):
        rows = pl.ds(pl.multiple_of((to // GROUPS) * COLS + chunk * CHUNK_COLS, CHUNK_COLS), CHUNK_COLS)
        return remote(
            x_all.at[:, rows, lanes_of(to % GROUPS)], xt.at[t, :, chunk_of(chunk)],
            x_ssem.at[to], x_rsem.at[chunk, t], tm=to,
        )

    def owned(p):
        return p // 8, pl.ds(pl.multiple_of((p % 8) * 16, 16), 16)

    own_f, own_n = owned(h)

    def s_copy(to, half):
        f, rows = owned(to)
        lanes = pl.ds(0, HALF + 128 * (1 - half))
        return remote(
            s_send.at[half, f, rows, lanes], s_recv.at[half, h, :, lanes],
            s_ssem.at[to], s_rsem.at[half, h], height=to,
        )

    def x_half(half):
        lanes = pl.ds(HALF * half, HALF)
        xh = mm(normed[...], w_in_v[:, lanes]).astype(BF16)
        x_all[0, :, lanes] = xh[:128]
        x_all[1, :, lanes] = xh[128:]

    for load in small[1:]:
        load.wait()
    loads[2].wait()
    loads[3].wait()
    x_half(0)
    logits = mm_rows(normed[...], w_dt_v[...]).astype(BF16).astype(F32)
    dt = softplus(logits + dt_bias[...])
    rates = jnp.concatenate([rate[0:1, :], rate[1:2, :]], axis=1)
    decay = -dt * rates * LOG2E
    both = jnp.concatenate([dt, decay, jnp.zeros((TOK, 32), F32)], axis=1)
    for r in range(2):
        turned = jnp.concatenate([both[64 * r : 64 * r + 64], both[128 + 64 * r : 192 + 64 * r]], axis=0).T
        for g in range(GROUPS):
            l_send[g, r, 0:8] = turned[24 + 6 * g : 32 + 6 * g]
            l_send[g, r, 8:16] = turned[72 + 6 * g : 80 + 6 * g]

    pad = jnp.zeros((TOK, 8), F32)
    dt_s = jnp.concatenate([dt[:, :HEADS], pad], axis=1)
    decay_s = jnp.concatenate([decay[:, :HEADS], pad], axis=1)
    row, col = iota((TOK, TOK), 0), iota((TOK, TOK), 1)
    order_s = ((row >= col) & ((row >> 7) == (col >> 7))).astype(F32).astype(BF16)
    run = cumulative(order_s, decay_s)
    run_s[...] = run
    for f in range(2):
        runt_s[f] = jnp.concatenate([run[128 * f : 128 * f + 128], jnp.zeros((128, 96), F32)], axis=1).T[:32]
    ends = [run[127:128], run[255:256]]
    for f in range(2):
        total = jnp.concatenate([parts(jnp.exp2(ends[f]), 3).astype(F32), jnp.zeros((1, 32), F32)], axis=1)
        s_send[0, f, :, HALF:] = jnp.broadcast_to(total, (STATE, 128)).astype(BF16)
    end = jnp.concatenate([jnp.broadcast_to(e, (128, 32)) for e in ends], axis=0)
    to_end = parts(jnp.exp2(end - run) * dt_s, 2)
    dt_parts = parts(dt_s, 2)
    from_start = parts(jnp.exp2(run), 2)

    def state_half(half):
        for part in range(2):
            lanes = pl.ds(HALF * half + GL * part, GL)
            spread = spread_s[0:64, lanes]
            weight = mm(to_end, spread)
            for f in range(2):
                rows = slice(128 * f, 128 * f + 128)
                x = x_all[f, :, lanes].astype(F32)
                s_send[half, f, :, pl.ds(GL * part, GL)] = mm_tokens(
                    bc_s[rows, :STATE], (x * weight[rows]).astype(BF16)
                ).astype(BF16)

        @pl.loop(1, HT)
        def _(k):
            s_copy((h + k) % HT, half).start()

        lanes = pl.ds(0, HALF + 128 * (1 - half))
        s_recv[half, h, :, lanes] = s_send[half, own_f, own_n, lanes]

    loads[4].wait()
    for load in loads[5:]:
        load.start()
    x_half(1)

    def x_send(chunk):
        @pl.loop(1, TM)
        def _(k):
            x_copy((t + k) % TM, chunk).start()

    x_send(0)
    state_half(0)
    x_send(1)

    @pl.loop(1, TM)
    def _(k):
        l_copy((t + k) % TM).start()

    state_half(1)
    x_send(2)
    x_send(3)

    ltr[t] = l_send[own_group, own_row]
    own_rows = pl.ds(pl.multiple_of(own_row * COLS, COLS), COLS)
    for f in range(2):
        xt[t, f] = x_all[f, own_rows, lanes_of(own_group)]

    for part in range(4):
        lanes = pl.ds(GL * part, GL)
        steps = mm(dt_parts, spread_s[0:64, lanes])
        e_run[:, lanes] = mm(from_start, spread_s[0:64, lanes])
        for f in range(2):
            xd_s[f, :, lanes] = (x_all[f, :, lanes].astype(F32) * steps[128 * f : 128 * f + 128]).astype(BF16)

    @pl.loop(0, 4)
    def _(k):
        for step in range(2):
            @pl.when(k == 2 * step)
            def _():
                loads[5 + step].wait()
        v = mm(normed[...], w_in_v[:, pl.ds(pl.multiple_of(INNER + GL * k, 128), GL)]).astype(BF16).astype(F32)
        gate[:, lanes_of(k)] = v / (1.0 + jnp.exp(-v))

    @pl.loop(1, 4)
    def _(k):
        source = (t + 2 * k) % TM
        remote(bct_send.at[0], bct.at[source], b_ssem.at[source], b_rsem.at[source], tm=source).wait_recv()
        bc_pass(source).start()

    half = iota((128, 128), 1) < 64
    causal = iota((128, 128), 0) >= iota((128, 128), 1)

    @pl.loop(0, 2)
    def _(f):
        rows = pl.ds(pl.multiple_of(f * 128, 128), 128)
        b, c = bc_s[rows, :STATE], bc_s[rows, STATE:]
        scores = mm_rows(c, b)
        scores = jnp.where(causal, scores, 0.0)
        run_f, runt_f = run_s[rows, :], runt_s[f]
        for pair in range(HEADS // 2):
            weights = []
            for head in (2 * pair, 2 * pair + 1):
                spread = run_f[:, head : head + 1] - runt_f[head : head + 1, :]
                weights.append((scores * jnp.exp2(jnp.minimum(spread, 0.0))).astype(BF16))
            lanes = pl.ds(128 * pair, 128)
            x = xd_s[f, :, lanes]
            none = jnp.zeros_like(x)
            both_x = jnp.concatenate([jnp.where(half, x, none), jnp.where(half, none, x)], axis=0)
            sp_out[rows, lanes] = mm(jnp.concatenate(weights, axis=1), both_x)

    def band_decays():
        row = iota((HT, 128), 0)
        totals = jnp.zeros((HT, 128), F32)
        for k in range(HT):
            totals = jnp.where(row == k, s_recv[0, k, :, HALF:].astype(F32), totals)
        totals = totals[:, :96].astype(BF16)
        for half in range(2):
            d_exp[half] = mm(totals, spread_s[:, pl.ds(HALF * half, HALF)])

    def i_copy(to, half):
        f, rows = owned(h)
        return remote(
            inc_send.at[half, to], inc_recv.at[half, f, rows], i_ssem.at[to], i_rsem.at[half, h], height=to
        )

    def prefix(half):
        @pl.loop(1, HT)
        def _(k):
            source = (h + k) % HT
            lanes = pl.ds(0, HALF + 128 * (1 - half))
            remote(
                s_send.at[half, 0, pl.ds(0, 16), lanes], s_recv.at[half, source, :, lanes],
                s_ssem.at[source], s_rsem.at[half, source], height=source,
            ).wait_recv()

        if half == 0:
            band_decays()

        before = jnp.zeros((16, HALF), F32)
        for k in range(HT):
            inc_send[half, k] = before.astype(BF16)
            if k < HT - 1:
                before = before * d_exp[half, k : k + 1, :] + s_recv[half, k, :, :HALF].astype(F32)

        @pl.loop(1, HT)
        def _(k):
            i_copy((h + k) % HT, half).start()

        inc_recv[half, own_f, own_n, :] = inc_send[half, h]

    @pl.loop(1, TM)
    def _(k):
        source = (t + k) % TM
        remote(l_send.at[0, 0], ltr.at[source], l_ssem.at[source], l_rsem.at[source], tm=source).wait_recv()

    @pl.loop(0, 4)
    def _(k):
        source = (t + 2 * k) % TM ^ 1
        remote(bct_send.at[0], bct.at[source], b_ssem.at[source], b_rsem.at[source], tm=source).wait_recv()

    columns = ltr[...].reshape(TM * 16, 128).T
    for s in range(TM):
        lcol[s] = columns[:, 16 * s : 16 * s + 16]

    state[...] = jnp.zeros_like(state)

    def y_copy(to, cols, half):
        return remote(
            y_send.at[to, :, cols], y_recv.at[t, :, cols], y_ssem.at[to], y_rsem.at[half, t], tm=to
        )

    @pl.loop(0, CHUNKS)
    def _(chunk):
        cols = chunk_of(chunk)

        @pl.loop(1, TM)
        def _(k):
            source = (t + k) % TM
            remote(
                x_all.at[:, pl.ds(0, CHUNK_COLS), pl.ds(0, GL)], xt.at[source, :, cols],
                x_ssem.at[source], x_rsem.at[chunk, source], tm=source,
            ).wait_recv()

        def tokens_of(f):
            return pl.ds(pl.multiple_of(f * COLS + chunk * CHUNK_COLS, CHUNK_COLS), CHUNK_COLS)

        def gathered(get, width):
            return jnp.concatenate([get(f).reshape(128, width) for f in range(2)], axis=0)

        x = gathered(lambda f: xt[:, f, cols, :], GL)
        bcv = gathered(lambda f: bct[:, f, cols, :], 2 * STATE)
        dl = gathered(lambda f: lcol[:, tokens_of(f), :], 16)
        b, c = bcv[:, :STATE], bcv[:, STATE:]
        dtv, decays = dl[:, :8], dl[:, 8:]
        runs = cumulative(order_t[...], decays)
        runs_row = jnp.concatenate([runs, jnp.zeros((TOK, 120), F32)], axis=1).T[:8]
        last = runs[TOK - 1 : TOK]
        weight = mm(parts(jnp.exp2(last - runs) * dtv, 2), spread_t[...])
        steps = mm(parts(dtv, 2), spread_t[...])
        grown = mm(parts(jnp.exp2(runs), 2), spread_t[...])
        scores = mm_rows(c, b)
        scores = scores * order_t[...].astype(F32)
        xf = x.astype(F32)
        xd = (xf * steps).astype(BF16)
        xw = (xf * weight).astype(BF16)
        earlier = mm(c, state[...].astype(BF16)) * grown
        state[...] = state[...] * grown[TOK - 1 : TOK] + mm_tokens(b, xw)
        half_x = iota((TOK, 128), 1) < 64
        for pair in range(GHEADS // 2):
            weights = []
            for head in (2 * pair, 2 * pair + 1):
                spread = runs[:, head : head + 1] - runs_row[head : head + 1, :]
                weights.append((scores * jnp.exp2(jnp.minimum(spread, 0.0))).astype(BF16))
            lanes = slice(128 * pair, 128 * pair + 128)
            xp = xd[:, lanes]
            none = jnp.zeros_like(xp)
            both_x = jnp.concatenate([jnp.where(half_x, xp, none), jnp.where(half_x, none, xp)], axis=0)
            y = mm(jnp.concatenate(weights, axis=1), both_x) + earlier[:, lanes]
            y = y.astype(BF16)
            for f in range(2):
                y_send[:, f, cols, lanes] = y[128 * f : 128 * f + 128].reshape(TM, CHUNK_COLS, 128)

        @pl.loop(1, TM)
        def _(k):
            y_copy((t + k) % TM, cols, chunk // 2).start()

        for half in range(2):
            @pl.when(chunk == half)
            def _():
                prefix(half)

    y_recv[t] = y_send[t]

    for half in range(2):
        @pl.loop(1, HT)
        def _(k):
            source = (h + k) % HT
            f, rows = owned(source)
            remote(
                inc_send.at[half, source], inc_recv.at[half, f, rows],
                i_ssem.at[source], i_rsem.at[half, source], height=source,
            ).wait_recv()

        for f in range(2):
            rows = slice(128 * f, 128 * f + 128)
            for part in range(2):
                lanes = pl.ds(HALF * half + GL * part, GL)
                earlier = mm(bc_s[rows, STATE:], inc_recv[half, f, :, pl.ds(GL * part, GL)])
                sp_out[rows, lanes] += e_run[rows, lanes] * earlier

    def out_copy(part, k):
        rows = pl.ds(pl.multiple_of(k * COLS + part * 32, 32), 32)
        return pltpu.make_async_copy(mixed_v.at[part, k], out.at[rows], out_sem.at[part, k])

    @pl.loop(0, 2)
    def _(part):
        cols = pl.ds(pl.multiple_of(part * 32, 32), 32)

        @pl.loop(1, TM)
        def _(k):
            source = (t + k) % TM
            remote(
                y_send.at[source, :, cols], y_recv.at[source, :, cols],
                y_ssem.at[source], y_rsem.at[part, source], tm=source,
            ).wait_recv()

        for k in range(4):
            f, r = k // 2, k % 2
            rows = pl.ds(pl.multiple_of(k * COLS + part * 32, 32), 32)
            temporal = jnp.concatenate([y_recv[GROUPS * r + g, f, cols, :] for g in range(GROUPS)], axis=1)
            gated = (sp_out[rows, :] + temporal.astype(F32)) * gate[rows, :]
            mean_square = jnp.mean(gated * gated, axis=-1, keepdims=True)
            normed[32 * k : 32 * k + 32, :] = (
                gated * lax.rsqrt(mean_square + EPSILON) * out_gain[...].reshape(1, INNER)
            ).astype(BF16)

        @pl.when(part == 0)
        def _():
            loads[7].wait()

        @pl.loop(0, 2)
        def _(k):
            lanes = pl.ds(pl.multiple_of(HALF * k, 128), HALF)
            mixed = mm(normed[0:128, :], w_out_v[:, lanes]).astype(BF16)
            for block in range(4):
                mixed_v[part, block, :, lanes] = mixed[32 * block : 32 * block + 32]

        @pl.loop(0, 4)
        def _(k):
            out_copy(part, k).start()

    @pl.loop(0, 4)
    def _(k):
        out_copy(0, k).wait()
        out_copy(1, k).wait()

    bc_copy(t ^ 1).wait_send()

    @pl.loop(1, 4)
    def _(k):
        bc_copy((t + 2 * k) % TM).wait_send()
        bc_pass((t + 2 * k) % TM).wait_send()

    @pl.loop(1, TM)
    def _(k):
        to = (t + k) % TM
        l_copy(to).wait_send()
        remote(xt.at[to], xt.at[to], x_ssem.at[to], x_rsem.at[0, to], tm=to).wait_send()
        y_copy(to, pl.ds(0, COLS), 0).wait_send()

    @pl.loop(1, HT)
    def _(k):
        to = (h + k) % HT
        for half in range(2):
            s_copy(to, half).wait_send()
            i_copy(to, half).wait_send()


def per_device(tokens, norm_gain, in_weight, bc_weight, dt_weight, dt_bias, decay_rate, out_gain, out_weight):
    hbm = pl.BlockSpec(memory_space=pl.ANY)
    dma = pltpu.SemaphoreType.DMA
    def keep(v):
        return pltpu.with_memory_space_constraint(v, pltpu.HBM)

    mixed = pl.pallas_call(
        kernel,
        out_shape=jax.ShapeDtypeStruct((TOK, D), BF16),
        in_specs=[hbm] * 9,
        out_specs=pl.BlockSpec(memory_space=pltpu.VMEM),
        scratch_shapes=[
            pltpu.VMEM((D,), F32),
            pltpu.VMEM((1, 2 * HEADS), F32),
            pltpu.VMEM((2, HEADS), F32),
            pltpu.VMEM((INNER,), F32),
            pltpu.VMEM((TOK, D), BF16),
            pltpu.VMEM((D, 2 * INNER), BF16),
            pltpu.VMEM((D, 4 * STATE), BF16),
            pltpu.VMEM((2 * HEADS, D), BF16),
            pltpu.VMEM((INNER, D), BF16),
            pltpu.VMEM((TOK, D), BF16),
            pltpu.VMEM((2, 128, INNER), BF16),
            pltpu.VMEM((TOK, INNER), F32),
            pltpu.VMEM((TOK, 2 * STATE), BF16),
            pltpu.VMEM((2, 2, COLS, 2 * STATE), BF16),
            pltpu.VMEM((GROUPS, 2, 16, 128), F32),
            pltpu.VMEM((2, 2, STATE, HALF + 128), BF16),
            pltpu.VMEM((TM, 2, COLS, GL), BF16),
            pltpu.VMEM((TM, 2, COLS, 2 * STATE), BF16),
            pltpu.VMEM((TM, 16, 128), F32),
            pltpu.VMEM((2, HT, 16, HALF + 128), BF16),
            pltpu.VMEM((2, HT, 16, HALF), BF16),
            pltpu.VMEM((2, 2, STATE, HALF), BF16),
            pltpu.VMEM((TM, 2, COLS, GL), BF16),
            pltpu.VMEM((TM, 2, COLS, GL), BF16),
            pltpu.VMEM((2, 128, INNER), BF16),
            pltpu.VMEM((TOK, INNER), F32),
            pltpu.VMEM((TOK, INNER), F32),
            pltpu.VMEM((TOK, 32), F32),
            pltpu.VMEM((2, 32, 128), F32),
            pltpu.VMEM((96, INNER), BF16),
            pltpu.VMEM((16, GL), BF16),
            pltpu.VMEM((TOK, TOK), BF16),
            pltpu.VMEM((TM, 128, 16), F32),
            pltpu.VMEM((STATE, GL), F32),
            pltpu.VMEM((2, HT, HALF), F32),
            pltpu.VMEM((2, 4, 32, D), BF16),
            dma((8,)), dma((4,)), dma((2, 4)),
            dma((TM,)), dma((CHUNKS, TM)),
            dma((TM,)), dma((TM,)), dma((TM,)),
            dma((TM,)), dma((TM,)),
            dma((HT,)), dma((2, HT)),
            dma((HT,)), dma((2, HT)),
            dma((TM,)), dma((2, TM)),
        ],
        compiler_params=pltpu.CompilerParams(
            collective_id=0, has_side_effects=True, vmem_limit_bytes=40 * 1024 * 1024
        ),
        name="layer",
    )(
        keep(tokens.reshape(TOK, D)),
        keep(norm_gain),
        keep(in_weight),
        keep(bc_weight),
        keep(dt_weight.T),
        keep(dt_bias.reshape(1, 2 * HEADS)),
        keep(decay_rate),
        keep(out_gain),
        keep(out_weight),
    )
    return mixed.reshape(tokens.shape)


def solution(mesh):
    in_specs = (P("tm", "height", None, None), P(), P(), P(), P(), P(), P(), P(), P())
    out_specs = P("tm", "height", None, None)
    return jax.shard_map(
        per_device, mesh=mesh, in_specs=in_specs, out_specs=out_specs, check_vma=False
    )
```

```python
import functools

import jax
import jax.numpy as jnp
from jax import lax
from jax.experimental import pallas as pl
from jax.experimental.pallas import tpu as pltpu
from jax.sharding import PartitionSpec as P

EPSILON = 1e-05
LOG2E = 1.4426950408889634
BF16 = jnp.bfloat16
F32 = jnp.float32

D = 1536
INNER = 1536
HEADS = 24
STATE = 128
COLS = 64
TM = 8
HT = 16
GROUPS = 4
GHEADS = HEADS // GROUPS
GL = GHEADS * 64
HALF = INNER // 2
TOK = 256
CHUNK_COLS = 16
CHUNKS = COLS // CHUNK_COLS


def mm(a, b):
    return jnp.dot(a, b, preferred_element_type=F32)


def mm_tokens(a, b):
    return lax.dot_general(a, b, (((0,), (0,)), ((), ())), preferred_element_type=F32)


def mm_rows(a, b):
    return lax.dot_general(a, b, (((1,), (1,)), ((), ())), preferred_element_type=F32)


def softplus(v):
    return jnp.maximum(v, 0.0) + jnp.log1p(jnp.exp(-jnp.abs(v)))


def parts(v, count):
    pieces, rest = [], v
    for _ in range(count):
        piece = rest.astype(BF16).astype(F32)
        pieces.append(piece)
        rest = rest - piece
    return jnp.concatenate(pieces, axis=1).astype(BF16)


def cumulative(order, v):
    width = v.shape[1]
    sums = mm(order, parts(v, 3))
    return sums[:, :width] + sums[:, width : 2 * width] + sums[:, 2 * width :]


def iota(shape, dim):
    return lax.broadcasted_iota(jnp.int32, shape, dim)


def kernel(
    tokens, gain_in, w_in, w_bc, w_dt, dt_bias_in, rate_in, out_gain_in, w_out, out,
    gain, dt_bias, rate, out_gain,
    tok_v, w_in_v, w_bc_v, w_dt_v, w_out_v,
    normed, x_all, gate, bc_s, bct_send, l_send, s_send,
    xt, bct, ltr, s_recv, inc_send, inc_recv, y_send, y_recv,
    xd_s, sp_out, e_run, run_s, runt_s, spread_s, spread_t, order_t, lcol, state, d_exp,
    scale_v, scale_in, load_sem, small_sem, x_ssem, x_rsem, b_ssem, b_rsem, l_ssem, l_rsem,
    s_ssem, s_rsem, i_ssem, i_rsem, y_ssem, y_rsem,
):
    t = lax.axis_index("tm")
    h = lax.axis_index("height")

    def remote(src, dst, ssem, rsem, **where):
        return pltpu.make_async_remote_copy(
            src_ref=src, dst_ref=dst, send_sem=ssem, recv_sem=rsem,
            device_id=where, device_id_type=pl.DeviceIdType.MESH,
        )

    def received(ref, sem):
        remote(ref, ref, sem, sem, tm=t ^ 1).wait_recv()

    def sent(ref, sem):
        remote(ref, ref, sem, sem, tm=t ^ 1).wait_send()

    own_row, own_group = t // GROUPS, t % GROUPS

    def lanes_of(index):
        return pl.ds(pl.multiple_of(index * GL, 128), GL)

    def half_lanes(start, half):
        return pl.ds(pl.multiple_of(start + half * HALF, 128), HALF)

    loads = [
        pltpu.make_async_copy(tokens, tok_v, load_sem.at[0]),
        pltpu.make_async_copy(w_bc, w_bc_v, load_sem.at[1]),
        pltpu.make_async_copy(w_dt, w_dt_v, load_sem.at[2]),
    ]
    for step in range(4):
        where = pl.ds(HALF * step, HALF)
        loads.append(pltpu.make_async_copy(w_in.at[:, where], w_in_v.at[:, where], load_sem.at[3 + step]))
    loads.append(pltpu.make_async_copy(w_out, w_out_v, load_sem.at[7]))
    small = [
        pltpu.make_async_copy(source, target, small_sem.at[k])
        for k, (source, target) in enumerate(
            ((gain_in, gain), (dt_bias_in, dt_bias), (rate_in, rate), (out_gain_in, out_gain))
        )
    ]
    small[0].start()
    for load in loads[:5]:
        load.start()
    for load in small[1:]:
        load.start()

    barrier = pltpu.get_barrier_semaphore()

    @pl.loop(1, TM)
    def _(k):
        pl.semaphore_signal(barrier, inc=1, device_id={"tm": (t + k) % TM}, device_id_type=pl.DeviceIdType.MESH)

    @pl.loop(1, HT)
    def _(k):
        pl.semaphore_signal(barrier, inc=1, device_id={"height": (h + k) % HT}, device_id_type=pl.DeviceIdType.MESH)

    spread_s[...] = ((iota((96, INNER), 0) & 31) == (iota((96, INNER), 1) >> 6)).astype(F32).astype(BF16)
    spread_t[...] = ((iota((16, GL), 0) & 7) == (iota((16, GL), 1) >> 6)).astype(F32).astype(BF16)

    def place(index):
        return (index & 15) * 16 + ((index >> 4) & 7) * 2 + (index >> 7)

    order_t[...] = (place(iota((TOK, TOK), 0)) >= place(iota((TOK, TOK), 1))).astype(F32).astype(BF16)

    small[0].wait()
    loads[0].wait()

    tok = tok_v[...].astype(F32)
    normed[...] = (tok * gain[...].reshape(1, D)).astype(BF16)
    scale = lax.rsqrt(jnp.mean(tok * tok, axis=-1, keepdims=True) + EPSILON)
    scale_in[...] = scale

    loads[1].wait()
    bc = (mm(normed[...], w_bc_v[...]) * scale).astype(BF16)
    bc_s[...] = bc[:, : 2 * STATE]
    for f in range(2):
        for r in range(2):
            at = 128 * f + 64 * r
            bct_send[r, f] = bc[at : at + 64, 2 * STATE :]

    pl.semaphore_wait(barrier, TM - 1 + HT - 1)

    def bc_copy(to):
        return remote(bct_send.at[to // GROUPS], bct.at[t], b_ssem.at[0], b_rsem.at[(to + t) % 2], tm=to)

    def bc_pass(source):
        return remote(bct.at[source], bct.at[source], b_ssem.at[1], b_rsem.at[1], tm=t ^ 1)

    @pl.loop(1, 4)
    def _(k):
        bc_copy((t + 2 * k) % TM).start()

    bc_copy(t ^ 1).start()
    bct[t] = bct_send[own_row]

    def l_copy(to):
        return remote(l_send.at[to % GROUPS, to // GROUPS], ltr.at[t], l_ssem.at[0], l_rsem.at[0], tm=to)

    def chunk_of(chunk):
        return pl.ds(pl.multiple_of(chunk * CHUNK_COLS, CHUNK_COLS), CHUNK_COLS)

    def x_copy(to, chunk):
        rows = pl.ds(pl.multiple_of((to // GROUPS) * COLS + chunk * CHUNK_COLS, CHUNK_COLS), CHUNK_COLS)
        return remote(
            x_all.at[:, rows, lanes_of(to % GROUPS)], xt.at[t, :, chunk_of(chunk)],
            x_ssem.at[0], x_rsem.at[chunk], tm=to,
        )

    def owned(p):
        return p // 8, pl.ds(pl.multiple_of((p % 8) * 16, 16), 16)

    own_f, own_n = owned(h)

    def s_copy(to, half):
        f, rows = owned(to)
        lanes = pl.ds(0, HALF + 128 * (1 - half))
        return remote(
            s_send.at[half, f, rows, lanes], s_recv.at[half, h, :, lanes],
            s_ssem.at[half], s_rsem.at[half], height=to,
        )

    def x_half(half):
        lanes = pl.ds(HALF * half, HALF)
        xh = (mm(normed[...], w_in_v[:, lanes]) * scale).astype(BF16)
        x_all[0, :, lanes] = xh[:128]
        x_all[1, :, lanes] = xh[128:]

    for load in small[1:]:
        load.wait()
    loads[2].wait()
    loads[3].wait()
    loads[4].wait()
    for load in loads[5:]:
        load.start()
    logits = (mm_rows(normed[...], w_dt_v[...]) * scale).astype(BF16).astype(F32)
    dt = softplus(logits + dt_bias[...])
    rates = jnp.concatenate([rate[0:1, :], rate[1:2, :]], axis=1)
    decay = -dt * rates * LOG2E
    both = jnp.concatenate([dt, decay, jnp.zeros((TOK, 32), F32)], axis=1)
    for r in range(2):
        turned = jnp.concatenate([both[64 * r : 64 * r + 64], both[128 + 64 * r : 192 + 64 * r]], axis=0).T
        for g in range(GROUPS):
            l_send[g, r, 0:8] = turned[24 + 6 * g : 32 + 6 * g]
            l_send[g, r, 8:16] = turned[72 + 6 * g : 80 + 6 * g]

    pad = jnp.zeros((TOK, 8), F32)
    dt_s = jnp.concatenate([dt[:, :HEADS], pad], axis=1)
    decay_s = jnp.concatenate([decay[:, :HEADS], pad], axis=1)
    row, col = iota((TOK, TOK), 0), iota((TOK, TOK), 1)
    order_s = ((row >= col) & ((row >> 7) == (col >> 7))).astype(F32).astype(BF16)
    run = cumulative(order_s, decay_s)
    run_s[...] = run
    for f in range(2):
        runt_s[f] = jnp.concatenate([run[128 * f : 128 * f + 128], jnp.zeros((128, 96), F32)], axis=1).T[:32]
    ends = [run[127:128], run[255:256]]
    for f in range(2):
        total = jnp.concatenate([parts(jnp.exp2(ends[f]), 3).astype(F32), jnp.zeros((1, 32), F32)], axis=1)
        s_send[0, f, :, HALF:] = jnp.broadcast_to(total, (STATE, 128)).astype(BF16)
    end = jnp.concatenate([jnp.broadcast_to(e, (128, 32)) for e in ends], axis=0)
    to_end = parts(jnp.exp2(end - run) * dt_s, 2)
    dt_parts = parts(dt_s, 2)
    from_start = parts(jnp.exp2(run), 2)

    def state_half(half):
        for part in range(2):
            lanes = pl.ds(HALF * half + GL * part, GL)
            spread = spread_s[0:64, lanes]
            weight = mm(to_end, spread)
            for f in range(2):
                rows = slice(128 * f, 128 * f + 128)
                x = x_all[f, :, lanes].astype(F32)
                s_send[half, f, :, pl.ds(GL * part, GL)] = mm_tokens(
                    bc_s[rows, :STATE], (x * weight[rows]).astype(BF16)
                ).astype(BF16)

        @pl.loop(1, HT)
        def _(k):
            s_copy((h + k) % HT, half).start()

        lanes = pl.ds(0, HALF + 128 * (1 - half))
        s_recv[half, h, :, lanes] = s_send[half, own_f, own_n, lanes]

    x_half(0)
    x_half(1)

    def x_send(chunk):
        @pl.loop(1, TM)
        def _(k):
            x_copy((t + k) % TM, chunk).start()

    x_send(0)
    state_half(0)
    x_send(1)

    @pl.loop(1, TM)
    def _(k):
        l_copy((t + k) % TM).start()

    state_half(1)
    x_send(2)
    x_send(3)

    ltr[t] = l_send[own_group, own_row]
    own_rows = pl.ds(pl.multiple_of(own_row * COLS, COLS), COLS)
    for f in range(2):
        xt[t, f] = x_all[f, own_rows, lanes_of(own_group)]

    for part in range(4):
        lanes = pl.ds(GL * part, GL)
        steps = mm(dt_parts, spread_s[0:64, lanes])
        e_run[:, lanes] = mm(from_start, spread_s[0:64, lanes])
        for f in range(2):
            xd_s[f, :, lanes] = (x_all[f, :, lanes].astype(F32) * steps[128 * f : 128 * f + 128]).astype(BF16)

    @pl.loop(0, 4)
    def _(k):
        for step in range(2):
            @pl.when(k == 2 * step)
            def _():
                loads[5 + step].wait()
        v = mm(normed[...], w_in_v[:, pl.ds(pl.multiple_of(INNER + GL * k, 128), GL)])
        v = (v * scale_in[...]).astype(BF16).astype(F32)
        gate[:, lanes_of(k)] = v / (1.0 + jnp.exp(-v))

    received(bct.at[pl.ds(0, 3)], b_rsem.at[0])

    @pl.loop(1, 4)
    def _(k):
        source = (t + 2 * k) % TM
        bc_pass(source).start()

    half = iota((128, 128), 1) < 64
    causal = iota((128, 128), 0) >= iota((128, 128), 1)

    @pl.loop(0, 2)
    def _(f):
        rows = pl.ds(pl.multiple_of(f * 128, 128), 128)
        b, c = bc_s[rows, :STATE], bc_s[rows, STATE:]
        scores = mm_rows(c, b)
        scores = jnp.where(causal, scores, 0.0)
        run_f, runt_f = run_s[rows, :], runt_s[f]
        for pair in range(HEADS // 2):
            weights = []
            for head in (2 * pair, 2 * pair + 1):
                spread = run_f[:, head : head + 1] - runt_f[head : head + 1, :]
                weights.append((scores * jnp.exp2(jnp.minimum(spread, 0.0))).astype(BF16))
            lanes = pl.ds(128 * pair, 128)
            x = xd_s[f, :, lanes]
            none = jnp.zeros_like(x)
            both_x = jnp.concatenate([jnp.where(half, x, none), jnp.where(half, none, x)], axis=0)
            sp_out[rows, lanes] = mm(jnp.concatenate(weights, axis=1), both_x)

    def band_decays():
        row = iota((HT, 128), 0)
        totals = jnp.zeros((HT, 128), F32)
        for k in range(HT):
            totals = jnp.where(row == k, s_recv[0, k, :, HALF:].astype(F32), totals)
        totals = totals[:, :96].astype(BF16)
        for half in range(2):
            d_exp[half] = mm(totals, spread_s[:, pl.ds(HALF * half, HALF)])

    def i_copy(to, half):
        f, rows = owned(h)
        return remote(
            inc_send.at[half, to], inc_recv.at[half, f, rows], i_ssem.at[half], i_rsem.at[half], height=to
        )

    def prefix(half):
        received(s_recv.at[half, pl.ds(0, HT - 1), :, pl.ds(0, HALF + 128 * (1 - half))], s_rsem.at[half])
        if half == 0:
            band_decays()

        before = jnp.zeros((16, HALF), F32)
        for k in range(HT):
            inc_send[half, k] = before.astype(BF16)
            if k < HT - 1:
                before = before * d_exp[half, k : k + 1, :] + s_recv[half, k, :, :HALF].astype(F32)

        @pl.loop(1, HT)
        def _(k):
            i_copy((h + k) % HT, half).start()

        inc_recv[half, own_f, own_n, :] = inc_send[half, h]

    received(ltr.at[pl.ds(0, TM - 1)], l_rsem.at[0])
    received(bct.at[pl.ds(0, 4)], b_rsem.at[1])
    columns = ltr[...].reshape(TM * 16, 128).T
    for s in range(TM):
        lcol[s] = columns[:, 16 * s : 16 * s + 16]

    state[...] = jnp.zeros_like(state)

    def y_copy(to, cols, part):
        return remote(
            y_send.at[to, :, cols], y_recv.at[t, :, cols], y_ssem.at[0], y_rsem.at[part], tm=to
        )

    @pl.loop(0, CHUNKS)
    def _(chunk):
        cols = chunk_of(chunk)

        received(xt.at[pl.ds(0, TM - 1), :, cols], x_rsem.at[chunk])

        def tokens_of(f):
            return pl.ds(pl.multiple_of(f * COLS + chunk * CHUNK_COLS, CHUNK_COLS), CHUNK_COLS)

        def gathered(get, width):
            return jnp.concatenate([get(f).reshape(128, width) for f in range(2)], axis=0)

        x = gathered(lambda f: xt[:, f, cols, :], GL)
        bcv = gathered(lambda f: bct[:, f, cols, :], 2 * STATE)
        dl = gathered(lambda f: lcol[:, tokens_of(f), :], 16)
        b, c = bcv[:, :STATE], bcv[:, STATE:]
        dtv, decays = dl[:, :8], dl[:, 8:]
        runs = cumulative(order_t[...], decays)
        runs_row = jnp.concatenate([runs, jnp.zeros((TOK, 120), F32)], axis=1).T[:8]
        last = runs[TOK - 1 : TOK]
        weight = mm(parts(jnp.exp2(last - runs) * dtv, 2), spread_t[...])
        steps = mm(parts(dtv, 2), spread_t[...])
        grown = mm(parts(jnp.exp2(runs), 2), spread_t[...])
        scores = mm_rows(c, b)
        scores = scores * order_t[...].astype(F32)
        xf = x.astype(F32)
        xd = (xf * steps).astype(BF16)
        xw = (xf * weight).astype(BF16)
        earlier = mm(c, state[...].astype(BF16)) * grown
        state[...] = state[...] * grown[TOK - 1 : TOK] + mm_tokens(b, xw)
        half_x = iota((TOK, 128), 1) < 64
        for pair in range(GHEADS // 2):
            weights = []
            for head in (2 * pair, 2 * pair + 1):
                spread = runs[:, head : head + 1] - runs_row[head : head + 1, :]
                weights.append((scores * jnp.exp2(jnp.minimum(spread, 0.0))).astype(BF16))
            lanes = slice(128 * pair, 128 * pair + 128)
            xp = xd[:, lanes]
            none = jnp.zeros_like(xp)
            both_x = jnp.concatenate([jnp.where(half_x, xp, none), jnp.where(half_x, none, xp)], axis=0)
            y = mm(jnp.concatenate(weights, axis=1), both_x) + earlier[:, lanes]
            y = y.astype(BF16)
            for f in range(2):
                y_send[:, f, cols, lanes] = y[128 * f : 128 * f + 128].reshape(TM, CHUNK_COLS, 128)

        @pl.loop(1, TM)
        def _(k):
            y_copy((t + k) % TM, cols, chunk * 3 // 4).start()

        for half in range(2):
            @pl.when(chunk == half)
            def _():
                prefix(half)

    y_recv[t] = y_send[t]

    for half in range(2):
        received(inc_send.at[half, pl.ds(0, HT - 1)], i_rsem.at[half])

        for f in range(2):
            rows = slice(128 * f, 128 * f + 128)
            for part in range(2):
                lanes = pl.ds(HALF * half + GL * part, GL)
                earlier = mm(bc_s[rows, STATE:], inc_recv[half, f, :, pl.ds(GL * part, GL)])
                sp_out[rows, lanes] += e_run[rows, lanes] * earlier

    def finish(part, start, width):
        cols = pl.ds(start, width)

        received(y_recv.at[pl.ds(0, TM - 1), :, cols], y_rsem.at[part])

        scales = []
        for k in range(4):
            f, r = k // 2, k % 2
            rows = slice(k * COLS + start, k * COLS + start + width)
            squares = jnp.zeros((width, 128), F32)
            for g in range(GROUPS):
                y = y_recv[GROUPS * r + g, f, cols, :].astype(F32)
                lanes = slice(GL * g, GL * g + GL)
                gated = (sp_out[rows, lanes] + y) * gate[rows, lanes]
                normed[width * k : width * k + width, lanes] = (
                    gated * out_gain[GL * g : GL * g + GL].reshape(1, GL)
                ).astype(BF16)
                gated = gated * gated
                squares += gated[:, :128] + gated[:, 128:256] + gated[:, 256:]
            mean_square = jnp.sum(squares, axis=-1, keepdims=True) * (1.0 / INNER)
            scales.append(lax.rsqrt(mean_square + EPSILON))
        scale_v[0 : 4 * width, :] = jnp.concatenate(scales, axis=0)

        @pl.loop(0, 2)
        def _(k):
            lanes = pl.ds(pl.multiple_of(HALF * k, 128), HALF)
            mixed = mm(normed[0 : 4 * width, :], w_out_v[:, lanes]) * scale_v[0 : 4 * width, :]
            mixed = mixed.astype(BF16)
            for block in range(4):
                out[block * COLS + start : block * COLS + start + width, lanes] = (
                    mixed[width * block : width * block + width]
                )

    loads[7].wait()
    finish(0, 0, 32)
    finish(1, 32, 16)
    finish(2, 48, 16)

    sent(bct.at[pl.ds(0, 4)], b_ssem.at[0])
    sent(bct.at[pl.ds(0, 3)], b_ssem.at[1])
    sent(ltr.at[pl.ds(0, TM - 1)], l_ssem.at[0])
    sent(xt.at[pl.ds(0, TM - 1)], x_ssem.at[0])
    sent(y_send.at[pl.ds(0, TM - 1)], y_ssem.at[0])
    for half in range(2):
        sent(s_recv.at[half, pl.ds(0, HT - 1), :, pl.ds(0, HALF + 128 * (1 - half))], s_ssem.at[half])
        sent(inc_send.at[half, pl.ds(0, HT - 1)], i_ssem.at[half])


def per_device(tokens, norm_gain, in_weight, bc_weight, dt_weight, dt_bias, decay_rate, out_gain, out_weight):
    hbm = pl.BlockSpec(memory_space=pl.ANY)
    dma = pltpu.SemaphoreType.DMA
    def keep(v):
        return pltpu.with_memory_space_constraint(v, pltpu.HBM)

    mixed = pl.pallas_call(
        kernel,
        out_shape=jax.ShapeDtypeStruct((TOK, D), BF16),
        in_specs=[hbm] * 9,
        out_specs=pl.BlockSpec(memory_space=pltpu.VMEM),
        scratch_shapes=[
            pltpu.VMEM((D,), F32),
            pltpu.VMEM((1, 2 * HEADS), F32),
            pltpu.VMEM((2, HEADS), F32),
            pltpu.VMEM((INNER,), F32),
            pltpu.VMEM((TOK, D), BF16),
            pltpu.VMEM((D, 2 * INNER), BF16),
            pltpu.VMEM((D, 4 * STATE), BF16),
            pltpu.VMEM((2 * HEADS, D), BF16),
            pltpu.VMEM((INNER, D), BF16),
            pltpu.VMEM((TOK, D), BF16),
            pltpu.VMEM((2, 128, INNER), BF16),
            pltpu.VMEM((TOK, INNER), F32),
            pltpu.VMEM((TOK, 2 * STATE), BF16),
            pltpu.VMEM((2, 2, COLS, 2 * STATE), BF16),
            pltpu.VMEM((GROUPS, 2, 16, 128), F32),
            pltpu.VMEM((2, 2, STATE, HALF + 128), BF16),
            pltpu.VMEM((TM, 2, COLS, GL), BF16),
            pltpu.VMEM((TM, 2, COLS, 2 * STATE), BF16),
            pltpu.VMEM((TM, 16, 128), F32),
            pltpu.VMEM((2, HT, 16, HALF + 128), BF16),
            pltpu.VMEM((2, HT, 16, HALF), BF16),
            pltpu.VMEM((2, 2, STATE, HALF), BF16),
            pltpu.VMEM((TM, 2, COLS, GL), BF16),
            pltpu.VMEM((TM, 2, COLS, GL), BF16),
            pltpu.VMEM((2, 128, INNER), BF16),
            pltpu.VMEM((TOK, INNER), F32),
            pltpu.VMEM((TOK, INNER), F32),
            pltpu.VMEM((TOK, 32), F32),
            pltpu.VMEM((2, 32, 128), F32),
            pltpu.VMEM((96, INNER), BF16),
            pltpu.VMEM((16, GL), BF16),
            pltpu.VMEM((TOK, TOK), BF16),
            pltpu.VMEM((TM, 128, 16), F32),
            pltpu.VMEM((STATE, GL), F32),
            pltpu.VMEM((2, HT, HALF), F32),
            pltpu.VMEM((128, 1), F32),
            pltpu.VMEM((TOK, 1), F32),
            dma((8,)), dma((4,)),
            dma((1,)), dma((CHUNKS,)),
            dma((2,)), dma((2,)),
            dma((1,)), dma((1,)),
            dma((2,)), dma((2,)),
            dma((2,)), dma((2,)),
            dma((1,)), dma((3,)),
        ],
        compiler_params=pltpu.CompilerParams(
            collective_id=0, has_side_effects=True, vmem_limit_bytes=40 * 1024 * 1024
        ),
        name="layer",
    )(
        keep(tokens.reshape(TOK, D)),
        keep(norm_gain),
        keep(in_weight),
        keep(bc_weight),
        keep(dt_weight.T),
        keep(dt_bias.reshape(1, 2 * HEADS)),
        keep(decay_rate),
        keep(out_gain),
        keep(out_weight),
    )
    return mixed.reshape(tokens.shape)


def solution(mesh):
    in_specs = (P("tm", "height", None, None), P(), P(), P(), P(), P(), P(), P(), P())
    out_specs = P("tm", "height", None, None)
    return jax.shard_map(
        per_device, mesh=mesh, in_specs=in_specs, out_specs=out_specs, check_vma=False
    )
```

```python
import functools

import jax
import jax.numpy as jnp
from jax import lax
from jax.experimental import pallas as pl
from jax.experimental.pallas import tpu as pltpu
from jax.sharding import PartitionSpec as P

EPSILON = 1e-05
LOG2E = 1.4426950408889634
BF16 = jnp.bfloat16
F32 = jnp.float32

D = 1536
INNER = 1536
HEADS = 24
STATE = 128
COLS = 64
TM = 8
HT = 16
GROUPS = 4
GHEADS = HEADS // GROUPS
GL = GHEADS * 64
HALF = INNER // 2
TOK = 256
CHUNK_COLS = 16
CHUNKS = COLS // CHUNK_COLS


def mm(a, b):
    return jnp.dot(a, b, preferred_element_type=F32)


def mm_tokens(a, b):
    return lax.dot_general(a, b, (((0,), (0,)), ((), ())), preferred_element_type=F32)


def mm_rows(a, b):
    return lax.dot_general(a, b, (((1,), (1,)), ((), ())), preferred_element_type=F32)


def softplus(v):
    return jnp.maximum(v, 0.0) + jnp.log1p(jnp.exp(-jnp.abs(v)))


def parts(v, count):
    pieces, rest = [], v
    for _ in range(count):
        piece = rest.astype(BF16).astype(F32)
        pieces.append(piece)
        rest = rest - piece
    return jnp.concatenate(pieces, axis=1).astype(BF16)


def cumulative(order, v):
    width = v.shape[1]
    sums = mm(order, parts(v, 3))
    return sums[:, :width] + sums[:, width : 2 * width] + sums[:, 2 * width :]


def iota(shape, dim):
    return lax.broadcasted_iota(jnp.int32, shape, dim)


def kernel(
    tokens, gain_in, w_in, w_bc, w_dt, dt_bias_in, rate_in, out_gain_in, w_out, out,
    gain, dt_bias, rate, out_gain,
    tok_v, w_in_v, w_bc_v, w_dt_v, w_out_v,
    normed, x_all, gate, bc_s, bct_send, l_send, s_send,
    xt, bct, ltr, s_recv, inc_send, inc_recv, y_send, y_recv,
    xd_s, sp_out, e_run, run_s, runt_s, spread_s, spread_t, order_t, lcol, state, d_exp,
    scale_v, scale_in, load_sem, small_sem, x_ssem, x_rsem, b_ssem, b_rsem, l_ssem, l_rsem,
    s_ssem, s_rsem, i_ssem, i_rsem, y_ssem, y_rsem,
):
    t = lax.axis_index("tm")
    h = lax.axis_index("height")

    def remote(src, dst, ssem, rsem, **where):
        return pltpu.make_async_remote_copy(
            src_ref=src, dst_ref=dst, send_sem=ssem, recv_sem=rsem,
            device_id=where, device_id_type=pl.DeviceIdType.MESH,
        )

    def received(ref, sem):
        remote(ref, ref, sem, sem, tm=t ^ 1).wait_recv()

    def sent(ref, sem):
        remote(ref, ref, sem, sem, tm=t ^ 1).wait_send()

    own_row, own_group = t // GROUPS, t % GROUPS

    def lanes_of(index):
        return pl.ds(pl.multiple_of(index * GL, 128), GL)

    def half_lanes(start, half):
        return pl.ds(pl.multiple_of(start + half * HALF, 128), HALF)

    loads = [
        pltpu.make_async_copy(tokens, tok_v, load_sem.at[0]),
        pltpu.make_async_copy(w_bc, w_bc_v, load_sem.at[1]),
        pltpu.make_async_copy(w_dt, w_dt_v, load_sem.at[2]),
    ]
    for step in range(4):
        where = pl.ds(HALF * step, HALF)
        loads.append(pltpu.make_async_copy(w_in.at[:, where], w_in_v.at[:, where], load_sem.at[3 + step]))
    loads.append(pltpu.make_async_copy(w_out, w_out_v, load_sem.at[7]))
    small = [
        pltpu.make_async_copy(source, target, small_sem.at[k])
        for k, (source, target) in enumerate(
            ((gain_in, gain), (dt_bias_in, dt_bias), (rate_in, rate), (out_gain_in, out_gain))
        )
    ]
    small[0].start()
    for load in loads[:5]:
        load.start()
    for load in small[1:]:
        load.start()

    barrier = pltpu.get_barrier_semaphore()

    @pl.loop(1, TM)
    def _(k):
        pl.semaphore_signal(barrier, inc=1, device_id={"tm": (t + k) % TM}, device_id_type=pl.DeviceIdType.MESH)

    @pl.loop(1, HT)
    def _(k):
        pl.semaphore_signal(barrier, inc=1, device_id={"height": (h + k) % HT}, device_id_type=pl.DeviceIdType.MESH)

    spread_s[...] = ((iota((96, INNER), 0) & 31) == (iota((96, INNER), 1) >> 6)).astype(F32).astype(BF16)
    spread_t[...] = ((iota((16, GL), 0) & 7) == (iota((16, GL), 1) >> 6)).astype(F32).astype(BF16)

    def place(index):
        return (index & 15) * 16 + ((index >> 4) & 7) * 2 + (index >> 7)

    order_t[...] = (place(iota((TOK, TOK), 0)) >= place(iota((TOK, TOK), 1))).astype(F32).astype(BF16)

    small[0].wait()
    loads[0].wait()

    tok = tok_v[...].astype(F32)
    normed[...] = (tok * gain[...].reshape(1, D)).astype(BF16)
    scale = lax.rsqrt(jnp.mean(tok * tok, axis=-1, keepdims=True) + EPSILON)
    scale_in[...] = scale

    loads[1].wait()
    bc = (mm(normed[...], w_bc_v[...]) * scale).astype(BF16)
    bc_s[...] = bc[:, : 2 * STATE]
    for f in range(2):
        for r in range(2):
            at = 128 * f + 64 * r
            bct_send[r, f] = bc[at : at + 64, 2 * STATE :]

    pl.semaphore_wait(barrier, TM - 1 + HT - 1)

    def bc_copy(to):
        return remote(bct_send.at[to // GROUPS], bct.at[t], b_ssem.at[0], b_rsem.at[(to + t) % 2], tm=to)

    def bc_pass(source):
        return remote(bct.at[source], bct.at[source], b_ssem.at[1], b_rsem.at[1], tm=t ^ 1)

    @pl.loop(1, 4)
    def _(k):
        bc_copy((t + 2 * k) % TM).start()

    bc_copy(t ^ 1).start()
    bct[t] = bct_send[own_row]

    def l_copy(to):
        return remote(l_send.at[to % GROUPS, to // GROUPS], ltr.at[t], l_ssem.at[0], l_rsem.at[0], tm=to)

    def chunk_of(chunk):
        return pl.ds(pl.multiple_of(chunk * CHUNK_COLS, CHUNK_COLS), CHUNK_COLS)

    def x_copy(to, chunk):
        rows = pl.ds(pl.multiple_of((to // GROUPS) * COLS + chunk * CHUNK_COLS, CHUNK_COLS), CHUNK_COLS)
        return remote(
            x_all.at[:, rows, lanes_of(to % GROUPS)], xt.at[t, :, chunk_of(chunk)],
            x_ssem.at[0], x_rsem.at[chunk], tm=to,
        )

    def owned(p):
        return p // 8, pl.ds(pl.multiple_of((p % 8) * 16, 16), 16)

    own_f, own_n = owned(h)

    def s_copy(to, half):
        f, rows = owned(to)
        lanes = pl.ds(0, HALF + 128 * (1 - half))
        return remote(
            s_send.at[half, f, rows, lanes], s_recv.at[half, h, :, lanes],
            s_ssem.at[half], s_rsem.at[half], height=to,
        )

    def x_half(half):
        lanes = pl.ds(HALF * half, HALF)
        xh = (mm(normed[...], w_in_v[:, lanes]) * scale).astype(BF16)
        x_all[0, :, lanes] = xh[:128]
        x_all[1, :, lanes] = xh[128:]

    for load in small[1:]:
        load.wait()
    loads[2].wait()
    loads[3].wait()
    loads[4].wait()
    for load in loads[5:]:
        load.start()
    logits = (mm_rows(normed[...], w_dt_v[...]) * scale).astype(BF16).astype(F32)
    dt = softplus(logits + dt_bias[...])
    rates = jnp.concatenate([rate[0:1, :], rate[1:2, :]], axis=1)
    decay = -dt * rates * LOG2E
    both = jnp.concatenate([dt, decay, jnp.zeros((TOK, 32), F32)], axis=1)
    for r in range(2):
        turned = jnp.concatenate([both[64 * r : 64 * r + 64], both[128 + 64 * r : 192 + 64 * r]], axis=0).T
        for g in range(GROUPS):
            l_send[g, r, 0:8] = turned[24 + 6 * g : 32 + 6 * g]
            l_send[g, r, 8:16] = turned[72 + 6 * g : 80 + 6 * g]

    pad = jnp.zeros((TOK, 8), F32)
    dt_s = jnp.concatenate([dt[:, :HEADS], pad], axis=1)
    decay_s = jnp.concatenate([decay[:, :HEADS], pad], axis=1)
    row, col = iota((TOK, TOK), 0), iota((TOK, TOK), 1)
    order_s = ((row >= col) & ((row >> 7) == (col >> 7))).astype(F32).astype(BF16)
    run = cumulative(order_s, decay_s)
    run_s[...] = run
    for f in range(2):
        runt_s[f] = jnp.concatenate([run[128 * f : 128 * f + 128], jnp.zeros((128, 96), F32)], axis=1).T[:32]
    ends = [run[127:128], run[255:256]]
    for f in range(2):
        total = jnp.concatenate([parts(jnp.exp2(ends[f]), 3).astype(F32), jnp.zeros((1, 32), F32)], axis=1)
        s_send[0, f, :, HALF:] = jnp.broadcast_to(total, (STATE, 128)).astype(BF16)
    end = jnp.concatenate([jnp.broadcast_to(e, (128, 32)) for e in ends], axis=0)
    to_end = parts(jnp.exp2(end - run) * dt_s, 2)
    dt_parts = parts(dt_s, 2)
    from_start = parts(jnp.exp2(run), 2)

    def state_half(half):
        for part in range(2):
            lanes = pl.ds(HALF * half + GL * part, GL)
            spread = spread_s[0:64, lanes]
            weight = mm(to_end, spread)
            for f in range(2):
                rows = slice(128 * f, 128 * f + 128)
                x = x_all[f, :, lanes].astype(F32)
                s_send[half, f, :, pl.ds(GL * part, GL)] = mm_tokens(
                    bc_s[rows, :STATE], (x * weight[rows]).astype(BF16)
                ).astype(BF16)

        @pl.loop(1, HT)
        def _(k):
            s_copy((h + k) % HT, half).start()

        lanes = pl.ds(0, HALF + 128 * (1 - half))
        s_recv[half, h, :, lanes] = s_send[half, own_f, own_n, lanes]

    x_half(0)
    x_half(1)

    def x_send(chunk):
        @pl.loop(1, TM)
        def _(k):
            x_copy((t + 3 * k) % TM, chunk).start()

    x_send(0)
    state_half(0)
    state_half(1)

    @pl.loop(1, TM)
    def _(k):
        l_copy((t + k) % TM).start()

    x_send(1)
    x_send(2)
    x_send(3)

    ltr[t] = l_send[own_group, own_row]
    own_rows = pl.ds(pl.multiple_of(own_row * COLS, COLS), COLS)
    for f in range(2):
        xt[t, f] = x_all[f, own_rows, lanes_of(own_group)]

    for part in range(4):
        lanes = pl.ds(GL * part, GL)
        steps = mm(dt_parts, spread_s[0:64, lanes])
        e_run[:, lanes] = mm(from_start, spread_s[0:64, lanes])
        for f in range(2):
            xd_s[f, :, lanes] = (x_all[f, :, lanes].astype(F32) * steps[128 * f : 128 * f + 128]).astype(BF16)

    @pl.loop(0, 4)
    def _(k):
        for step in range(2):
            @pl.when(k == 2 * step)
            def _():
                loads[5 + step].wait()
        v = mm(normed[...], w_in_v[:, pl.ds(pl.multiple_of(INNER + GL * k, 128), GL)])
        v = (v * scale_in[...]).astype(BF16).astype(F32)
        gate[:, lanes_of(k)] = v / (1.0 + jnp.exp(-v))

    received(bct.at[pl.ds(0, 3)], b_rsem.at[0])

    @pl.loop(1, 4)
    def _(k):
        source = (t + 2 * k) % TM
        bc_pass(source).start()

    half = iota((128, 128), 1) < 64
    causal = iota((128, 128), 0) >= iota((128, 128), 1)

    @pl.loop(0, 2)
    def _(f):
        rows = pl.ds(pl.multiple_of(f * 128, 128), 128)
        b, c = bc_s[rows, :STATE], bc_s[rows, STATE:]
        scores = mm_rows(c, b)
        scores = jnp.where(causal, scores, 0.0)
        run_f, runt_f = run_s[rows, :], runt_s[f]
        for pair in range(HEADS // 2):
            weights = []
            for head in (2 * pair, 2 * pair + 1):
                spread = run_f[:, head : head + 1] - runt_f[head : head + 1, :]
                weights.append((scores * jnp.exp2(jnp.minimum(spread, 0.0))).astype(BF16))
            lanes = pl.ds(128 * pair, 128)
            x = xd_s[f, :, lanes]
            none = jnp.zeros_like(x)
            both_x = jnp.concatenate([jnp.where(half, x, none), jnp.where(half, none, x)], axis=0)
            sp_out[rows, lanes] = mm(jnp.concatenate(weights, axis=1), both_x)

    def band_decays():
        row = iota((HT, 128), 0)
        totals = jnp.zeros((HT, 128), F32)
        for k in range(HT):
            totals = jnp.where(row == k, s_recv[0, k, :, HALF:].astype(F32), totals)
        totals = totals[:, :96].astype(BF16)
        for half in range(2):
            d_exp[half] = mm(totals, spread_s[:, pl.ds(HALF * half, HALF)])

    def i_copy(to, half):
        f, rows = owned(h)
        return remote(
            inc_send.at[half, to], inc_recv.at[half, f, rows], i_ssem.at[half], i_rsem.at[half], height=to
        )

    def prefix(half):
        received(s_recv.at[half, pl.ds(0, HT - 1), :, pl.ds(0, HALF + 128 * (1 - half))], s_rsem.at[half])
        if half == 0:
            band_decays()

        before = jnp.zeros((16, HALF), F32)
        for k in range(HT):
            inc_send[half, k] = before.astype(BF16)
            if k < HT - 1:
                before = before * d_exp[half, k : k + 1, :] + s_recv[half, k, :, :HALF].astype(F32)

        @pl.loop(1, HT)
        def _(k):
            i_copy((h + k) % HT, half).start()

        inc_recv[half, own_f, own_n, :] = inc_send[half, h]

    received(ltr.at[pl.ds(0, TM - 1)], l_rsem.at[0])
    received(bct.at[pl.ds(0, 4)], b_rsem.at[1])
    columns = ltr[...].reshape(TM * 16, 128).T
    for s in range(TM):
        lcol[s] = columns[:, 16 * s : 16 * s + 16]

    state[...] = jnp.zeros_like(state)

    def y_copy(to, cols, part):
        return remote(
            y_send.at[to, :, cols], y_recv.at[t, :, cols], y_ssem.at[0], y_rsem.at[part], tm=to
        )

    @pl.loop(0, CHUNKS)
    def _(chunk):
        cols = chunk_of(chunk)

        received(xt.at[pl.ds(0, TM - 1), :, cols], x_rsem.at[chunk])

        def tokens_of(f):
            return pl.ds(pl.multiple_of(f * COLS + chunk * CHUNK_COLS, CHUNK_COLS), CHUNK_COLS)

        def gathered(get, width):
            return jnp.concatenate([get(f).reshape(128, width) for f in range(2)], axis=0)

        x = gathered(lambda f: xt[:, f, cols, :], GL)
        bcv = gathered(lambda f: bct[:, f, cols, :], 2 * STATE)
        dl = gathered(lambda f: lcol[:, tokens_of(f), :], 16)
        b, c = bcv[:, :STATE], bcv[:, STATE:]
        dtv, decays = dl[:, :8], dl[:, 8:]
        runs = cumulative(order_t[...], decays)
        runs_row = jnp.concatenate([runs, jnp.zeros((TOK, 120), F32)], axis=1).T[:8]
        last = runs[TOK - 1 : TOK]
        weight = mm(parts(jnp.exp2(last - runs) * dtv, 2), spread_t[...])
        steps = mm(parts(dtv, 2), spread_t[...])
        grown = mm(parts(jnp.exp2(runs), 2), spread_t[...])
        scores = mm_rows(c, b)
        scores = scores * order_t[...].astype(F32)
        xf = x.astype(F32)
        xd = (xf * steps).astype(BF16)
        xw = (xf * weight).astype(BF16)
        earlier = mm(c, state[...].astype(BF16)) * grown
        state[...] = state[...] * grown[TOK - 1 : TOK] + mm_tokens(b, xw)
        half_x = iota((TOK, 128), 1) < 64
        for pair in range(GHEADS // 2):
            weights = []
            for head in (2 * pair, 2 * pair + 1):
                spread = runs[:, head : head + 1] - runs_row[head : head + 1, :]
                weights.append((scores * jnp.exp2(jnp.minimum(spread, 0.0))).astype(BF16))
            lanes = slice(128 * pair, 128 * pair + 128)
            xp = xd[:, lanes]
            none = jnp.zeros_like(xp)
            both_x = jnp.concatenate([jnp.where(half_x, xp, none), jnp.where(half_x, none, xp)], axis=0)
            y = mm(jnp.concatenate(weights, axis=1), both_x) + earlier[:, lanes]
            y = y.astype(BF16)
            for f in range(2):
                y_send[:, f, cols, lanes] = y[128 * f : 128 * f + 128].reshape(TM, CHUNK_COLS, 128)

        @pl.loop(1, TM)
        def _(k):
            y_copy((t + 3 * k) % TM, cols, chunk * 3 // 4).start()

        for half in range(2):
            @pl.when(chunk == 2 * half)
            def _():
                prefix(half)

    y_recv[t] = y_send[t]

    for half in range(2):
        received(inc_send.at[half, pl.ds(0, HT - 1)], i_rsem.at[half])

        for f in range(2):
            rows = slice(128 * f, 128 * f + 128)
            for part in range(2):
                lanes = pl.ds(HALF * half + GL * part, GL)
                earlier = mm(bc_s[rows, STATE:], inc_recv[half, f, :, pl.ds(GL * part, GL)])
                sp_out[rows, lanes] += e_run[rows, lanes] * earlier

    def finish(part, start, width):
        cols = pl.ds(start, width)

        received(y_recv.at[pl.ds(0, TM - 1), :, cols], y_rsem.at[part])

        scales = []
        for k in range(4):
            f, r = k // 2, k % 2
            rows = slice(k * COLS + start, k * COLS + start + width)
            squares = jnp.zeros((width, 128), F32)
            for g in range(GROUPS):
                y = y_recv[GROUPS * r + g, f, cols, :].astype(F32)
                lanes = slice(GL * g, GL * g + GL)
                gated = (sp_out[rows, lanes] + y) * gate[rows, lanes]
                normed[width * k : width * k + width, lanes] = (
                    gated * out_gain[GL * g : GL * g + GL].reshape(1, GL)
                ).astype(BF16)
                gated = gated * gated
                squares += gated[:, :128] + gated[:, 128:256] + gated[:, 256:]
            mean_square = jnp.sum(squares, axis=-1, keepdims=True) * (1.0 / INNER)
            scales.append(lax.rsqrt(mean_square + EPSILON))
        scale_v[0 : 4 * width, :] = jnp.concatenate(scales, axis=0)

        @pl.loop(0, 2)
        def _(k):
            lanes = pl.ds(pl.multiple_of(HALF * k, 128), HALF)
            mixed = mm(normed[0 : 4 * width, :], w_out_v[:, lanes]) * scale_v[0 : 4 * width, :]
            mixed = mixed.astype(BF16)
            for block in range(4):
                out[block * COLS + start : block * COLS + start + width, lanes] = (
                    mixed[width * block : width * block + width]
                )

    loads[7].wait()
    finish(0, 0, 32)
    finish(1, 32, 16)
    finish(2, 48, 16)

    sent(bct.at[pl.ds(0, 4)], b_ssem.at[0])
    sent(bct.at[pl.ds(0, 3)], b_ssem.at[1])
    sent(ltr.at[pl.ds(0, TM - 1)], l_ssem.at[0])
    sent(xt.at[pl.ds(0, TM - 1)], x_ssem.at[0])
    sent(y_send.at[pl.ds(0, TM - 1)], y_ssem.at[0])
    for half in range(2):
        sent(s_recv.at[half, pl.ds(0, HT - 1), :, pl.ds(0, HALF + 128 * (1 - half))], s_ssem.at[half])
        sent(inc_send.at[half, pl.ds(0, HT - 1)], i_ssem.at[half])


def per_device(tokens, norm_gain, in_weight, bc_weight, dt_weight, dt_bias, decay_rate, out_gain, out_weight):
    hbm = pl.BlockSpec(memory_space=pl.ANY)
    dma = pltpu.SemaphoreType.DMA
    def keep(v):
        return pltpu.with_memory_space_constraint(v, pltpu.HBM)

    mixed = pl.pallas_call(
        kernel,
        out_shape=jax.ShapeDtypeStruct((TOK, D), BF16),
        in_specs=[hbm] * 9,
        out_specs=pl.BlockSpec(memory_space=pltpu.VMEM),
        scratch_shapes=[
            pltpu.VMEM((D,), F32),
            pltpu.VMEM((1, 2 * HEADS), F32),
            pltpu.VMEM((2, HEADS), F32),
            pltpu.VMEM((INNER,), F32),
            pltpu.VMEM((TOK, D), BF16),
            pltpu.VMEM((D, 2 * INNER), BF16),
            pltpu.VMEM((D, 4 * STATE), BF16),
            pltpu.VMEM((2 * HEADS, D), BF16),
            pltpu.VMEM((INNER, D), BF16),
            pltpu.VMEM((TOK, D), BF16),
            pltpu.VMEM((2, 128, INNER), BF16),
            pltpu.VMEM((TOK, INNER), F32),
            pltpu.VMEM((TOK, 2 * STATE), BF16),
            pltpu.VMEM((2, 2, COLS, 2 * STATE), BF16),
            pltpu.VMEM((GROUPS, 2, 16, 128), F32),
            pltpu.VMEM((2, 2, STATE, HALF + 128), BF16),
            pltpu.VMEM((TM, 2, COLS, GL), BF16),
            pltpu.VMEM((TM, 2, COLS, 2 * STATE), BF16),
            pltpu.VMEM((TM, 16, 128), F32),
            pltpu.VMEM((2, HT, 16, HALF + 128), BF16),
            pltpu.VMEM((2, HT, 16, HALF), BF16),
            pltpu.VMEM((2, 2, STATE, HALF), BF16),
            pltpu.VMEM((TM, 2, COLS, GL), BF16),
            pltpu.VMEM((TM, 2, COLS, GL), BF16),
            pltpu.VMEM((2, 128, INNER), BF16),
            pltpu.VMEM((TOK, INNER), F32),
            pltpu.VMEM((TOK, INNER), F32),
            pltpu.VMEM((TOK, 32), F32),
            pltpu.VMEM((2, 32, 128), F32),
            pltpu.VMEM((96, INNER), BF16),
            pltpu.VMEM((16, GL), BF16),
            pltpu.VMEM((TOK, TOK), BF16),
            pltpu.VMEM((TM, 128, 16), F32),
            pltpu.VMEM((STATE, GL), F32),
            pltpu.VMEM((2, HT, HALF), F32),
            pltpu.VMEM((128, 1), F32),
            pltpu.VMEM((TOK, 1), F32),
            dma((8,)), dma((4,)),
            dma((1,)), dma((CHUNKS,)),
            dma((2,)), dma((2,)),
            dma((1,)), dma((1,)),
            dma((2,)), dma((2,)),
            dma((2,)), dma((2,)),
            dma((1,)), dma((3,)),
        ],
        compiler_params=pltpu.CompilerParams(
            collective_id=0, has_side_effects=True, vmem_limit_bytes=40 * 1024 * 1024
        ),
        name="layer",
    )(
        keep(tokens.reshape(TOK, D)),
        keep(norm_gain),
        keep(in_weight),
        keep(bc_weight),
        keep(dt_weight.T),
        keep(dt_bias.reshape(1, 2 * HEADS)),
        keep(decay_rate),
        keep(out_gain),
        keep(out_weight),
    )
    return mixed.reshape(tokens.shape)


def solution(mesh):
    in_specs = (P("tm", "height", None, None), P(), P(), P(), P(), P(), P(), P(), P())
    out_specs = P("tm", "height", None, None)
    return jax.shard_map(
        per_device, mesh=mesh, in_specs=in_specs, out_specs=out_specs, check_vma=False
    )
```

```python
import functools

import jax
import jax.numpy as jnp
from jax import lax
from jax.experimental import pallas as pl
from jax.experimental.pallas import tpu as pltpu
from jax.sharding import PartitionSpec as P

EPSILON = 1e-05
LOG2E = 1.4426950408889634
BF16 = jnp.bfloat16
F32 = jnp.float32

D = 1536
INNER = 1536
HEADS = 24
STATE = 128
COLS = 64
TM = 8
HT = 16
GROUPS = 4
GHEADS = HEADS // GROUPS
GL = GHEADS * 64
HALF = INNER // 2
TOK = 256
CHUNK_COLS = 16
CHUNKS = COLS // CHUNK_COLS


def mm(a, b):
    return jnp.dot(a, b, preferred_element_type=F32)


def mm_tokens(a, b):
    return lax.dot_general(a, b, (((0,), (0,)), ((), ())), preferred_element_type=F32)


def mm_rows(a, b):
    return lax.dot_general(a, b, (((1,), (1,)), ((), ())), preferred_element_type=F32)


def softplus(v):
    return jnp.maximum(v, 0.0) + jnp.log1p(jnp.exp(-jnp.abs(v)))


def parts(v, count):
    pieces, rest = [], v
    for _ in range(count):
        piece = rest.astype(BF16).astype(F32)
        pieces.append(piece)
        rest = rest - piece
    return jnp.concatenate(pieces, axis=1).astype(BF16)


def cumulative(order, v):
    width = v.shape[1]
    sums = mm(order, parts(v, 3))
    return sums[:, :width] + sums[:, width : 2 * width] + sums[:, 2 * width :]


def iota(shape, dim):
    return lax.broadcasted_iota(jnp.int32, shape, dim)


def kernel(
    tokens, gain_in, w_in, w_bc, w_dt, dt_bias_in, rate_in, out_gain_in, w_out, out,
    gain, dt_bias, rate, out_gain,
    tok_v, w_in_v, w_bc_v, w_dt_v, w_out_v,
    normed, x_all, gate, bc_s, bct_send, l_send, d_send, s_send,
    xt, bct, ltr, d_recv, s_recv, inc_send, inc_recv, y_send, y_recv,
    xd_s, sp_out, e_run, run_s, runt_s, spread_s, spread_t, order_t, lcol, state, d_exp,
    scale_v, scale_in, load_sem, small_sem, x_ssem, x_rsem, b_ssem, b_rsem, l_ssem, l_rsem, d_ssem, d_rsem,
    s_ssem, s_rsem, i_ssem, i_rsem, y_ssem, y_rsem,
):
    t = lax.axis_index("tm")
    h = lax.axis_index("height")

    def remote(src, dst, ssem, rsem, **where):
        return pltpu.make_async_remote_copy(
            src_ref=src, dst_ref=dst, send_sem=ssem, recv_sem=rsem,
            device_id=where, device_id_type=pl.DeviceIdType.MESH,
        )

    def received(ref, sem):
        remote(ref, ref, sem, sem, tm=t ^ 1).wait_recv()

    def sent(ref, sem):
        remote(ref, ref, sem, sem, tm=t ^ 1).wait_send()

    own_row, own_group = t // GROUPS, t % GROUPS

    def lanes_of(index):
        return pl.ds(pl.multiple_of(index * GL, 128), GL)

    def half_lanes(start, half):
        return pl.ds(pl.multiple_of(start + half * HALF, 128), HALF)

    loads = [
        pltpu.make_async_copy(tokens, tok_v, load_sem.at[0]),
        pltpu.make_async_copy(w_bc, w_bc_v, load_sem.at[1]),
        pltpu.make_async_copy(w_dt, w_dt_v, load_sem.at[2]),
    ]
    for step in range(4):
        where = pl.ds(HALF * step, HALF)
        loads.append(pltpu.make_async_copy(w_in.at[:, where], w_in_v.at[:, where], load_sem.at[3 + step]))
    loads.append(pltpu.make_async_copy(w_out, w_out_v, load_sem.at[7]))
    small = [
        pltpu.make_async_copy(source, target, small_sem.at[k])
        for k, (source, target) in enumerate(
            ((gain_in, gain), (dt_bias_in, dt_bias), (rate_in, rate), (out_gain_in, out_gain))
        )
    ]
    small[0].start()
    for load in loads[:5]:
        load.start()
    for load in small[1:]:
        load.start()

    barrier = pltpu.get_barrier_semaphore()

    @pl.loop(1, TM)
    def _(k):
        pl.semaphore_signal(barrier, inc=1, device_id={"tm": (t + k) % TM}, device_id_type=pl.DeviceIdType.MESH)

    @pl.loop(1, HT)
    def _(k):
        pl.semaphore_signal(barrier, inc=1, device_id={"height": (h + k) % HT}, device_id_type=pl.DeviceIdType.MESH)

    spread_s[...] = ((iota((96, INNER), 0) & 31) == (iota((96, INNER), 1) >> 6)).astype(F32).astype(BF16)
    spread_t[...] = ((iota((16, GL), 0) & 7) == (iota((16, GL), 1) >> 6)).astype(F32).astype(BF16)

    def place(index):
        return (index & 15) * 16 + ((index >> 4) & 7) * 2 + (index >> 7)

    order_t[...] = (place(iota((TOK, TOK), 0)) >= place(iota((TOK, TOK), 1))).astype(F32).astype(BF16)

    small[0].wait()
    loads[0].wait()

    tok = tok_v[...].astype(F32)
    normed[...] = (tok * gain[...].reshape(1, D)).astype(BF16)
    scale = lax.rsqrt(jnp.mean(tok * tok, axis=-1, keepdims=True) + EPSILON)
    scale_in[...] = scale

    loads[1].wait()
    bc = (mm(normed[...], w_bc_v[...]) * scale).astype(BF16)
    bc_s[...] = bc[:, : 2 * STATE]
    for f in range(2):
        for r in range(2):
            at = 128 * f + 64 * r
            bct_send[r, f] = bc[at : at + 64, 2 * STATE :]

    pl.semaphore_wait(barrier, TM - 1 + HT - 1)

    def bc_copy(to):
        return remote(bct_send.at[to // GROUPS], bct.at[t], b_ssem.at[0], b_rsem.at[(to + t) % 2], tm=to)

    def bc_pass(source):
        return remote(bct.at[source], bct.at[source], b_ssem.at[1], b_rsem.at[1], tm=t ^ 1)

    @pl.loop(1, 4)
    def _(k):
        bc_copy((t + 2 * k) % TM).start()

    bc_copy(t ^ 1).start()
    bct[t] = bct_send[own_row]

    def l_copy(to):
        return remote(l_send.at[to % GROUPS, to // GROUPS], ltr.at[t], l_ssem.at[0], l_rsem.at[0], tm=to)

    def chunk_of(chunk):
        return pl.ds(pl.multiple_of(chunk * CHUNK_COLS, CHUNK_COLS), CHUNK_COLS)

    def x_copy(to, chunk):
        rows = pl.ds(pl.multiple_of((to // GROUPS) * COLS + chunk * CHUNK_COLS, CHUNK_COLS), CHUNK_COLS)
        return remote(
            x_all.at[:, rows, lanes_of(to % GROUPS)], xt.at[t, :, chunk_of(chunk)],
            x_ssem.at[0], x_rsem.at[chunk], tm=to,
        )

    def owned(p):
        return p // 8, pl.ds(pl.multiple_of((p % 8) * 16, 16), 16)

    own_f, own_n = owned(h)

    def s_copy(to, half):
        f, rows = owned(to)
        return remote(
            s_send.at[half, f, rows], s_recv.at[half, h], s_ssem.at[half], s_rsem.at[half], height=to
        )

    def d_copy(to):
        return remote(d_send.at[to // 8], d_recv.at[h], d_ssem.at[0], d_rsem.at[0], height=to)

    def x_half(half):
        lanes = pl.ds(HALF * half, HALF)
        xh = (mm(normed[...], w_in_v[:, lanes]) * scale).astype(BF16)
        x_all[0, :, lanes] = xh[:128]
        x_all[1, :, lanes] = xh[128:]

    for load in small[1:]:
        load.wait()
    loads[2].wait()
    loads[3].wait()
    logits = (mm_rows(normed[...], w_dt_v[...]) * scale).astype(BF16).astype(F32)
    dt = softplus(logits + dt_bias[...])
    rates = jnp.concatenate([rate[0:1, :], rate[1:2, :]], axis=1)
    decay = -dt * rates * LOG2E
    both = jnp.concatenate([dt, decay, jnp.zeros((TOK, 32), F32)], axis=1)
    for r in range(2):
        turned = jnp.concatenate([both[64 * r : 64 * r + 64], both[128 + 64 * r : 192 + 64 * r]], axis=0).T
        for g in range(GROUPS):
            l_send[g, r, 0:8] = turned[24 + 6 * g : 32 + 6 * g]
            l_send[g, r, 8:16] = turned[72 + 6 * g : 80 + 6 * g]

    pad = jnp.zeros((TOK, 8), F32)
    dt_s = jnp.concatenate([dt[:, :HEADS], pad], axis=1)
    decay_s = jnp.concatenate([decay[:, :HEADS], pad], axis=1)
    row, col = iota((TOK, TOK), 0), iota((TOK, TOK), 1)
    order_s = ((row >= col) & ((row >> 7) == (col >> 7))).astype(F32).astype(BF16)
    run = cumulative(order_s, decay_s)
    run_s[...] = run
    for f in range(2):
        runt_s[f] = jnp.concatenate([run[128 * f : 128 * f + 128], jnp.zeros((128, 96), F32)], axis=1).T[:32]
    ends = [run[127:128], run[255:256]]
    for f in range(2):
        d_send[f] = jnp.concatenate([jnp.exp2(ends[f]), jnp.zeros((1, 96), F32)], axis=1)
    end = jnp.concatenate([jnp.broadcast_to(e, (128, 32)) for e in ends], axis=0)
    to_end = parts(jnp.exp2(end - run) * dt_s, 2)
    dt_parts = parts(dt_s, 2)
    from_start = parts(jnp.exp2(run), 2)

    def state_half(half):
        for part in range(2):
            lanes = pl.ds(HALF * half + GL * part, GL)
            spread = spread_s[0:64, lanes]
            weight = mm(to_end, spread)
            for f in range(2):
                rows = slice(128 * f, 128 * f + 128)
                x = x_all[f, :, lanes].astype(F32)
                s_send[half, f, :, pl.ds(GL * part, GL)] = mm_tokens(
                    bc_s[rows, :STATE], (x * weight[rows]).astype(BF16)
                ).astype(BF16)

        @pl.loop(1, HT)
        def _(k):
            s_copy((h + k) % HT, half).start()

        s_recv[half, h] = s_send[half, own_f, own_n]

    x_half(0)
    state_half(0)
    loads[4].wait()
    for load in loads[5:]:
        load.start()
    x_half(1)

    def x_send(chunk):
        @pl.loop(1, TM)
        def _(k):
            x_copy((t + 3 * k) % TM, chunk).start()

    x_send(0)

    @pl.loop(1, HT)
    def _(k):
        d_copy((h + k) % HT).start()

    d_recv[h] = d_send[h // 8]
    state_half(1)

    @pl.loop(1, TM)
    def _(k):
        l_copy((t + k) % TM).start()

    x_send(1)
    x_send(2)
    x_send(3)

    ltr[t] = l_send[own_group, own_row]
    own_rows = pl.ds(pl.multiple_of(own_row * COLS, COLS), COLS)
    for f in range(2):
        xt[t, f] = x_all[f, own_rows, lanes_of(own_group)]

    for part in range(4):
        lanes = pl.ds(GL * part, GL)
        steps = mm(dt_parts, spread_s[0:64, lanes])
        e_run[:, lanes] = mm(from_start, spread_s[0:64, lanes])
        for f in range(2):
            xd_s[f, :, lanes] = (x_all[f, :, lanes].astype(F32) * steps[128 * f : 128 * f + 128]).astype(BF16)

    @pl.loop(0, 4)
    def _(k):
        for step in range(2):
            @pl.when(k == 2 * step)
            def _():
                loads[5 + step].wait()
        v = mm(normed[...], w_in_v[:, pl.ds(pl.multiple_of(INNER + GL * k, 128), GL)])
        v = (v * scale_in[...]).astype(BF16).astype(F32)
        gate[:, lanes_of(k)] = v / (1.0 + jnp.exp(-v))

    received(bct.at[pl.ds(0, 3)], b_rsem.at[0])

    @pl.loop(1, 4)
    def _(k):
        source = (t + 2 * k) % TM
        bc_pass(source).start()

    half = iota((128, 128), 1) < 64
    causal = iota((128, 128), 0) >= iota((128, 128), 1)

    @pl.loop(0, 2)
    def _(f):
        rows = pl.ds(pl.multiple_of(f * 128, 128), 128)
        b, c = bc_s[rows, :STATE], bc_s[rows, STATE:]
        scores = mm_rows(c, b)
        scores = jnp.where(causal, scores, 0.0)
        run_f, runt_f = run_s[rows, :], runt_s[f]
        for pair in range(HEADS // 2):
            weights = []
            for head in (2 * pair, 2 * pair + 1):
                spread = run_f[:, head : head + 1] - runt_f[head : head + 1, :]
                weights.append((scores * jnp.exp2(jnp.minimum(spread, 0.0))).astype(BF16))
            lanes = pl.ds(128 * pair, 128)
            x = xd_s[f, :, lanes]
            none = jnp.zeros_like(x)
            both_x = jnp.concatenate([jnp.where(half, x, none), jnp.where(half, none, x)], axis=0)
            sp_out[rows, lanes] = mm(jnp.concatenate(weights, axis=1), both_x)

    def band_decays():
        received(d_recv.at[pl.ds(0, HT - 1)], d_rsem.at[0])
        totals = parts(jnp.concatenate([d_recv[k] for k in range(HT)], axis=0)[:, :32], 3)
        for half in range(2):
            d_exp[half] = mm(totals, spread_s[:, pl.ds(HALF * half, HALF)])

    def i_copy(to, half):
        f, rows = owned(h)
        return remote(
            inc_send.at[half, to], inc_recv.at[half, f, rows], i_ssem.at[half], i_rsem.at[half], height=to
        )

    def prefix(half):
        received(s_recv.at[half, pl.ds(0, HT - 1)], s_rsem.at[half])
        if half == 0:
            band_decays()

        before = jnp.zeros((16, HALF), F32)
        for k in range(HT):
            inc_send[half, k] = before.astype(BF16)
            if k < HT - 1:
                before = before * d_exp[half, k : k + 1, :] + s_recv[half, k].astype(F32)

        @pl.loop(1, HT)
        def _(k):
            i_copy((h + k) % HT, half).start()

        inc_recv[half, own_f, own_n, :] = inc_send[half, h]

    received(ltr.at[pl.ds(0, TM - 1)], l_rsem.at[0])
    received(bct.at[pl.ds(0, 4)], b_rsem.at[1])
    columns = ltr[...].reshape(TM * 16, 128).T
    for s in range(TM):
        lcol[s] = columns[:, 16 * s : 16 * s + 16]

    state[...] = jnp.zeros_like(state)

    def y_copy(to, cols, part):
        return remote(
            y_send.at[to, :, cols], y_recv.at[t, :, cols], y_ssem.at[0], y_rsem.at[part], tm=to
        )

    @pl.loop(0, CHUNKS)
    def _(chunk):
        cols = chunk_of(chunk)

        received(xt.at[pl.ds(0, TM - 1), :, cols], x_rsem.at[chunk])

        def tokens_of(f):
            return pl.ds(pl.multiple_of(f * COLS + chunk * CHUNK_COLS, CHUNK_COLS), CHUNK_COLS)

        def gathered(get, width):
            return jnp.concatenate([get(f).reshape(128, width) for f in range(2)], axis=0)

        x = gathered(lambda f: xt[:, f, cols, :], GL)
        bcv = gathered(lambda f: bct[:, f, cols, :], 2 * STATE)
        dl = gathered(lambda f: lcol[:, tokens_of(f), :], 16)
        b, c = bcv[:, :STATE], bcv[:, STATE:]
        dtv, decays = dl[:, :8], dl[:, 8:]
        runs = cumulative(order_t[...], decays)
        runs_row = jnp.concatenate([runs, jnp.zeros((TOK, 120), F32)], axis=1).T[:8]
        last = runs[TOK - 1 : TOK]
        weight = mm(parts(jnp.exp2(last - runs) * dtv, 2), spread_t[...])
        steps = mm(parts(dtv, 2), spread_t[...])
        grown = mm(parts(jnp.exp2(runs), 2), spread_t[...])
        scores = mm_rows(c, b)
        scores = scores * order_t[...].astype(F32)
        xf = x.astype(F32)
        xd = (xf * steps).astype(BF16)
        xw = (xf * weight).astype(BF16)
        earlier = mm(c, state[...].astype(BF16)) * grown
        state[...] = state[...] * grown[TOK - 1 : TOK] + mm_tokens(b, xw)
        half_x = iota((TOK, 128), 1) < 64
        for pair in range(GHEADS // 2):
            weights = []
            for head in (2 * pair, 2 * pair + 1):
                spread = runs[:, head : head + 1] - runs_row[head : head + 1, :]
                weights.append((scores * jnp.exp2(jnp.minimum(spread, 0.0))).astype(BF16))
            lanes = slice(128 * pair, 128 * pair + 128)
            xp = xd[:, lanes]
            none = jnp.zeros_like(xp)
            both_x = jnp.concatenate([jnp.where(half_x, xp, none), jnp.where(half_x, none, xp)], axis=0)
            y = mm(jnp.concatenate(weights, axis=1), both_x) + earlier[:, lanes]
            y = y.astype(BF16)
            for f in range(2):
                y_send[:, f, cols, lanes] = y[128 * f : 128 * f + 128].reshape(TM, CHUNK_COLS, 128)

        @pl.loop(1, TM)
        def _(k):
            y_copy((t + 3 * k) % TM, cols, chunk // 2).start()

        for half in range(2):
            @pl.when(chunk == 2 * half)
            def _():
                prefix(half)

    y_recv[t] = y_send[t]

    for half in range(2):
        received(inc_send.at[half, pl.ds(0, HT - 1)], i_rsem.at[half])

        for f in range(2):
            rows = slice(128 * f, 128 * f + 128)
            for part in range(2):
                lanes = pl.ds(HALF * half + GL * part, GL)
                earlier = mm(bc_s[rows, STATE:], inc_recv[half, f, :, pl.ds(GL * part, GL)])
                sp_out[rows, lanes] += e_run[rows, lanes] * earlier

    def finish(part, start, width):
        cols = pl.ds(start, width)

        received(y_recv.at[pl.ds(0, TM - 1), :, cols], y_rsem.at[part])

        scales = []
        for k in range(4):
            f, r = k // 2, k % 2
            rows = slice(k * COLS + start, k * COLS + start + width)
            squares = jnp.zeros((width, 128), F32)
            for g in range(GROUPS):
                y = y_recv[GROUPS * r + g, f, cols, :].astype(F32)
                lanes = slice(GL * g, GL * g + GL)
                gated = (sp_out[rows, lanes] + y) * gate[rows, lanes]
                normed[width * k : width * k + width, lanes] = (
                    gated * out_gain[GL * g : GL * g + GL].reshape(1, GL)
                ).astype(BF16)
                gated = gated * gated
                squares += gated[:, :128] + gated[:, 128:256] + gated[:, 256:]
            mean_square = jnp.sum(squares, axis=-1, keepdims=True) * (1.0 / INNER)
            scales.append(lax.rsqrt(mean_square + EPSILON))
        scale_v[0 : 4 * width, :] = jnp.concatenate(scales, axis=0)

        @pl.loop(0, 2)
        def _(k):
            lanes = pl.ds(pl.multiple_of(HALF * k, 128), HALF)
            mixed = mm(normed[0 : 4 * width, :], w_out_v[:, lanes]) * scale_v[0 : 4 * width, :]
            mixed = mixed.astype(BF16)
            for block in range(4):
                out[block * COLS + start : block * COLS + start + width, lanes] = (
                    mixed[width * block : width * block + width]
                )

    loads[7].wait()
    finish(0, 0, 32)
    finish(1, 32, 32)

    sent(bct.at[pl.ds(0, 4)], b_ssem.at[0])
    sent(bct.at[pl.ds(0, 3)], b_ssem.at[1])
    sent(ltr.at[pl.ds(0, TM - 1)], l_ssem.at[0])
    sent(d_recv.at[pl.ds(0, HT - 1)], d_ssem.at[0])
    sent(xt.at[pl.ds(0, TM - 1)], x_ssem.at[0])
    sent(y_send.at[pl.ds(0, TM - 1)], y_ssem.at[0])
    for half in range(2):
        sent(s_recv.at[half, pl.ds(0, HT - 1)], s_ssem.at[half])
        sent(inc_send.at[half, pl.ds(0, HT - 1)], i_ssem.at[half])


def per_device(tokens, norm_gain, in_weight, bc_weight, dt_weight, dt_bias, decay_rate, out_gain, out_weight):
    hbm = pl.BlockSpec(memory_space=pl.ANY)
    dma = pltpu.SemaphoreType.DMA
    def keep(v):
        return pltpu.with_memory_space_constraint(v, pltpu.HBM)

    mixed = pl.pallas_call(
        kernel,
        out_shape=jax.ShapeDtypeStruct((TOK, D), BF16),
        in_specs=[hbm] * 9,
        out_specs=pl.BlockSpec(memory_space=pltpu.VMEM),
        scratch_shapes=[
            pltpu.VMEM((D,), F32),
            pltpu.VMEM((1, 2 * HEADS), F32),
            pltpu.VMEM((2, HEADS), F32),
            pltpu.VMEM((INNER,), F32),
            pltpu.VMEM((TOK, D), BF16),
            pltpu.VMEM((D, 2 * INNER), BF16),
            pltpu.VMEM((D, 4 * STATE), BF16),
            pltpu.VMEM((2 * HEADS, D), BF16),
            pltpu.VMEM((INNER, D), BF16),
            pltpu.VMEM((TOK, D), BF16),
            pltpu.VMEM((2, 128, INNER), BF16),
            pltpu.VMEM((TOK, INNER), F32),
            pltpu.VMEM((TOK, 2 * STATE), BF16),
            pltpu.VMEM((2, 2, COLS, 2 * STATE), BF16),
            pltpu.VMEM((GROUPS, 2, 16, 128), F32),
            pltpu.VMEM((2, 1, 128), F32),
            pltpu.VMEM((2, 2, STATE, HALF), BF16),
            pltpu.VMEM((TM, 2, COLS, GL), BF16),
            pltpu.VMEM((TM, 2, COLS, 2 * STATE), BF16),
            pltpu.VMEM((TM, 16, 128), F32),
            pltpu.VMEM((HT, 1, 128), F32),
            pltpu.VMEM((2, HT, 16, HALF), BF16),
            pltpu.VMEM((2, HT, 16, HALF), BF16),
            pltpu.VMEM((2, 2, STATE, HALF), BF16),
            pltpu.VMEM((TM, 2, COLS, GL), BF16),
            pltpu.VMEM((TM, 2, COLS, GL), BF16),
            pltpu.VMEM((2, 128, INNER), BF16),
            pltpu.VMEM((TOK, INNER), F32),
            pltpu.VMEM((TOK, INNER), F32),
            pltpu.VMEM((TOK, 32), F32),
            pltpu.VMEM((2, 32, 128), F32),
            pltpu.VMEM((96, INNER), BF16),
            pltpu.VMEM((16, GL), BF16),
            pltpu.VMEM((TOK, TOK), BF16),
            pltpu.VMEM((TM, 128, 16), F32),
            pltpu.VMEM((STATE, GL), F32),
            pltpu.VMEM((2, HT, HALF), F32),
            pltpu.VMEM((128, 1), F32),
            pltpu.VMEM((TOK, 1), F32),
            dma((8,)), dma((4,)),
            dma((1,)), dma((CHUNKS,)),
            dma((2,)), dma((2,)),
            dma((1,)), dma((1,)),
            dma((1,)), dma((1,)),
            dma((2,)), dma((2,)),
            dma((2,)), dma((2,)),
            dma((1,)), dma((2,)),
        ],
        compiler_params=pltpu.CompilerParams(
            collective_id=0, has_side_effects=True, vmem_limit_bytes=40 * 1024 * 1024
        ),
        name="layer",
    )(
        keep(tokens.reshape(TOK, D)),
        keep(norm_gain),
        keep(in_weight),
        keep(bc_weight),
        keep(dt_weight.T),
        keep(dt_bias.reshape(1, 2 * HEADS)),
        keep(decay_rate),
        keep(out_gain),
        keep(out_weight),
    )
    return mixed.reshape(tokens.shape)


def solution(mesh):
    in_specs = (P("tm", "height", None, None), P(), P(), P(), P(), P(), P(), P(), P())
    out_specs = P("tm", "height", None, None)
    return jax.shard_map(
        per_device, mesh=mesh, in_specs=in_specs, out_specs=out_specs, check_vma=False
    )
```

```python
import functools

import jax
import jax.numpy as jnp
from jax import lax
from jax.experimental import pallas as pl
from jax.experimental.pallas import tpu as pltpu
from jax.sharding import PartitionSpec as P

EPSILON = 1e-05
LOG2E = 1.4426950408889634
BF16 = jnp.bfloat16
F32 = jnp.float32

D = 1536
INNER = 1536
HEADS = 24
STATE = 128
COLS = 64
TM = 8
HT = 16
GROUPS = 4
GHEADS = HEADS // GROUPS
GL = GHEADS * 64
HALF = INNER // 2
TOK = 256
CHUNK_COLS = 16
CHUNKS = COLS // CHUNK_COLS


def mm(a, b):
    return jnp.dot(a, b, preferred_element_type=F32)


def mm_tokens(a, b):
    return lax.dot_general(a, b, (((0,), (0,)), ((), ())), preferred_element_type=F32)


def mm_rows(a, b):
    return lax.dot_general(a, b, (((1,), (1,)), ((), ())), preferred_element_type=F32)


def softplus(v):
    return jnp.maximum(v, 0.0) + jnp.log1p(jnp.exp(-jnp.abs(v)))


def parts(v, count):
    pieces, rest = [], v
    for _ in range(count):
        piece = rest.astype(BF16).astype(F32)
        pieces.append(piece)
        rest = rest - piece
    return jnp.concatenate(pieces, axis=1).astype(BF16)


def cumulative(order, v):
    width = v.shape[1]
    sums = mm(order, parts(v, 3))
    return sums[:, :width] + sums[:, width : 2 * width] + sums[:, 2 * width :]


def iota(shape, dim):
    return lax.broadcasted_iota(jnp.int32, shape, dim)


def kernel(
    tokens, gain_in, w_in, w_bc, w_dt, dt_bias_in, rate_in, out_gain_in, w_out, out,
    gain, dt_bias, rate, out_gain,
    tok_v, w_in_v, w_bc_v, w_dt_v, w_out_v,
    normed, x_all, gate, bc_s, bct_send, l_send, d_send, s_send,
    xt, bct, ltr, d_recv, s_recv, inc_send, inc_recv, y_send, y_recv,
    xd_s, sp_out, e_run, run_s, runt_s, spread_s, spread_t, order_t, lcol, state, d_exp,
    scale_v, scale_in, load_sem, small_sem, x_ssem, x_rsem, b_ssem, b_rsem, l_ssem, l_rsem, d_ssem, d_rsem,
    s_ssem, s_rsem, i_ssem, i_rsem, y_ssem, y_rsem,
):
    t = lax.axis_index("tm")
    h = lax.axis_index("height")

    def remote(src, dst, ssem, rsem, **where):
        return pltpu.make_async_remote_copy(
            src_ref=src, dst_ref=dst, send_sem=ssem, recv_sem=rsem,
            device_id=where, device_id_type=pl.DeviceIdType.MESH,
        )

    def received(ref, sem):
        remote(ref, ref, sem, sem, tm=t ^ 1).wait_recv()

    def sent(ref, sem):
        remote(ref, ref, sem, sem, tm=t ^ 1).wait_send()

    own_row, own_group = t // GROUPS, t % GROUPS

    def lanes_of(index):
        return pl.ds(pl.multiple_of(index * GL, 128), GL)

    def half_lanes(start, half):
        return pl.ds(pl.multiple_of(start + half * HALF, 128), HALF)

    loads = [
        pltpu.make_async_copy(tokens, tok_v, load_sem.at[0]),
        pltpu.make_async_copy(w_bc, w_bc_v, load_sem.at[1]),
        pltpu.make_async_copy(w_dt, w_dt_v, load_sem.at[2]),
    ]
    for step in range(4):
        where = pl.ds(HALF * step, HALF)
        loads.append(pltpu.make_async_copy(w_in.at[:, where], w_in_v.at[:, where], load_sem.at[3 + step]))
    loads.append(pltpu.make_async_copy(w_out, w_out_v, load_sem.at[7]))
    small = [
        pltpu.make_async_copy(source, target, small_sem.at[k])
        for k, (source, target) in enumerate(
            ((gain_in, gain), (dt_bias_in, dt_bias), (rate_in, rate), (out_gain_in, out_gain))
        )
    ]
    small[0].start()
    for load in loads[:5]:
        load.start()
    for load in small[1:]:
        load.start()

    barrier = pltpu.get_barrier_semaphore()

    @pl.loop(1, TM)
    def _(k):
        pl.semaphore_signal(barrier, inc=1, device_id={"tm": (t + k) % TM}, device_id_type=pl.DeviceIdType.MESH)

    @pl.loop(1, HT)
    def _(k):
        pl.semaphore_signal(barrier, inc=1, device_id={"height": (h + k) % HT}, device_id_type=pl.DeviceIdType.MESH)

    spread_s[...] = ((iota((96, INNER), 0) & 31) == (iota((96, INNER), 1) >> 6)).astype(F32).astype(BF16)
    spread_t[...] = ((iota((16, GL), 0) & 7) == (iota((16, GL), 1) >> 6)).astype(F32).astype(BF16)

    def place(index):
        return (index & 15) * 16 + ((index >> 4) & 7) * 2 + (index >> 7)

    order_t[...] = (place(iota((TOK, TOK), 0)) >= place(iota((TOK, TOK), 1))).astype(F32).astype(BF16)

    small[0].wait()
    loads[0].wait()

    tok = tok_v[...].astype(F32)
    normed[...] = (tok * gain[...].reshape(1, D)).astype(BF16)
    scale = lax.rsqrt(jnp.mean(tok * tok, axis=-1, keepdims=True) + EPSILON)
    scale_in[...] = scale

    loads[1].wait()
    bc = (mm(normed[...], w_bc_v[...]) * scale).astype(BF16)
    bc_s[...] = bc[:, : 2 * STATE]
    for f in range(2):
        for r in range(2):
            at = 128 * f + 64 * r
            bct_send[r, f] = bc[at : at + 64, 2 * STATE :]

    pl.semaphore_wait(barrier, TM - 1 + HT - 1)

    def bc_copy(to):
        return remote(bct_send.at[to // GROUPS], bct.at[t], b_ssem.at[0], b_rsem.at[(to + t) % 2], tm=to)

    def bc_pass(source):
        return remote(bct.at[source], bct.at[source], b_ssem.at[1], b_rsem.at[1], tm=t ^ 1)

    @pl.loop(1, 4)
    def _(k):
        bc_copy((t + 2 * k) % TM).start()

    bc_copy(t ^ 1).start()
    bct[t] = bct_send[own_row]

    def l_copy(to):
        return remote(l_send.at[to % GROUPS, to // GROUPS], ltr.at[t], l_ssem.at[0], l_rsem.at[0], tm=to)

    def chunk_of(chunk):
        return pl.ds(pl.multiple_of(chunk * CHUNK_COLS, CHUNK_COLS), CHUNK_COLS)

    def x_copy(to, chunk):
        rows = pl.ds(pl.multiple_of((to // GROUPS) * COLS + chunk * CHUNK_COLS, CHUNK_COLS), CHUNK_COLS)
        return remote(
            x_all.at[:, rows, lanes_of(to % GROUPS)], xt.at[t, :, chunk_of(chunk)],
            x_ssem.at[0], x_rsem.at[chunk], tm=to,
        )

    def owned(p):
        return p // 8, pl.ds(pl.multiple_of((p % 8) * 16, 16), 16)

    own_f, own_n = owned(h)

    def s_copy(to, half):
        f, rows = owned(to)
        return remote(
            s_send.at[half, f, rows], s_recv.at[half, h], s_ssem.at[half], s_rsem.at[half], height=to
        )

    def d_copy(to):
        return remote(d_send.at[to // 8], d_recv.at[h], d_ssem.at[0], d_rsem.at[0], height=to)

    def x_half(half):
        lanes = pl.ds(HALF * half, HALF)
        xh = (mm(normed[...], w_in_v[:, lanes]) * scale).astype(BF16)
        x_all[0, :, lanes] = xh[:128]
        x_all[1, :, lanes] = xh[128:]

    for load in small[1:]:
        load.wait()
    loads[2].wait()
    loads[3].wait()
    logits = (mm_rows(normed[...], w_dt_v[...]) * scale).astype(BF16).astype(F32)
    dt = softplus(logits + dt_bias[...])
    rates = jnp.concatenate([rate[0:1, :], rate[1:2, :]], axis=1)
    decay = -dt * rates * LOG2E
    both = jnp.concatenate([dt, decay, jnp.zeros((TOK, 32), F32)], axis=1)
    for r in range(2):
        turned = jnp.concatenate([both[64 * r : 64 * r + 64], both[128 + 64 * r : 192 + 64 * r]], axis=0).T
        for g in range(GROUPS):
            l_send[g, r, 0:8] = turned[24 + 6 * g : 32 + 6 * g]
            l_send[g, r, 8:16] = turned[72 + 6 * g : 80 + 6 * g]

    pad = jnp.zeros((TOK, 8), F32)
    dt_s = jnp.concatenate([dt[:, :HEADS], pad], axis=1)
    decay_s = jnp.concatenate([decay[:, :HEADS], pad], axis=1)
    row, col = iota((TOK, TOK), 0), iota((TOK, TOK), 1)
    order_s = ((row >= col) & ((row >> 7) == (col >> 7))).astype(F32).astype(BF16)
    run = cumulative(order_s, decay_s)
    run_s[...] = run
    for f in range(2):
        runt_s[f] = jnp.concatenate([run[128 * f : 128 * f + 128], jnp.zeros((128, 96), F32)], axis=1).T[:32]
    ends = [run[127:128], run[255:256]]
    for f in range(2):
        d_send[f] = jnp.concatenate([jnp.exp2(ends[f]), jnp.zeros((1, 96), F32)], axis=1)
    end = jnp.concatenate([jnp.broadcast_to(e, (128, 32)) for e in ends], axis=0)
    to_end = parts(jnp.exp2(end - run) * dt_s, 2)
    dt_parts = parts(dt_s, 2)
    from_start = parts(jnp.exp2(run), 2)

    def state_half(half):
        for part in range(2):
            lanes = pl.ds(HALF * half + GL * part, GL)
            spread = spread_s[0:64, lanes]
            weight = mm(to_end, spread)
            for f in range(2):
                rows = slice(128 * f, 128 * f + 128)
                x = x_all[f, :, lanes].astype(F32)
                s_send[half, f, :, pl.ds(GL * part, GL)] = mm_tokens(
                    bc_s[rows, :STATE], (x * weight[rows]).astype(BF16)
                ).astype(BF16)

        @pl.loop(1, HT)
        def _(k):
            s_copy((h + k) % HT, half).start()

        s_recv[half, h] = s_send[half, own_f, own_n]

    x_half(0)
    state_half(0)
    loads[4].wait()
    for load in loads[5:]:
        load.start()
    x_half(1)

    def x_send(chunk):
        @pl.loop(1, TM)
        def _(k):
            x_copy((t + 3 * k) % TM, chunk).start()

    x_send(0)

    @pl.loop(1, HT)
    def _(k):
        d_copy((h + k) % HT).start()

    d_recv[h] = d_send[h // 8]
    state_half(1)

    @pl.loop(1, TM)
    def _(k):
        l_copy((t + k) % TM).start()

    x_send(1)
    x_send(2)
    x_send(3)

    ltr[t] = l_send[own_group, own_row]
    own_rows = pl.ds(pl.multiple_of(own_row * COLS, COLS), COLS)
    for f in range(2):
        xt[t, f] = x_all[f, own_rows, lanes_of(own_group)]

    for part in range(4):
        lanes = pl.ds(GL * part, GL)
        steps = mm(dt_parts, spread_s[0:64, lanes])
        e_run[:, lanes] = mm(from_start, spread_s[0:64, lanes])
        for f in range(2):
            xd_s[f, :, lanes] = (x_all[f, :, lanes].astype(F32) * steps[128 * f : 128 * f + 128]).astype(BF16)

    @pl.loop(0, 4)
    def _(k):
        for step in range(2):
            @pl.when(k == 2 * step)
            def _():
                loads[5 + step].wait()
        v = mm(normed[...], w_in_v[:, pl.ds(pl.multiple_of(INNER + GL * k, 128), GL)])
        v = (v * scale_in[...]).astype(BF16).astype(F32)
        gate[:, lanes_of(k)] = v / (1.0 + jnp.exp(-v))

    received(bct.at[pl.ds(0, 3)], b_rsem.at[0])

    @pl.loop(1, 4)
    def _(k):
        source = (t + 2 * k) % TM
        bc_pass(source).start()

    half = iota((128, 128), 1) < 64
    causal = iota((128, 128), 0) >= iota((128, 128), 1)

    @pl.loop(0, 2)
    def _(f):
        rows = pl.ds(pl.multiple_of(f * 128, 128), 128)
        b, c = bc_s[rows, :STATE], bc_s[rows, STATE:]
        scores = mm_rows(c, b)
        scores = jnp.where(causal, scores, 0.0)
        run_f, runt_f = run_s[rows, :], runt_s[f]
        for pair in range(HEADS // 2):
            weights = []
            for head in (2 * pair, 2 * pair + 1):
                spread = run_f[:, head : head + 1] - runt_f[head : head + 1, :]
                weights.append((scores * jnp.exp2(jnp.minimum(spread, 0.0))).astype(BF16))
            lanes = pl.ds(128 * pair, 128)
            x = xd_s[f, :, lanes]
            none = jnp.zeros_like(x)
            both_x = jnp.concatenate([jnp.where(half, x, none), jnp.where(half, none, x)], axis=0)
            sp_out[rows, lanes] = mm(jnp.concatenate(weights, axis=1), both_x)

    def band_decays():
        received(d_recv.at[pl.ds(0, HT - 1)], d_rsem.at[0])
        totals = parts(jnp.concatenate([d_recv[k] for k in range(HT)], axis=0)[:, :32], 3)
        for half in range(2):
            d_exp[half] = mm(totals, spread_s[:, pl.ds(HALF * half, HALF)])

    def i_copy(to, half):
        f, rows = owned(h)
        return remote(
            inc_send.at[half, to], inc_recv.at[half, f, rows], i_ssem.at[half], i_rsem.at[half], height=to
        )

    def prefix(half):
        received(s_recv.at[half, pl.ds(0, HT - 1)], s_rsem.at[half])
        if half == 0:
            band_decays()

        before = jnp.zeros((16, HALF), F32)
        for k in range(HT):
            inc_send[half, k] = before.astype(BF16)
            if k < HT - 1:
                before = before * d_exp[half, k : k + 1, :] + s_recv[half, k].astype(F32)

        @pl.loop(1, HT)
        def _(k):
            i_copy((h + k) % HT, half).start()

        inc_recv[half, own_f, own_n, :] = inc_send[half, h]

    received(ltr.at[pl.ds(0, TM - 1)], l_rsem.at[0])
    received(bct.at[pl.ds(0, 4)], b_rsem.at[1])
    columns = ltr[...].reshape(TM * 16, 128).T
    for s in range(TM):
        lcol[s] = columns[:, 16 * s : 16 * s + 16]

    state[...] = jnp.zeros_like(state)

    def y_copy(to, cols, part):
        return remote(
            y_send.at[to, :, cols], y_recv.at[t, :, cols], y_ssem.at[0], y_rsem.at[part], tm=to
        )

    @pl.loop(0, CHUNKS)
    def _(chunk):
        cols = chunk_of(chunk)

        received(xt.at[pl.ds(0, TM - 1), :, cols], x_rsem.at[chunk])

        def tokens_of(f):
            return pl.ds(pl.multiple_of(f * COLS + chunk * CHUNK_COLS, CHUNK_COLS), CHUNK_COLS)

        def gathered(get, width):
            return jnp.concatenate([get(f).reshape(128, width) for f in range(2)], axis=0)

        x = gathered(lambda f: xt[:, f, cols, :], GL)
        bcv = gathered(lambda f: bct[:, f, cols, :], 2 * STATE)
        dl = gathered(lambda f: lcol[:, tokens_of(f), :], 16)
        b, c = bcv[:, :STATE], bcv[:, STATE:]
        dtv, decays = dl[:, :8], dl[:, 8:]
        runs = cumulative(order_t[...], decays)
        runs_row = jnp.concatenate([runs, jnp.zeros((TOK, 120), F32)], axis=1).T[:8]
        last = runs[TOK - 1 : TOK]
        weight = mm(parts(jnp.exp2(last - runs) * dtv, 2), spread_t[...])
        steps = mm(parts(dtv, 2), spread_t[...])
        grown = mm(parts(jnp.exp2(runs), 2), spread_t[...])
        scores = mm_rows(c, b)
        scores = scores * order_t[...].astype(F32)
        xf = x.astype(F32)
        xd = (xf * steps).astype(BF16)
        xw = (xf * weight).astype(BF16)
        earlier = mm(c, state[...].astype(BF16)) * grown
        state[...] = state[...] * grown[TOK - 1 : TOK] + mm_tokens(b, xw)
        half_x = iota((TOK, 128), 1) < 64
        for pair in range(GHEADS // 2):
            weights = []
            for head in (2 * pair, 2 * pair + 1):
                spread = runs[:, head : head + 1] - runs_row[head : head + 1, :]
                weights.append((scores * jnp.exp2(jnp.minimum(spread, 0.0))).astype(BF16))
            lanes = slice(128 * pair, 128 * pair + 128)
            xp = xd[:, lanes]
            none = jnp.zeros_like(xp)
            both_x = jnp.concatenate([jnp.where(half_x, xp, none), jnp.where(half_x, none, xp)], axis=0)
            y = mm(jnp.concatenate(weights, axis=1), both_x) + earlier[:, lanes]
            y = y.astype(BF16)
            for f in range(2):
                y_send[:, f, cols, lanes] = y[128 * f : 128 * f + 128].reshape(TM, CHUNK_COLS, 128)

        @pl.loop(1, TM)
        def _(k):
            y_copy((t + 3 * k) % TM, cols, chunk // 2).start()

        for half in range(2):
            @pl.when(chunk == 2 * half)
            def _():
                prefix(half)

    y_recv[t] = y_send[t]

    for half in range(2):
        received(inc_send.at[half, pl.ds(0, HT - 1)], i_rsem.at[half])

        for f in range(2):
            rows = slice(128 * f, 128 * f + 128)
            for part in range(2):
                lanes = pl.ds(HALF * half + GL * part, GL)
                earlier = mm(bc_s[rows, STATE:], inc_recv[half, f, :, pl.ds(GL * part, GL)])
                sp_out[rows, lanes] += e_run[rows, lanes] * earlier

    def finish(part, start, width):
        cols = pl.ds(start, width)

        received(y_recv.at[pl.ds(0, TM - 1), :, cols], y_rsem.at[part])

        scales = []
        for k in range(4):
            f, r = k // 2, k % 2
            rows = slice(k * COLS + start, k * COLS + start + width)
            squares = jnp.zeros((width, 128), F32)
            for g in range(GROUPS):
                y = y_recv[GROUPS * r + g, f, cols, :].astype(F32)
                lanes = slice(GL * g, GL * g + GL)
                gated = (sp_out[rows, lanes] + y) * gate[rows, lanes]
                normed[width * k : width * k + width, lanes] = (
                    gated * out_gain[GL * g : GL * g + GL].reshape(1, GL)
                ).astype(BF16)
                gated = gated * gated
                squares += gated[:, :128] + gated[:, 128:256] + gated[:, 256:]
            mean_square = jnp.sum(squares, axis=-1, keepdims=True) * (1.0 / INNER)
            scales.append(lax.rsqrt(mean_square + EPSILON))
        scale_v[0 : 4 * width, :] = jnp.concatenate(scales, axis=0)

        for k in range(2):
            lanes = pl.ds(HALF * k, HALF)
            mixed = mm(normed[0 : 4 * width, :], w_out_v[:, lanes]) * scale_v[0 : 4 * width, :]
            mixed = mixed.astype(BF16)
            for block in range(4):
                out[block * COLS + start : block * COLS + start + width, lanes] = (
                    mixed[width * block : width * block + width]
                )

    loads[7].wait()
    finish(0, 0, 32)
    finish(1, 32, 32)

    sent(bct.at[pl.ds(0, 4)], b_ssem.at[0])
    sent(bct.at[pl.ds(0, 3)], b_ssem.at[1])
    sent(ltr.at[pl.ds(0, TM - 1)], l_ssem.at[0])
    sent(d_recv.at[pl.ds(0, HT - 1)], d_ssem.at[0])
    sent(xt.at[pl.ds(0, TM - 1)], x_ssem.at[0])
    sent(y_send.at[pl.ds(0, TM - 1)], y_ssem.at[0])
    for half in range(2):
        sent(s_recv.at[half, pl.ds(0, HT - 1)], s_ssem.at[half])
        sent(inc_send.at[half, pl.ds(0, HT - 1)], i_ssem.at[half])


def per_device(tokens, norm_gain, in_weight, bc_weight, dt_weight, dt_bias, decay_rate, out_gain, out_weight):
    hbm = pl.BlockSpec(memory_space=pl.ANY)
    dma = pltpu.SemaphoreType.DMA
    def keep(v):
        return pltpu.with_memory_space_constraint(v, pltpu.HBM)

    mixed = pl.pallas_call(
        kernel,
        out_shape=jax.ShapeDtypeStruct((TOK, D), BF16),
        in_specs=[hbm] * 9,
        out_specs=pl.BlockSpec(memory_space=pltpu.VMEM),
        scratch_shapes=[
            pltpu.VMEM((D,), F32),
            pltpu.VMEM((1, 2 * HEADS), F32),
            pltpu.VMEM((2, HEADS), F32),
            pltpu.VMEM((INNER,), F32),
            pltpu.VMEM((TOK, D), BF16),
            pltpu.VMEM((D, 2 * INNER), BF16),
            pltpu.VMEM((D, 4 * STATE), BF16),
            pltpu.VMEM((2 * HEADS, D), BF16),
            pltpu.VMEM((INNER, D), BF16),
            pltpu.VMEM((TOK, D), BF16),
            pltpu.VMEM((2, 128, INNER), BF16),
            pltpu.VMEM((TOK, INNER), F32),
            pltpu.VMEM((TOK, 2 * STATE), BF16),
            pltpu.VMEM((2, 2, COLS, 2 * STATE), BF16),
            pltpu.VMEM((GROUPS, 2, 16, 128), F32),
            pltpu.VMEM((2, 1, 128), F32),
            pltpu.VMEM((2, 2, STATE, HALF), BF16),
            pltpu.VMEM((TM, 2, COLS, GL), BF16),
            pltpu.VMEM((TM, 2, COLS, 2 * STATE), BF16),
            pltpu.VMEM((TM, 16, 128), F32),
            pltpu.VMEM((HT, 1, 128), F32),
            pltpu.VMEM((2, HT, 16, HALF), BF16),
            pltpu.VMEM((2, HT, 16, HALF), BF16),
            pltpu.VMEM((2, 2, STATE, HALF), BF16),
            pltpu.VMEM((TM, 2, COLS, GL), BF16),
            pltpu.VMEM((TM, 2, COLS, GL), BF16),
            pltpu.VMEM((2, 128, INNER), BF16),
            pltpu.VMEM((TOK, INNER), F32),
            pltpu.VMEM((TOK, INNER), F32),
            pltpu.VMEM((TOK, 32), F32),
            pltpu.VMEM((2, 32, 128), F32),
            pltpu.VMEM((96, INNER), BF16),
            pltpu.VMEM((16, GL), BF16),
            pltpu.VMEM((TOK, TOK), BF16),
            pltpu.VMEM((TM, 128, 16), F32),
            pltpu.VMEM((STATE, GL), F32),
            pltpu.VMEM((2, HT, HALF), F32),
            pltpu.VMEM((128, 1), F32),
            pltpu.VMEM((TOK, 1), F32),
            dma((8,)), dma((4,)),
            dma((1,)), dma((CHUNKS,)),
            dma((2,)), dma((2,)),
            dma((1,)), dma((1,)),
            dma((1,)), dma((1,)),
            dma((2,)), dma((2,)),
            dma((2,)), dma((2,)),
            dma((1,)), dma((2,)),
        ],
        compiler_params=pltpu.CompilerParams(
            collective_id=0, has_side_effects=True, vmem_limit_bytes=40 * 1024 * 1024
        ),
        name="layer",
    )(
        keep(tokens.reshape(TOK, D)),
        keep(norm_gain),
        keep(in_weight),
        keep(bc_weight),
        keep(dt_weight.T),
        keep(dt_bias.reshape(1, 2 * HEADS)),
        keep(decay_rate),
        keep(out_gain),
        keep(out_weight),
    )
    return mixed.reshape(tokens.shape)


def solution(mesh):
    in_specs = (P("tm", "height", None, None), P(), P(), P(), P(), P(), P(), P(), P())
    out_specs = P("tm", "height", None, None)
    return jax.shard_map(
        per_device, mesh=mesh, in_specs=in_specs, out_specs=out_specs, check_vma=False
    )
```
